256 devices in a mesh: band: 128 (over x_hi, y, z, core), grid: 2 (over x_lo).
Axes of the slice: x: 4 (x_hi: 2, x_lo: 2; x = x_hi * 2 + x_lo), y: 4, z: 8, core: 2. Of those that a mesh axis runs over, the one named last changes fastest.
Arguments:
- orbitals: float32 [128, 72, 5184], P('band', 'grid'), may hold values from -6 to 6
- owners: int32 [128], replicated, may hold values from 0 to 127, each once
Outputs:
- exchange_field: float32 [2, 128, 186624], P('grid', None, 'band')
- intersection: float32 [128, 128], replicated
The draws below stay inside these ranges and needn't reach their ends.
Inputs may be any that keep to these rules, and one draw needn't show every extreme that they name: owners holds every index of the band axis exactly once; only its first 2 entries are used.
All inputs are finite; a program needn't handle non-finite values.
Results may differ from the reference program's by a relative error of at most 0.00019.
Values sent between devices are 32-bit elements; how exact they have to be, the bound alone decides.
A program may use at most 64 MiB of HBM per device.

```python
import math
import jax
import jax.numpy as jnp
from jax import lax

NX = 72
NY = 72
NZ = 72
B_DEV = 1
ROUNDS = 2
BANDS = 128
NYZ = 5184
SLAB = 186624
OWNERS = 128
N_BAND = 128
N_GRID = 2


def levels(own_key, extent, split, smallest, largest):
    def one(axis_at, parts):
        steps = jax.random.uniform(jax.random.fold_in(jax.random.fold_in(own_key, 6), axis_at), (parts,), jnp.float32, smallest / len(split), largest / len(split))
        return jnp.repeat(jnp.exp(steps), extent[axis_at] // parts).reshape((-1,) + (1,) * (len(extent) - axis_at - 1))

    gain = one(*split[0])
    for cut in split[1:]:
        gain = gain * one(*cut)
    return gain


def gaussian(key, shape, scale, bound, split=(), kind=jnp.bfloat16):
    entries = scale * jax.random.normal(key, shape, jnp.float32)
    if split:
        entries = entries * levels(key, shape, split, -0.22, 0.18)
    return jnp.clip(entries, -bound, bound).astype(kind)


def setup_inputs(seed: int = 0) -> dict:
    keys = jax.random.split(jax.random.key(seed), 3)
    return {
        "orbitals": gaussian(keys[0], (BANDS, NX, NYZ), 1.0, 6.0, ((0, 128), (1, 2)), jnp.float32),
        "owners": jax.random.permutation(keys[1], OWNERS).astype(jnp.int32),
    }


def make_kernel():
    sq_x = (2.0 * math.pi * jnp.fft.fftfreq(NX)) ** 2
    sq_y = (2.0 * math.pi * jnp.fft.fftfreq(NY)) ** 2
    sq_z = (2.0 * math.pi * jnp.fft.rfftfreq(NZ)) ** 2
    total_sq = sq_x[:, None, None] + sq_y[None, :, None] + sq_z[None, None, :]
    positive = total_sq > 0
    return jnp.where(positive, math.pi / jnp.where(positive, total_sq, 1.0), 0.0)


def reference(orbitals, owners):
    grid_field = orbitals.reshape(BANDS, NX, NY, NZ)
    kernel = make_kernel()
    accumulated = jnp.zeros((BANDS, NX, NY, NZ), jnp.float32)
    for round_index in range(ROUNDS):
        owner_band = (owners[round_index] * B_DEV).astype(jnp.int32)
        lent_bands = lax.dynamic_slice_in_dim(grid_field, owner_band, B_DEV, 0)

        def one_group(own_bands):
            density = own_bands[:, None] * lent_bands[None]
            spectrum = jnp.fft.rfftn(density, axes=(2, 3, 4))
            potential = jnp.fft.irfftn(spectrum * kernel, s=(NX, NY, NZ), axes=(2, 3, 4))
            return -0.25 * jnp.sum(lent_bands[None] * potential, axis=1)

        contribution = lax.map(one_group, grid_field.reshape(N_BAND, B_DEV, NX, NY, NZ))
        accumulated = accumulated + contribution.reshape(BANDS, NX, NY, NZ).astype(accumulated.dtype)
    flat_field = accumulated.reshape(BANDS, NX * NY * NZ)
    exchange_field = jnp.transpose(flat_field.reshape(BANDS, N_GRID, SLAB), (1, 0, 2))
    intersection = jnp.dot(orbitals.reshape(BANDS, NX * NY * NZ), flat_field.T,
                      precision=lax.Precision.HIGHEST, preferred_element_type=jnp.float32) / (NX * NY * NZ)
    return exchange_field, intersection
```

```python
import math

import jax
import jax.numpy as jnp
from jax import lax
from jax.sharding import PartitionSpec as P

NX = 72
NY = 72
NZ = 72


HIGHEST_PRECISION = lax.Precision.HIGHEST
EXCHANGE_FRACTION = 0.25


def real_table(length):
    positions = jnp.arange(length, dtype=jnp.int32)
    nyquist = length // 2
    frequency = jnp.where(positions <= nyquist, positions, positions - nyquist)
    phase_int = frequency[:, None] * positions[None, :] % length
    angles = phase_int.astype(jnp.float32) * (2.0 * math.pi / length)
    weights = jnp.where(
        (positions == 0) | (positions == nyquist), 1.0 / math.sqrt(length), math.sqrt(2.0 / length)
    ).astype(jnp.float32)
    basis = (
        jnp.where((positions <= nyquist)[:, None], jnp.cos(angles), jnp.sin(angles))
        * weights[:, None]
    )
    wavenum = frequency.astype(jnp.float32) * (2.0 * math.pi / length)
    return (basis, wavenum * wavenum)


def shards(orbitals, owners):
    _, local_x, plane_size = orbitals.shape
    table, sq = real_table(NX)
    total_sq = sq[:, None, None] + sq[None, :, None] + sq[None, None, :]
    positive = total_sq > 0
    kernel = jnp.where(positive, math.pi / jnp.where(positive, total_sq, 1.0), 0.0)
    slot = lax.axis_index("grid")
    swap = [(0, 1), (1, 0)]

    orb_cols = lax.all_to_all(
        orbitals.reshape(1, local_x * plane_size), "band", split_axis=1, concat_axis=0, tiled=True
    )
    picked = jnp.concatenate(
        [lax.dynamic_slice_in_dim(orb_cols, owners[r], 1, 0) for r in range(2)], axis=0
    )
    picked = lax.all_to_all(picked, "grid", split_axis=0, concat_axis=0, tiled=True)
    lent = lax.all_gather(picked, "band", axis=0, tiled=False)
    lent = jnp.swapaxes(lent, 0, 1).reshape(NX, NY, NZ)

    other = lax.ppermute(orbitals[0], "grid", swap)
    mine = orbitals[0]
    own = jnp.where(
        slot == 0, jnp.concatenate([mine, other], 0), jnp.concatenate([other, mine], 0)
    ).reshape(NX, NY, NZ)

    values = own * lent
    values = jnp.einsum("by,xyz->xbz", table, values, precision=HIGHEST_PRECISION)
    values = jnp.einsum("cz,xbz->xbc", table, values, precision=HIGHEST_PRECISION)
    values = jnp.einsum("ax,xyz->ayz", table, values, precision=HIGHEST_PRECISION) * kernel
    values = jnp.einsum("ax,ayz->xyz", table, values, precision=HIGHEST_PRECISION)
    values = jnp.einsum("by,xbz->xyz", table, values, precision=HIGHEST_PRECISION)
    values = jnp.einsum("cz,xyc->xyz", table, values, precision=HIGHEST_PRECISION)
    part = (-EXCHANGE_FRACTION * lent * values).reshape(2, local_x * plane_size)
    keep = lax.dynamic_slice_in_dim(part, slot, 1, 0)
    give = lax.dynamic_slice_in_dim(part, 1 - slot, 1, 0)
    field = keep + lax.ppermute(give, "grid", swap)

    field_cols = lax.all_to_all(field, "band", split_axis=1, concat_axis=0, tiled=True)
    partial = jnp.dot(
        orb_cols, field_cols.T, precision=HIGHEST_PRECISION, preferred_element_type=jnp.float32
    ) / (NX * NY * NZ)
    pieces = lax.all_to_all(partial, "band", split_axis=0, concat_axis=0, tiled=True)
    row = jnp.sum(pieces, axis=0, keepdims=True)
    row = row + lax.ppermute(row, "grid", swap)
    intersection = lax.all_to_all(
        jnp.broadcast_to(row, (128, 128)), "band", split_axis=0, concat_axis=0, tiled=True
    )
    return (field_cols[None], intersection)


def solution(mesh):
    in_specs = (P("band", "grid", None), P())
    out_specs = (P("grid", None, "band"), P())
    return jax.shard_map(shards, mesh=mesh, in_specs=in_specs, out_specs=out_specs, check_vma=False)
```

```python
import functools
import math

import jax
import jax.numpy as jnp
import numpy as np
from jax import lax
from jax.experimental import pallas as pl
from jax.experimental.pallas import tpu as pltpu
from jax.sharding import PartitionSpec as P

N = 72
PAD = 80
BF = jnp.bfloat16
F32 = jnp.float32

def tables():
    pos = np.arange(N)
    half = N // 2
    freq = np.where(pos <= half, pos, pos - half)
    ang = (freq[:, None] * pos[None, :] % N) * (2.0 * math.pi / N)
    w = np.where((pos == 0) | (pos == half), 1.0 / math.sqrt(N), math.sqrt(2.0 / N))
    basis = np.where((pos <= half)[:, None], np.cos(ang), np.sin(ang)) * w[:, None]
    sq = (freq * (2.0 * math.pi / N)) ** 2

    def split(t):
        hi = jnp.asarray(t, F32).astype(BF)
        lo = (jnp.asarray(t, F32) - hi.astype(F32)).astype(BF)
        return hi, lo

    def left(t):
        hi, lo = split(t)
        put = lambda a: jnp.pad(a, ((0, PAD - N), (0, PAD - N)))
        return jnp.concatenate([put(hi), put(hi), put(lo)], axis=1)

    def right(t):
        hi, lo = split(t)
        put = lambda a: jnp.pad(a, ((0, 128 - N), (0, 128 - N)))
        top = jnp.concatenate([put(hi), put(lo)], axis=1)
        low = jnp.concatenate([put(hi), jnp.zeros((128, 128), BF)], axis=1)
        return jnp.concatenate([top, low], axis=0)

    sq_rows = np.zeros((PAD, 128), np.float32); sq_rows[:N] = sq[:, None]
    sq_pair = np.zeros((N, 128), np.float32); sq_pair[:, :N] = sq[:, None] + sq[None, :]
    return (left(basis), left(basis.T), right(basis.T), right(basis), jnp.asarray(sq_rows), jnp.asarray(sq_pair))


def halves(v):
    hi = v.astype(BF)
    lo = (v - hi.astype(F32)).astype(BF)
    return hi, lo


def left_dot(table, planes):
    cols = []
    for v in planes:
        hi, lo = halves(v)
        cols.append(jnp.concatenate([hi, lo, hi], axis=0))
    out = jnp.dot(table, jnp.concatenate(cols, axis=1), preferred_element_type=F32)
    return [out[:, 128 * i : 128 * i + 128] for i in range(len(planes))]


def right_dot(v, table):
    hi, lo = halves(v)
    out = jnp.dot(jnp.concatenate([hi, lo], axis=1), table, preferred_element_type=F32)
    return out[:, :128] + out[:, 128:]


def pad_rows(v):
    return jnp.concatenate([v, jnp.zeros((PAD - N, 128), F32)], axis=0)


def convolve(own, lent, work, tl, til, tr, tir, sq_rows, sq_pair, UA, UB, UC):
    lane = lax.broadcasted_iota(jnp.int32, (1, 128), 1) < N

    def stage_a(step, carry):
        for u in range(UA):
            base = pl.multiple_of((step * UA + u) * 2 * N, 8)
            rows = pl.ds(base, 2 * N)
            d = jnp.where(lane, own[rows, :] * lent[rows, :], 0.0)
            z = right_dot(d, tr[...])
            a, b = left_dot(tl[...], [pad_rows(z[:N]), pad_rows(z[N:])])
            work[rows, :] = jnp.concatenate([a[:N], b[:N]], axis=0)
        return carry

    lax.fori_loop(0, 36 // UA, stage_a, 0)

    def stage_b(step, carry):
        for u in range(UB):
            b = (step * UB + u) * 2
            planes = [pad_rows(work[pl.ds(b + i, N, stride=N), :]) for i in range(2)]
            planes = left_dot(tl[...], planes)
            for i in range(2):
                total = sq_rows[...] + sq_pair[pl.ds(b + i, 1), :]
                positive = total > 0
                kern = jnp.where(positive, (-0.25 * math.pi) / jnp.where(positive, total, 1.0), 0.0)
                planes[i] = planes[i] * kern
            planes = left_dot(til[...], planes)
            for i in range(2):
                work[pl.ds(b + i, N, stride=N), :] = planes[i][:N]
        return carry

    lax.fori_loop(0, 36 // UB, stage_b, 0)

    def stage_c(step, carry):
        for u in range(UC):
            base = pl.multiple_of((step * UC + u) * 2 * N, 8)
            rows = pl.ds(base, 2 * N)
            v = work[rows, :]
            a, b = left_dot(til[...], [pad_rows(v[:N]), pad_rows(v[N:])])
            z = right_dot(jnp.concatenate([a[:N], b[:N]], axis=0), tir[...])
            own[rows, :] = z * lent[rows, :]
        return carry

    lax.fori_loop(0, 36 // UC, stage_c, 0)


def from_plane(ref, dst, slab):
    for y in range(N):
        dst[pl.ds(slab * 2592 + y, 36, stride=N), :N] = ref[:, N * y : N * y + N]


def spans():
    for j in range(81):
        first, at = divmod(N * j, 1458)
        fit = min(N, 1458 - at)
        yield j, first, at, fit


def from_blocks(ref, dst, slab):
    for j, first, at, fit in spans():
        rows = pl.ds(slab * 2592 + j, 32, stride=81)
        v = ref[first, :, at : at + fit]
        if fit < N:
            v = jnp.concatenate([v, ref[first + 1, :, : N - fit]], axis=1)
        dst[rows, :N] = v


def to_blocks(src, ref, slab):
    for j, first, at, fit in spans():
        v = src[pl.ds(slab * 2592 + j, 32, stride=81), :]
        ref[first, :, at : at + fit] = v[:, :fit]
        if fit < N:
            ref[first + 1, :, : N - fit] = v[:, fit:N]


def fft_kernel(U, mine, other, lent_in, tl, til, tr, tir, sq_rows, sq_pair, out, own, lent, work):
    from_plane(mine, own, 0)
    from_plane(other, own, 1)
    for s in range(2):
        from_blocks(lent_in.at[s], lent, s)
    convolve(own, lent, work, tl, til, tr, tir, sq_rows, sq_pair, *U)
    for s in range(2):
        to_blocks(own, out.at[s], s)


def fft_call(mine, other, lent, U=(9, 9, 9)):
    vm = pl.BlockSpec(memory_space=pltpu.VMEM)
    return pl.pallas_call(
        functools.partial(fft_kernel, U),
        out_shape=jax.ShapeDtypeStruct((2, 4, 32, 1458), F32),
        in_specs=[vm] * 9,
        out_specs=vm,
        scratch_shapes=[pltpu.VMEM((5184, 128), F32) for _ in range(3)],
        compiler_params=pltpu.CompilerParams(vmem_limit_bytes=48 << 20),
    )(mine, other, lent, *tables())


MESH = pl.DeviceIdType.MESH
BANDS = 128
CELLS = 1458


def send(src, dst, send_sem, recv_sem, device):
    return pltpu.make_async_remote_copy(
        src_ref=src, dst_ref=dst, send_sem=send_sem, recv_sem=recv_sem, device_id=device, device_id_type=MESH
    )


def greet(barrier, device):
    pl.semaphore_signal(barrier, inc=1, device_id=device, device_id_type=MESH)


def greet_bands(barrier, band):
    def one(k, carry):
        greet(barrier, {"band": lax.rem(band + k, BANDS)})
        return carry

    lax.fori_loop(1, BANDS, one, 0)


def lend_kernel(
    owners, orb, cols, other, lent, rows, blocks, picked,
    a2a_send, a2a_recv, own_sem, swap_send, swap_recv, ag_send, ag_recv,
):
    band, grid = lax.axis_index("band"), lax.axis_index("grid")
    partner = {"grid": 1 - grid}
    barrier = pltpu.get_barrier_semaphore()
    greet_bands(barrier, band)
    greet(barrier, partner)
    from_plane(orb, rows, 0)
    to_blocks(rows, blocks, 0)
    pl.semaphore_wait(barrier, BANDS)

    def block(c):
        return blocks.at[lax.rem(c, 4), pl.ds(lax.div(c, 4), 1), :]

    def a2a(to, slot):
        return send(block(to), cols.at[pl.ds(slot, 1), :], a2a_send.at[to], a2a_recv.at[slot], {"band": to})

    def start(k, carry):
        a2a(lax.rem(band + k, BANDS), band).start()
        return carry

    lax.fori_loop(1, BANDS, start, 0)
    own = pltpu.make_async_copy(block(band), cols.at[pl.ds(band, 1), :], own_sem)
    own.start()
    whole = send(orb, other, swap_send.at[0], swap_recv.at[0], partner)
    whole.start()

    def finish(k, carry):
        c = lax.rem(band + k, BANDS)
        a2a(c, c).wait_recv()
        return carry

    lax.fori_loop(1, BANDS, finish, 0)
    own.wait()

    core, z = lax.rem(band, 2), lax.rem(lax.div(band, 2), 8)
    xy = lax.div(band, 16)
    xh, y = lax.div(xy, 4), lax.rem(xy, 4)
    pick_mine, pick_other = owners[grid], owners[1 - grid]
    picked[0:1, :] = cols[pl.ds(pick_mine, 1), :]
    picked[1:2, :] = cols[pl.ds(pick_other, 1), :]

    def at(xy_, z_):
        return pl.ds(4 * xy_ + lax.div(z_, 2), 1)

    zlo = lax.rem(z, 2)
    keep = pltpu.make_async_copy(picked.at[pl.ds(0, 1), :], lent.at[0, zlo, core, at(xy, z), :], own_sem)
    keep.start()
    give = send(
        picked.at[pl.ds(1, 1), :], lent.at[1, zlo, core, at(xy, z), :], swap_send.at[1], swap_recv.at[1], partner
    )
    give.start()
    keep.wait()
    give.wait_recv()

    def device(xh_, y_, z_, core_):
        return {"band": ((xh_ * 4 + y_) * 8 + z_) * 2 + core_}

    started = []

    def along_z(d, z_, to):
        part = lent.at[:, lax.rem(z_, 2), core, at(xy, z_), :]
        return send(part, part, ag_send.at[d - 1], ag_recv.at[d - 1], device(xh, y, to, core))

    for d in range(1, 8):
        c = along_z(d, z, lax.rem(z + d, 8))
        c.start()
        started.append(c)
    for d in range(1, 8):
        along_z(d, lax.rem(z + 8 - d, 8), z).wait_recv()

    def column(xh_, y_):
        return lent.at[:, :, core, pl.ds(16 * xh_ + 4 * y_, 4), :]

    def copy(part, slot, to):
        return send(part, part, ag_send.at[slot], ag_recv.at[slot], to)

    c = copy(column(xh, y), 7, device(1 - xh, y, z, core))
    c.start()
    started.append(c)
    for d in range(1, 4):
        c = copy(column(xh, y), 7 + d, device(xh, lax.rem(y + d, 4), z, core))
        c.start()
        started.append(c)
    copy(column(1 - xh, y), 7, device(1 - xh, y, z, core)).wait_recv()
    for d in range(1, 4):
        c = copy(column(1 - xh, y), 10 + d, device(xh, lax.rem(y + d, 4), z, core))
        c.start()
        started.append(c)

    def half(xh_, core_):
        return lent.at[:, :, core_, pl.ds(16 * xh_, 16), :]

    for n, x_ in ((7, xh), (10, 1 - xh)):
        for d in range(1, 4):
            copy(column(x_, lax.rem(y + 4 - d, 4)), n + d, device(xh, y, z, core)).wait_recv()
        c = send(half(x_, core), half(x_, core), ag_send.at[n // 3 + 12], ag_recv.at[n // 3 + 12], device(xh, y, z, 1 - core))
        c.start()
        started.append(c)
    for n, x_ in ((7, xh), (10, 1 - xh)):
        send(half(x_, 1 - core), half(x_, 1 - core), ag_send.at[n // 3 + 12], ag_recv.at[n // 3 + 12], device(xh, y, z, core)).wait_recv()
    for c in started:
        c.wait_send()
    whole.wait()
    give.wait_send()

    def sent(k, carry):
        a2a(lax.rem(band + k, BANDS), band).wait_send()
        return carry

    lax.fori_loop(1, BANDS, sent, 0)


def lend_call(owners, orb):
    vm = pl.BlockSpec(memory_space=pltpu.VMEM)
    dma = pltpu.SemaphoreType.DMA
    return pl.pallas_call(
        lend_kernel,
        out_shape=(
            jax.ShapeDtypeStruct((BANDS, CELLS), F32),
            jax.ShapeDtypeStruct((36, 5184), F32),
            jax.ShapeDtypeStruct((2, 2, 2, 32, CELLS), F32),
        ),
        in_specs=[pl.BlockSpec(memory_space=pltpu.SMEM), vm],
        out_specs=(vm, vm, vm),
        scratch_shapes=[
            pltpu.VMEM((2592, 128), F32), pltpu.VMEM((4, 32, CELLS), F32), pltpu.VMEM((2, CELLS), F32),
            dma((BANDS,)), dma((BANDS,)), dma, dma((2,)), dma((2,)), dma((16,)), dma((16,)),
        ],
        compiler_params=pltpu.CompilerParams(collective_id=0, has_side_effects=True, vmem_limit_bytes=32 << 20),
    )(owners, orb)


def matrix_kernel(
    part, cols, field, matrix, summed, arrived, product, first, second,
    a2a_send, a2a_recv, own_sem, swap_send, swap_recv, m_send, m_recv,
):
    band, grid = lax.axis_index("band"), lax.axis_index("grid")
    xy, t = lax.div(band, 16), lax.rem(band, 16)
    barrier = pltpu.get_barrier_semaphore()
    greet_bands(barrier, band)
    for k in range(8):
        greet(barrier, {"band": 16 * lax.rem(xy + k, 8) + t, "grid": 1 - grid})
    pl.semaphore_wait(barrier, BANDS - 1 + 8)
    mine = lax.div(band, 32)

    def octet(k):
        return pl.ds(pl.multiple_of(8 * lax.rem(mine + k, 4), 8), 8)

    def swap(k):
        return send(
            part.at[1, :, octet(k), :], arrived.at[:, octet(k), :], swap_send.at[k], swap_recv.at[k], {"grid": 1 - grid}
        )

    for k in range(4):
        swap(k).start()

    def a2a(to, slot):
        return send(
            summed.at[lax.rem(to, 4), pl.ds(lax.div(to, 4), 1), :],
            field.at[pl.ds(slot, 1), :],
            a2a_send.at[to], a2a_recv.at[slot], {"band": to},
        )

    own = pltpu.make_async_copy(
        summed.at[lax.rem(band, 4), pl.ds(lax.div(band, 4), 1), :], field.at[pl.ds(band, 1), :], own_sem
    )
    for k in range(4):
        swap(k).wait_recv()
        rows = octet(k)
        summed[:, rows, :] = part[0, :, rows, :] + arrived[:, rows, :]

        def start(n, carry):
            to = 32 * lax.rem(mine + k, 4) + lax.rem(band + n, 32)
            a2a(to, band).start()
            return carry

        if k == 0:
            own.start()
        lax.fori_loop(1 if k == 0 else 0, 32, start, 0)

    def finish(k, carry):
        c = lax.rem(band + k, BANDS)
        a2a(c, c).wait_recv()
        return carry

    lax.fori_loop(1, BANDS, finish, 0)
    own.wait()
    oh, ol = halves(cols[...])
    fh, fl = halves(field[...])
    dot = lambda a, b: lax.dot_general(a, b, (((1,), (1,)), ((), ())), preferred_element_type=F32)
    product[...] = ((dot(oh, fl) + dot(ol, fh)) + dot(oh, fh)) * (1.0 / 373248.0)

    def block(c):
        return pl.ds(pl.multiple_of(8 * c, 8), 8)

    def scatter(k, to, slot):
        return send(
            product.at[block(to), :], first.at[slot], m_send.at[k], m_recv.at[k], {"band": 16 * xy + to}
        )

    for k in range(1, 16):
        scatter(k, lax.rem(t + k, 16), t).start()
    first[t] = product[block(t), :]
    for k in range(1, 16):
        scatter(k, t, lax.rem(t + 16 - k, 16)).wait_recv()
    total = first[0]
    for k in range(1, 16):
        total = total + first[k]
    where = 2 * xy + grid
    second[where] = total

    def across(k):
        q, g = k // 2, lax.rem(grid + k, 2)
        return lax.rem(xy + q, 8), g

    def share(k, slot, to):
        return send(second.at[slot], second.at[slot], m_send.at[15 + k], m_recv.at[15 + k], to)

    for k in range(1, 16):
        x_, g_ = across(k)
        share(k, where, {"band": 16 * x_ + t, "grid": g_}).start()
    for k in range(1, 16):
        x_, g_ = lax.rem(xy + 8 - k // 2, 8), lax.rem(grid + k, 2)
        share(k, 2 * x_ + g_, {"band": 16 * x_ + t, "grid": g_}).wait_recv()
    total = second[0]
    for k in range(1, 16):
        total = total + second[k]
    matrix[block(t), :] = total

    def spread(k, to, slot):
        return send(
            matrix.at[block(slot), :], matrix.at[block(slot), :], m_send.at[30 + k], m_recv.at[30 + k],
            {"band": 16 * xy + to},
        )

    for k in range(1, 16):
        spread(k, lax.rem(t + k, 16), t).start()
    for k in range(1, 16):
        spread(k, t, lax.rem(t + 16 - k, 16)).wait_recv()
    for k in range(4):
        swap(k).wait_send()
    for k in range(1, 16):
        scatter(k, lax.rem(t + k, 16), t).wait_send()
        share(k, where, {"grid": 1 - grid}).wait_send()
        spread(k, lax.rem(t + k, 16), t).wait_send()

    def sent(k, carry):
        a2a(lax.rem(band + k, BANDS), band).wait_send()
        return carry

    lax.fori_loop(1, BANDS, sent, 0)


def matrix_call(part, cols):
    vm = pl.BlockSpec(memory_space=pltpu.VMEM)
    dma = pltpu.SemaphoreType.DMA
    return pl.pallas_call(
        matrix_kernel,
        out_shape=(
            jax.ShapeDtypeStruct((BANDS, CELLS), F32),
            jax.ShapeDtypeStruct((BANDS, BANDS), F32),
        ),
        in_specs=[vm, vm],
        out_specs=(vm, vm),
        scratch_shapes=[
            pltpu.VMEM((4, 32, CELLS), F32), pltpu.VMEM((4, 32, CELLS), F32), pltpu.VMEM((BANDS, BANDS), F32),
            pltpu.VMEM((16, 8, BANDS), F32), pltpu.VMEM((16, 8, BANDS), F32),
            dma((BANDS,)), dma((BANDS,)), dma, dma((4,)), dma((4,)), dma((46,)), dma((46,)),
        ],
        compiler_params=pltpu.CompilerParams(collective_id=1, has_side_effects=True, vmem_limit_bytes=32 << 20),
    )(part, cols)


def shards(orbitals, owners):
    mine = orbitals[0]
    cols, other, lent = lend_call(owners, mine)
    part = fft_call(mine, other, lent.reshape(2, 4, 32, CELLS))
    field, matrix = matrix_call(part, cols)
    return (field[None], matrix)


def solution(mesh):
    in_specs = (P("band", "grid", None), P())
    out_specs = (P("grid", None, "band"), P())
    return jax.shard_map(shards, mesh=mesh, in_specs=in_specs, out_specs=out_specs, check_vma=False)
```

```python
import functools
import math

import jax
import jax.numpy as jnp
import numpy as np
from jax import lax
from jax.experimental import pallas as pl
from jax.experimental.pallas import tpu as pltpu
from jax.sharding import PartitionSpec as P

N = 72
PAD = 80
BF = jnp.bfloat16
F32 = jnp.float32

def tables():
    pos = np.arange(N)
    half = N // 2
    freq = np.where(pos <= half, pos, pos - half)
    ang = (freq[:, None] * pos[None, :] % N) * (2.0 * math.pi / N)
    w = np.where((pos == 0) | (pos == half), 1.0 / math.sqrt(N), math.sqrt(2.0 / N))
    basis = np.where((pos <= half)[:, None], np.cos(ang), np.sin(ang)) * w[:, None]
    sq = (freq * (2.0 * math.pi / N)) ** 2

    def split(t):
        hi = jnp.asarray(t, F32).astype(BF)
        lo = (jnp.asarray(t, F32) - hi.astype(F32)).astype(BF)
        return hi, lo

    def left(t):
        hi, lo = split(t)
        put = lambda a: jnp.pad(a, ((0, PAD - N), (0, PAD - N)))
        return jnp.concatenate([put(hi), put(hi), put(lo)], axis=1)

    def right(t):
        hi, lo = split(t)
        put = lambda a: jnp.pad(a, ((0, 128 - N), (0, 128 - N)))
        top = jnp.concatenate([put(hi), put(lo)], axis=1)
        low = jnp.concatenate([put(hi), jnp.zeros((128, 128), BF)], axis=1)
        return jnp.concatenate([top, low], axis=0)

    sq_rows = np.zeros((PAD, 128), np.float32); sq_rows[:N] = sq[:, None]
    sq_pair = np.zeros((N, 128), np.float32); sq_pair[:, :N] = sq[:, None] + sq[None, :]
    return (left(basis), left(basis.T), right(basis.T), right(basis), jnp.asarray(sq_rows), jnp.asarray(sq_pair))


def halves(v):
    hi = v.astype(BF)
    lo = (v - hi.astype(F32)).astype(BF)
    return hi, lo


def left_dot(table, planes):
    cols = []
    for v in planes:
        hi, lo = halves(v)
        cols.append(jnp.concatenate([hi, lo, hi], axis=0))
    out = jnp.dot(table, jnp.concatenate(cols, axis=1), preferred_element_type=F32)
    return [out[:, 128 * i : 128 * i + 128] for i in range(len(planes))]


def right_dot(v, table):
    hi, lo = halves(v)
    out = jnp.dot(jnp.concatenate([hi, lo], axis=1), table, preferred_element_type=F32)
    return out[:, :128] + out[:, 128:]


def pad_rows(v):
    return jnp.concatenate([v, jnp.zeros((PAD - N, 128), F32)], axis=0)


def convolve(own, lent, work, tl, til, tr, tir, sq_rows, sq_pair, UA, UB, UC):
    lane = lax.broadcasted_iota(jnp.int32, (1, 128), 1) < N

    def stage_a(step, carry):
        for u in range(UA):
            base = pl.multiple_of((step * UA + u) * 2 * N, 8)
            rows = pl.ds(base, 2 * N)
            d = jnp.where(lane, own[rows, :] * lent[rows, :], 0.0)
            z = right_dot(d, tr[...])
            a, b = left_dot(tl[...], [pad_rows(z[:N]), pad_rows(z[N:])])
            work[rows, :] = jnp.concatenate([a[:N], b[:N]], axis=0)
        return carry

    lax.fori_loop(0, 36 // UA, stage_a, 0)

    def stage_b(step, carry):
        for u in range(UB):
            b = (step * UB + u) * 2
            planes = [pad_rows(work[pl.ds(b + i, N, stride=N), :]) for i in range(2)]
            planes = left_dot(tl[...], planes)
            for i in range(2):
                total = sq_rows[...] + sq_pair[pl.ds(b + i, 1), :]
                positive = total > 0
                kern = jnp.where(positive, (-0.25 * math.pi) / jnp.where(positive, total, 1.0), 0.0)
                planes[i] = planes[i] * kern
            planes = left_dot(til[...], planes)
            for i in range(2):
                work[pl.ds(b + i, N, stride=N), :] = planes[i][:N]
        return carry

    lax.fori_loop(0, 36 // UB, stage_b, 0)

    def stage_c(step, carry):
        for u in range(UC):
            base = pl.multiple_of((step * UC + u) * 2 * N, 8)
            rows = pl.ds(base, 2 * N)
            v = work[rows, :]
            a, b = left_dot(til[...], [pad_rows(v[:N]), pad_rows(v[N:])])
            z = right_dot(jnp.concatenate([a[:N], b[:N]], axis=0), tir[...])
            own[rows, :] = z * lent[rows, :]
        return carry

    lax.fori_loop(0, 36 // UC, stage_c, 0)


def from_plane(ref, dst, slab):
    for y in range(N):
        dst[pl.ds(slab * 2592 + y, 36, stride=N), :N] = ref[:, N * y : N * y + N]


def spans():
    for j in range(81):
        first, at = divmod(N * j, 1458)
        fit = min(N, 1458 - at)
        yield j, first, at, fit


def from_blocks(ref, dst, slab):
    for j, first, at, fit in spans():
        rows = pl.ds(slab * 2592 + j, 32, stride=81)
        v = ref[first, :, at : at + fit]
        if fit < N:
            v = jnp.concatenate([v, ref[first + 1, :, : N - fit]], axis=1)
        dst[rows, :N] = v


def to_blocks(src, ref, slab):
    for h in range(4):
        for j, first, at, fit in spans():
            v = src[pl.ds(slab * 2592 + 81 * h + j, 8, stride=324), :]
            ref[4 * first + h, :, at : at + fit] = v[:, :fit]
            if fit < N:
                ref[4 * first + 4 + h, :, : N - fit] = v[:, fit:N]


def fft_kernel(U, whole, lent_in, tl, til, tr, tir, sq_rows, sq_pair, out, own, lent, work):
    for s in range(2):
        from_plane(whole.at[s], own, s)
        from_blocks(lent_in.at[s], lent, s)
    convolve(own, lent, work, tl, til, tr, tir, sq_rows, sq_pair, *U)
    for s in range(2):
        to_blocks(own, out.at[s], s)


def fft_call(whole, lent, U=(9, 9, 9)):
    vm = pl.BlockSpec(memory_space=pltpu.VMEM)
    return pl.pallas_call(
        functools.partial(fft_kernel, U),
        out_shape=jax.ShapeDtypeStruct((2, 16, 8, 1458), F32),
        in_specs=[vm] * 8,
        out_specs=vm,
        scratch_shapes=[pltpu.VMEM((5184, 128), F32) for _ in range(3)],
        compiler_params=pltpu.CompilerParams(vmem_limit_bytes=48 << 20),
    )(whole, lent, *tables())


MESH = pl.DeviceIdType.MESH
BANDS = 128
CELLS = 1458
CUT = 768


def send(src, dst, send_sem, recv_sem, device):
    return pltpu.make_async_remote_copy(
        src_ref=src, dst_ref=dst, send_sem=send_sem, recv_sem=recv_sem, device_id=device, device_id_type=MESH
    )


def greet(barrier, device):
    pl.semaphore_signal(barrier, inc=1, device_id=device, device_id_type=MESH)


class Place:
    def __init__(self):
        self.band, self.grid = lax.axis_index("band"), lax.axis_index("grid")
        self.p, self.q = lax.div(self.band, 16), lax.rem(self.band, 16)
        self.z, self.core = lax.div(self.q, 2), lax.rem(self.q, 2)
        self.xh, self.y = lax.div(self.p, 4), lax.rem(self.p, 4)
        self.twin = {"band": self.band + 1 - 2 * self.core}


def device(p, q, grid):
    return {"band": p * 16 + q, "grid": grid}


def meet(me):
    barrier = pltpu.get_barrier_semaphore()

    def near(k, carry):
        w = lax.rem(me.q * 2 + me.grid + k, 32)
        greet(barrier, device(me.p, lax.div(w, 2), lax.rem(w, 2)))
        return carry

    lax.fori_loop(1, 32, near, 0)

    def far(k, carry):
        p = lax.rem(me.p + k, 8)
        for n in range(4):
            greet(barrier, device(p, me.z * 2 + n // 2, n % 2))
        return carry

    lax.fori_loop(1, 8, far, 0)
    return barrier


MET = 31 + 28


def lane_parts():
    return pl.ds(0, CUT), pl.ds(CUT, CELLS - CUT)


def exchange(me, blocks, via_a, via_b, cols, slot, grid_to, sems):
    s1, r1, s2, r2, s3, r3, s4, r4, local = sems
    low, high = lane_parts()
    stays = jnp.logical_and(slot == me.q, grid_to == me.grid)
    moves = jnp.logical_not(stays)

    def seat(q):
        return lax.rem(q, 4) * 4 + lax.div(q, 4)

    def a1(k, p_to, p_from):
        return send(blocks.at[:, p_to, low], via_a.at[p_from], s1.at[k], r1.at[k], device(p_to, slot, grid_to))

    def b1(k, q_to, q_from):
        return send(blocks.at[seat(q_to), :, high], via_b.at[q_from], s2.at[k], r2.at[q_from], device(me.p, q_to, grid_to))

    def a2(k, q_to, q_from):
        return send(via_a.at[:, seat(q_to), :], cols.at[:, q_from, low], s3.at[k], r3.at[k], device(me.p, q_to, me.grid))

    def b2(k, p_to, p_from):
        return send(via_b.at[:, p_to, :], cols.at[p_from, :, high], s4.at[k], r4.at[k], device(p_to, me.q, me.grid))

    keep_a1 = pltpu.make_async_copy(blocks.at[:, me.p, low], via_a.at[me.p], local.at[0])
    keep_b1 = pltpu.make_async_copy(blocks.at[seat(me.q), :, high], via_b.at[me.q], local.at[1])
    keep_a2 = pltpu.make_async_copy(via_a.at[:, seat(me.q), :], cols.at[:, me.q, low], local.at[2])
    keep_b2 = pltpu.make_async_copy(via_b.at[:, me.p, :], cols.at[me.p, :, high], local.at[3])

    for k in range(1, 8):
        a1(k, lax.rem(me.p + k, 8), me.p).start()
    for k in range(1, 16):
        b1(k, lax.rem(me.q + k, 16), slot).start()

    @pl.when(stays)
    def _():
        keep_a1.start()
        keep_b1.start()

    @pl.when(moves)
    def _():
        a1(0, me.p, me.p).start()
        b1(0, me.q, slot).start()

    def middle_a():
        for k in range(1, 8):
            a1(k, me.p, lax.rem(me.p + 8 - k, 8)).wait_recv()

        @pl.when(stays)
        def _():
            keep_a1.wait()

        @pl.when(moves)
        def _():
            a1(0, me.p, me.p).wait_recv()

        for k in range(1, 16):
            a2(k, lax.rem(me.q + k, 16), me.q).start()
        keep_a2.start()

    def middle_b():
        for k in range(1, 16):
            b1(k, me.q, lax.rem(me.q + k, 16)).wait_recv()

        @pl.when(stays)
        def _():
            keep_b1.wait()

        @pl.when(moves)
        def _():
            b1(0, me.q, me.q).wait_recv()

        for k in range(1, 8):
            b2(k, lax.rem(me.p + k, 8), me.p).start()
        keep_b2.start()

    def finish():
        for k in range(1, 16):
            a2(k, me.q, lax.rem(me.q + 16 - k, 16)).wait_recv()
        for k in range(1, 8):
            b2(k, me.p, lax.rem(me.p + 8 - k, 8)).wait_recv()
        keep_a2.wait()
        keep_b2.wait()

    def drain():
        for k in range(1, 8):
            a1(k, lax.rem(me.p + k, 8), me.p).wait_send()
            b2(k, lax.rem(me.p + k, 8), me.p).wait_send()
        for k in range(1, 16):
            b1(k, lax.rem(me.q + k, 16), slot).wait_send()
            a2(k, lax.rem(me.q + k, 16), me.q).wait_send()

        @pl.when(moves)
        def _():
            a1(0, me.p, me.p).wait_send()
            b1(0, me.q, slot).wait_send()

    return middle_a, middle_b, finish, drain


def exchange_scratch():
    dma = pltpu.SemaphoreType.DMA
    return [
        pltpu.VMEM((8, 16, CUT), F32), pltpu.VMEM((16, 8, CELLS - CUT), F32),
        dma((8,)), dma((8,)), dma((16,)), dma((16,)), dma((16,)), dma((16,)), dma((8,)), dma((8,)), dma((4,)),
    ]


def gather_lent(me, picked, lent, send_sem, recv_sem, local):
    zlo, zhi = lax.rem(me.z, 2), lax.div(me.z, 2)

    def cell(q):
        z = lax.div(q, 2)
        return lent.at[me.grid, lax.rem(z, 2), lax.rem(q, 2), me.xh, pl.ds(4 * me.y + lax.div(z, 2), 1), :]

    def over_q(k, q_to, q_from):
        return send(
            picked.at[pl.ds(lax.rem(q_to, 2), 1), :], cell(q_from), send_sem.at[k], recv_sem.at[k],
            device(me.p, q_to, me.grid),
        )

    keep = pltpu.make_async_copy(picked.at[pl.ds(me.core, 1), :], cell(me.q), local)
    for k in range(1, 16):
        over_q(k, lax.rem(me.q + k, 16), me.q).start()
    keep.start()
    for k in range(1, 16):
        over_q(k, me.q, lax.rem(me.q + 16 - k, 16)).wait_recv()
    keep.wait()

    def piece(half, grid, xh, y):
        return lent.at[grid, :, half, xh, pl.ds(4 * y, 4), :]

    started = []

    def x_peer(n):
        return lax.rem(me.xh + n // 2, 2), lax.rem(me.grid + n, 2)

    def along_x(slot, half, y, n):
        xh, grid = x_peer(n)
        part = piece(half, me.grid, me.xh, y)
        return send(part, part, send_sem.at[slot + n], recv_sem.at[slot + n], device(4 * xh + me.y, me.q, grid))

    def from_x(slot, half, y, n):
        xh, grid = x_peer(n)
        part = piece(half, grid, xh, y)
        return send(part, part, send_sem.at[slot + n], recv_sem.at[slot + n], device(4 * xh + me.y, me.q, grid))

    def along_y(slot, half, xh, grid, n):
        part = piece(half, grid, xh, me.y)
        return send(part, part, send_sem.at[slot + n], recv_sem.at[slot + n], device(4 * me.xh + lax.rem(me.y + n, 4), me.q, me.grid))

    def from_y(slot, half, xh, grid, n):
        part = piece(half, grid, xh, lax.rem(me.y + 4 - n, 4))
        return send(part, part, send_sem.at[slot + n], recv_sem.at[slot + n], device(4 * me.xh + lax.rem(me.y + n, 4), me.q, me.grid))

    def go(copy):
        copy.start()
        started.append(copy)

    for n in range(1, 4):
        go(along_x(16, 0, me.y, n))
        go(along_y(20, 1, me.xh, me.grid, n))
    for n in range(1, 4):
        go(along_y(24, 0, me.xh, me.grid, n))
        go(along_x(40, 1, me.y, n))
    for m in range(1, 4):
        from_x(16, 0, me.y, m).wait_recv()
        xh, grid = x_peer(m)
        for n in range(1, 4):
            go(along_y(24 + 4 * m, 0, xh, grid, n))
        from_y(20, 1, me.xh, me.grid, m).wait_recv()
        for n in range(1, 4):
            go(along_x(40 + 4 * m, 1, lax.rem(me.y + 4 - m, 4), n))
    for m in range(4):
        xh, grid = x_peer(m)
        for n in range(1, 4):
            from_y(24 + 4 * m, 0, xh, grid, n).wait_recv()
            from_x(40 + 4 * m, 1, lax.rem(me.y + 4 - m, 4), n).wait_recv()

    def drain():
        for k in range(1, 16):
            over_q(k, lax.rem(me.q + k, 16), me.q).wait_send()
        for c in started:
            c.wait_send()

    return drain


def lend_kernel(
    owners, orb, cols, whole, lent, rows, blocks, picked, own_sem, w_send, w_recv, g_send, g_recv,
    via_a, via_b, *sems,
):
    me = Place()
    partner = {"grid": 1 - me.grid}
    barrier = meet(me)
    from_plane(orb, rows, 0)
    to_blocks(rows, blocks, 0)
    pl.semaphore_wait(barrier, MET)
    same = me.core == me.grid
    differ = jnp.logical_not(same)
    middle_a, middle_b, finish, drain = exchange(me, blocks, via_a, via_b, cols, me.q, me.grid, sems)
    keep = pltpu.make_async_copy(orb, whole.at[me.grid], own_sem.at[0])
    to_twin = send(orb, whole.at[me.grid], w_send.at[0], w_recv.at[0], me.twin)
    to_partner = send(orb, whole.at[me.grid], w_send.at[0], w_recv.at[1], partner)
    from_partner = send(orb, whole.at[1 - me.grid], w_send.at[0], w_recv.at[1], partner)
    forward = send(whole.at[1 - me.grid], whole.at[1 - me.grid], w_send.at[1], w_recv.at[1], me.twin)

    @pl.when(same)
    def _():
        keep.start()
        to_twin.start()

    @pl.when(differ)
    def _():
        to_partner.start()

    middle_a()
    middle_b()
    finish()
    for r in range(2):
        owner = owners[r]
        picked[r : r + 1, :] = cols[pl.ds(lax.div(owner, 16), 1), pl.ds(lax.rem(owner, 16), 1), :].reshape(1, CELLS)

    @pl.when(same)
    def _():
        from_partner.wait_recv()
        forward.start()

    drain_gather = gather_lent(me, picked, lent, g_send, g_recv, own_sem.at[1])

    @pl.when(same)
    def _():
        keep.wait()
        to_twin.wait_send()
        forward.wait_send()

    @pl.when(differ)
    def _():
        to_twin.wait_recv()
        forward.wait_recv()
        to_partner.wait_send()

    drain_gather()
    drain()


def lend_call(owners, orb):
    vm = pl.BlockSpec(memory_space=pltpu.VMEM)
    dma = pltpu.SemaphoreType.DMA
    return pl.pallas_call(
        lend_kernel,
        out_shape=(
            jax.ShapeDtypeStruct((8, 16, CELLS), F32),
            jax.ShapeDtypeStruct((2, 36, 5184), F32),
            jax.ShapeDtypeStruct((2, 2, 2, 2, 16, CELLS), F32),
        ),
        in_specs=[pl.BlockSpec(memory_space=pltpu.SMEM), vm],
        out_specs=(vm, vm, vm),
        scratch_shapes=[
            pltpu.VMEM((2592, 128), F32), pltpu.VMEM((16, 8, CELLS), F32), pltpu.VMEM((2, CELLS), F32),
            dma((2,)), dma((2,)), dma((2,)), dma((56,)), dma((56,)),
        ] + exchange_scratch(),
        compiler_params=pltpu.CompilerParams(collective_id=0, has_side_effects=True, vmem_limit_bytes=40 << 20),
    )(owners, orb)


def add_up(me, product, matrix, first, second, m_send, m_recv):
    p, q, grid = me.p, me.q, me.grid

    def block(c):
        return pl.ds(pl.multiple_of(8 * c, 8), 8)

    def scatter(k, to, slot):
        return send(product.at[block(to), :], first.at[slot], m_send.at[k], m_recv.at[k], device(p, to, grid))

    for k in range(1, 16):
        scatter(k, lax.rem(q + k, 16), q).start()
    first[q] = product[block(q), :]
    for k in range(1, 16):
        scatter(k, q, lax.rem(q + 16 - k, 16)).wait_recv()
    total = first[0]
    for k in range(1, 16):
        total = total + first[k]
    where = 2 * p + grid
    second[where] = total

    def share(k, slot, p_to, g_to):
        return send(second.at[slot], second.at[slot], m_send.at[15 + k], m_recv.at[15 + k], device(p_to, q, g_to))

    for k in range(1, 16):
        share(k, where, lax.rem(p + k // 2, 8), lax.rem(grid + k, 2)).start()
    for k in range(1, 16):
        p_, g_ = lax.rem(p + 8 - k // 2, 8), lax.rem(grid + k, 2)
        share(k, 2 * p_ + g_, p_, g_).wait_recv()
    total = second[0]
    for k in range(1, 16):
        total = total + second[k]
    matrix[block(q), :] = total

    def spread(k, to, slot):
        return send(
            matrix.at[block(slot), :], matrix.at[block(slot), :], m_send.at[30 + k], m_recv.at[30 + k],
            device(p, to, grid),
        )

    for k in range(1, 16):
        spread(k, lax.rem(q + k, 16), q).start()
    for k in range(1, 16):
        spread(k, q, lax.rem(q + 16 - k, 16)).wait_recv()

    for k in range(1, 16):
        scatter(k, lax.rem(q + k, 16), q).wait_send()
        share(k, where, lax.rem(p + k // 2, 8), lax.rem(grid + k, 2)).wait_send()
        spread(k, lax.rem(q + k, 16), q).wait_send()


def matrix_kernel(
    part, cols, field, matrix, summed, arrived, product, first, second, t_send, t_recv, m_send, m_recv,
    via_a, via_b, *sems,
):
    me = Place()
    barrier = meet(me)
    pl.semaphore_wait(barrier, MET)

    def give(n):
        piece = pl.ds(4 * n, 4)
        return send(part.at[1 - me.core, piece], arrived.at[piece], t_send.at[n], t_recv.at[n], me.twin)

    for n in range(4):
        give(n).start()
    for n in range(4):
        give(n).wait_recv()
        piece = pl.ds(4 * n, 4)
        summed[piece] = part[me.core, piece] + arrived[piece]
    middle_a, middle_b, finish, drain = exchange(
        me, summed, via_a, via_b, field, 2 * me.z + me.grid, me.core, sems
    )
    middle_a()
    middle_b()
    finish()
    oh, ol = halves(cols[...].reshape(BANDS, CELLS))
    fh, fl = halves(field[...].reshape(BANDS, CELLS))
    dot = lambda a, b: lax.dot_general(a, b, (((1,), (1,)), ((), ())), preferred_element_type=F32)
    product[...] = ((dot(oh, fl) + dot(ol, fh)) + dot(oh, fh)) * (1.0 / 373248.0)
    add_up(me, product, matrix, first, second, m_send, m_recv)
    for n in range(4):
        give(n).wait_send()
    drain()


def matrix_call(part, cols):
    vm = pl.BlockSpec(memory_space=pltpu.VMEM)
    dma = pltpu.SemaphoreType.DMA
    return pl.pallas_call(
        matrix_kernel,
        out_shape=(
            jax.ShapeDtypeStruct((8, 16, CELLS), F32),
            jax.ShapeDtypeStruct((BANDS, BANDS), F32),
        ),
        in_specs=[vm, vm],
        out_specs=(vm, vm),
        scratch_shapes=[
            pltpu.VMEM((16, 8, CELLS), F32), pltpu.VMEM((16, 8, CELLS), F32), pltpu.VMEM((BANDS, BANDS), F32),
            pltpu.VMEM((16, 8, BANDS), F32), pltpu.VMEM((16, 8, BANDS), F32),
            dma((4,)), dma((4,)), dma((46,)), dma((46,)),
        ] + exchange_scratch(),
        compiler_params=pltpu.CompilerParams(collective_id=1, has_side_effects=True, vmem_limit_bytes=40 << 20),
    )(part, cols)


def shards(orbitals, owners):
    cols, whole, lent = lend_call(owners, orbitals[0])
    part = fft_call(whole, lent.reshape(2, 4, 32, CELLS))
    field, matrix = matrix_call(part, cols)
    return (field.reshape(1, BANDS, CELLS), matrix)


def solution(mesh):
    in_specs = (P("band", "grid", None), P())
    out_specs = (P("grid", None, "band"), P())
    return jax.shard_map(shards, mesh=mesh, in_specs=in_specs, out_specs=out_specs, check_vma=False)
```

```python
import functools
import math

import jax
import jax.numpy as jnp
import numpy as np
from jax import lax
from jax.experimental import pallas as pl
from jax.experimental.pallas import tpu as pltpu
from jax.sharding import PartitionSpec as P

N = 72
PAD = 80
BF = jnp.bfloat16
F32 = jnp.float32

def tables():
    pos = np.arange(N)
    half = N // 2
    freq = np.where(pos <= half, pos, pos - half)
    ang = (freq[:, None] * pos[None, :] % N) * (2.0 * math.pi / N)
    w = np.where((pos == 0) | (pos == half), 1.0 / math.sqrt(N), math.sqrt(2.0 / N))
    basis = np.where((pos <= half)[:, None], np.cos(ang), np.sin(ang)) * w[:, None]
    sq = (freq * (2.0 * math.pi / N)) ** 2

    def split(t):
        hi = jnp.asarray(t, F32).astype(BF)
        lo = (jnp.asarray(t, F32) - hi.astype(F32)).astype(BF)
        return hi, lo

    def left(t):
        hi, lo = split(t)
        put = lambda a: jnp.pad(a, ((0, PAD - N), (0, PAD - N)))
        return jnp.concatenate([put(hi), put(hi), put(lo)], axis=1)

    def right(t):
        hi, lo = split(t)
        put = lambda a: jnp.pad(a, ((0, 128 - N), (0, 128 - N)))
        top = jnp.concatenate([put(hi), put(lo)], axis=1)
        low = jnp.concatenate([put(hi), jnp.zeros((128, 128), BF)], axis=1)
        return jnp.concatenate([top, low], axis=0)

    sq_rows = np.zeros((PAD, 128), np.float32); sq_rows[:N] = sq[:, None]
    sq_pair = np.zeros((N, 128), np.float32); sq_pair[:, :N] = sq[:, None] + sq[None, :]
    return (left(basis), left(basis.T), right(basis.T), right(basis), jnp.asarray(sq_rows), jnp.asarray(sq_pair))


def halves(v):
    hi = v.astype(BF)
    lo = (v - hi.astype(F32)).astype(BF)
    return hi, lo


def left_dot(table, planes):
    cols = []
    for v in planes:
        hi, lo = halves(v)
        cols.append(jnp.concatenate([hi, lo, hi], axis=0))
    out = jnp.dot(table, jnp.concatenate(cols, axis=1), preferred_element_type=F32)
    return [out[:, 128 * i : 128 * i + 128] for i in range(len(planes))]


def right_dot(v, table):
    hi, lo = halves(v)
    out = jnp.dot(jnp.concatenate([hi, lo], axis=1), table, preferred_element_type=F32)
    return out[:, :128] + out[:, 128:]


def pad_rows(v):
    return jnp.concatenate([v, jnp.zeros((PAD - N, 128), F32)], axis=0)


def spectra(own, lent, work, tl, til, tr, sq_rows, sq_pair, UA, UB):
    lane = lax.broadcasted_iota(jnp.int32, (1, 128), 1) < N

    def stage_a(step, carry):
        for u in range(UA):
            base = pl.multiple_of((step * UA + u) * 2 * N, 8)
            rows = pl.ds(base, 2 * N)
            d = jnp.where(lane, own[rows, :] * lent[rows, :], 0.0)
            z = right_dot(d, tr[...])
            a, b = left_dot(tl[...], [pad_rows(z[:N]), pad_rows(z[N:])])
            work[rows, :] = jnp.concatenate([a[:N], b[:N]], axis=0)
        return carry

    lax.fori_loop(0, 36 // UA, stage_a, 0)

    def stage_b(step, carry):
        for u in range(UB):
            b = (step * UB + u) * 2
            planes = [pad_rows(work[pl.ds(b + i, N, stride=N), :]) for i in range(2)]
            planes = left_dot(tl[...], planes)
            for i in range(2):
                total = sq_rows[...] + sq_pair[pl.ds(b + i, 1), :]
                positive = total > 0
                kern = jnp.where(positive, (-0.25 * math.pi) / jnp.where(positive, total, 1.0), 0.0)
                planes[i] = planes[i] * kern
            planes = left_dot(til[...], planes)
            for i in range(2):
                work[pl.ds(b + i, N, stride=N), :] = planes[i][:N]
        return carry

    lax.fori_loop(0, 36 // UB, stage_b, 0)


def potentials(own, lent, work, til, tir, slab, UC):
    def stage_c(step, carry):
        for u in range(UC):
            base = pl.multiple_of(slab * 2592 + (step * UC + u) * 2 * N, 8)
            rows = pl.ds(base, 2 * N)
            v = work[rows, :]
            a, b = left_dot(til[...], [pad_rows(v[:N]), pad_rows(v[N:])])
            z = right_dot(jnp.concatenate([a[:N], b[:N]], axis=0), tir[...])
            own[rows, :] = z * lent[rows, :]
        return carry

    lax.fori_loop(0, 18 // UC, stage_c, 0)


def from_plane(ref, dst, slab):
    for y in range(N):
        dst[pl.ds(slab * 2592 + y, 36, stride=N), :N] = ref[:, N * y : N * y + N]


def spans():
    for j in range(81):
        first, at = divmod(N * j, 1458)
        fit = min(N, 1458 - at)
        yield j, first, at, fit


def from_blocks(ref, dst, slab):
    for j, first, at, fit in spans():
        rows = pl.ds(slab * 2592 + j, 32, stride=81)
        v = ref[first // 2, first % 2, :, at : at + fit]
        if fit < N:
            v = jnp.concatenate([v, ref[(first + 1) // 2, (first + 1) % 2, :, : N - fit]], axis=1)
        dst[rows, :N] = v


def to_blocks(src, ref, slab):
    for h in range(4):
        for j, first, at, fit in spans():
            v = src[pl.ds(slab * 2592 + 81 * h + j, 8, stride=324), :]
            ref[4 * first + h, :, at : at + fit] = v[:, :fit]
            if fit < N:
                ref[4 * first + 4 + h, :, : N - fit] = v[:, fit:N]


MESH = pl.DeviceIdType.MESH
BANDS = 128
CELLS = 1458
CUT = 768


def send(src, dst, send_sem, recv_sem, device):
    return pltpu.make_async_remote_copy(
        src_ref=src, dst_ref=dst, send_sem=send_sem, recv_sem=recv_sem, device_id=device, device_id_type=MESH
    )


def greet(barrier, device):
    pl.semaphore_signal(barrier, inc=1, device_id=device, device_id_type=MESH)


class Place:
    def __init__(self):
        self.band, self.grid = lax.axis_index("band"), lax.axis_index("grid")
        self.p, self.q = lax.div(self.band, 16), lax.rem(self.band, 16)
        self.z, self.core = lax.div(self.q, 2), lax.rem(self.q, 2)
        self.xh, self.y = lax.div(self.p, 4), lax.rem(self.p, 4)
        self.twin = {"band": self.band + 1 - 2 * self.core}


def device(p, q, grid):
    return {"band": p * 16 + q, "grid": grid}


def meet(me):
    barrier = pltpu.get_barrier_semaphore()

    def near(k, carry):
        w = lax.rem(me.q * 2 + me.grid + k, 32)
        greet(barrier, device(me.p, lax.div(w, 2), lax.rem(w, 2)))
        return carry

    lax.fori_loop(1, 32, near, 0)

    def far(k, carry):
        p = lax.rem(me.p + k, 8)
        for n in range(4):
            greet(barrier, device(p, me.z * 2 + n // 2, n % 2))
        return carry

    lax.fori_loop(1, 8, far, 0)
    return barrier


MET = 31 + 28


def lane_parts():
    return pl.ds(0, CUT), pl.ds(CUT, CELLS - CUT)


def exchange(me, blocks, via_a, via_b, cols, slot, grid_to, sems):
    s1, r1, s2, r2, s3, r3, s4, r4, local = sems
    low, high = lane_parts()
    stays = jnp.logical_and(slot == me.q, grid_to == me.grid)
    moves = jnp.logical_not(stays)

    def seat(q):
        return lax.rem(q, 4) * 4 + lax.div(q, 4)

    def a1(k, p_to, p_from):
        return send(blocks.at[:, p_to, low], via_a.at[p_from], s1.at[k], r1.at[k], device(p_to, slot, grid_to))

    def b1(k, q_to, q_from):
        return send(blocks.at[seat(q_to), :, high], via_b.at[q_from], s2.at[k], r2.at[q_from], device(me.p, q_to, grid_to))

    def a2(k, q_to, q_from):
        return send(via_a.at[:, seat(q_to), :], cols.at[:, q_from, low], s3.at[k], r3.at[k], device(me.p, q_to, me.grid))

    def b2(k, p_to, p_from):
        return send(via_b.at[:, p_to, :], cols.at[p_from, :, high], s4.at[k], r4.at[k], device(p_to, me.q, me.grid))

    keep_a1 = pltpu.make_async_copy(blocks.at[:, me.p, low], via_a.at[me.p], local.at[0])
    keep_b1 = pltpu.make_async_copy(blocks.at[seat(me.q), :, high], via_b.at[me.q], local.at[1])
    keep_a2 = pltpu.make_async_copy(via_a.at[:, seat(me.q), :], cols.at[:, me.q, low], local.at[2])
    keep_b2 = pltpu.make_async_copy(via_b.at[:, me.p, :], cols.at[me.p, :, high], local.at[3])

    for k in range(1, 8):
        a1(k, lax.rem(me.p + k, 8), me.p).start()
    for k in range(1, 16):
        b1(k, lax.rem(me.q + k, 16), slot).start()

    @pl.when(stays)
    def _():
        keep_a1.start()
        keep_b1.start()

    @pl.when(moves)
    def _():
        a1(0, me.p, me.p).start()
        b1(0, me.q, slot).start()

    def middle_a():
        for k in range(1, 8):
            a1(k, me.p, lax.rem(me.p + 8 - k, 8)).wait_recv()

        @pl.when(stays)
        def _():
            keep_a1.wait()

        @pl.when(moves)
        def _():
            a1(0, me.p, me.p).wait_recv()

        for k in range(1, 16):
            a2(k, lax.rem(me.q + k, 16), me.q).start()
        keep_a2.start()

    def middle_b():
        for k in range(1, 16):
            b1(k, me.q, lax.rem(me.q + k, 16)).wait_recv()

        @pl.when(stays)
        def _():
            keep_b1.wait()

        @pl.when(moves)
        def _():
            b1(0, me.q, me.q).wait_recv()

        for k in range(1, 8):
            b2(k, lax.rem(me.p + k, 8), me.p).start()
        keep_b2.start()

    def finish():
        for k in range(1, 16):
            a2(k, me.q, lax.rem(me.q + 16 - k, 16)).wait_recv()
        for k in range(1, 8):
            b2(k, me.p, lax.rem(me.p + 8 - k, 8)).wait_recv()
        keep_a2.wait()
        keep_b2.wait()

    def drain():
        for k in range(1, 8):
            a1(k, lax.rem(me.p + k, 8), me.p).wait_send()
            b2(k, lax.rem(me.p + k, 8), me.p).wait_send()
        for k in range(1, 16):
            b1(k, lax.rem(me.q + k, 16), slot).wait_send()
            a2(k, lax.rem(me.q + k, 16), me.q).wait_send()

        @pl.when(moves)
        def _():
            a1(0, me.p, me.p).wait_send()
            b1(0, me.q, slot).wait_send()

    return middle_a, middle_b, finish, drain


def exchange_scratch():
    dma = pltpu.SemaphoreType.DMA
    return [
        pltpu.VMEM((8, 16, CUT), F32), pltpu.VMEM((16, 8, CELLS - CUT), F32),
        dma((8,)), dma((8,)), dma((16,)), dma((16,)), dma((16,)), dma((16,)), dma((8,)), dma((8,)), dma((4,)),
    ]


def gather_lent(me, picked, lent, send_sem, recv_sem, local, meanwhile):
    zlo, zhi = lax.rem(me.z, 2), lax.div(me.z, 2)

    def cell(q):
        z = lax.div(q, 2)
        return lent.at[me.grid, lax.rem(z, 2), lax.rem(q, 2), pl.ds(4 * me.p + lax.div(z, 2), 1), :]

    def over_q(k, q_to, q_from):
        return send(
            picked.at[pl.ds(lax.rem(q_to, 2), 1), :], cell(q_from), send_sem.at[k], recv_sem.at[k],
            device(me.p, q_to, me.grid),
        )

    keep = pltpu.make_async_copy(picked.at[pl.ds(me.core, 1), :], cell(me.q), local)
    for k in range(1, 16):
        over_q(k, lax.rem(me.q + k, 16), me.q).start()
    keep.start()
    for k in range(1, 16):
        over_q(k, me.q, lax.rem(me.q + 16 - k, 16)).wait_recv()
    keep.wait()

    def piece(half, grid, xh, y):
        return lent.at[grid, :, half, pl.ds(16 * xh + 4 * y, 4), :]

    started = []

    def x_peer(n):
        return lax.rem(me.xh + n // 2, 2), lax.rem(me.grid + n, 2)

    def along_x(slot, half, y, n):
        xh, grid = x_peer(n)
        part = piece(half, me.grid, me.xh, y)
        return send(part, part, send_sem.at[slot + n], recv_sem.at[slot + n], device(4 * xh + me.y, me.q, grid))

    def from_x(slot, half, y, n):
        xh, grid = x_peer(n)
        part = piece(half, grid, xh, y)
        return send(part, part, send_sem.at[slot + n], recv_sem.at[slot + n], device(4 * xh + me.y, me.q, grid))

    def along_y(slot, half, xh, grid, n):
        part = piece(half, grid, xh, me.y)
        return send(part, part, send_sem.at[slot + n], recv_sem.at[slot + n], device(4 * me.xh + lax.rem(me.y + n, 4), me.q, me.grid))

    def from_y(slot, half, xh, grid, n):
        part = piece(half, grid, xh, lax.rem(me.y + 4 - n, 4))
        return send(part, part, send_sem.at[slot + n], recv_sem.at[slot + n], device(4 * me.xh + lax.rem(me.y + n, 4), me.q, me.grid))

    def go(copy):
        copy.start()
        started.append(copy)

    for n in range(1, 4):
        go(along_x(16, 0, me.y, n))
        go(along_y(20, 1, me.xh, me.grid, n))
    for n in range(1, 4):
        go(along_y(24, 0, me.xh, me.grid, n))
        go(along_x(40, 1, me.y, n))
    for m in range(1, 4):
        from_x(16, 0, me.y, m).wait_recv()
        xh, grid = x_peer(m)
        for n in range(1, 4):
            go(along_y(24 + 4 * m, 0, xh, grid, n))
        from_y(20, 1, me.xh, me.grid, m).wait_recv()
        for n in range(1, 4):
            go(along_x(40 + 4 * m, 1, lax.rem(me.y + 4 - m, 4), n))
    meanwhile()
    for m in range(4):
        xh, grid = x_peer(m)
        for n in range(1, 4):
            from_y(24 + 4 * m, 0, xh, grid, n).wait_recv()
            from_x(40 + 4 * m, 1, lax.rem(me.y + 4 - m, 4), n).wait_recv()

    def drain():
        for k in range(1, 16):
            over_q(k, lax.rem(me.q + k, 16), me.q).wait_send()
        for c in started:
            c.wait_send()

    return drain


def add_up(me, product, matrix, first, second, m_send, m_recv):
    p, q, grid = me.p, me.q, me.grid

    def block(c):
        return pl.ds(pl.multiple_of(8 * c, 8), 8)

    def scatter(k, to, slot):
        return send(product.at[block(to), :], first.at[slot], m_send.at[k], m_recv.at[k], device(p, to, grid))

    for k in range(1, 16):
        scatter(k, lax.rem(q + k, 16), q).start()
    first[q] = product[block(q), :]
    for k in range(1, 16):
        scatter(k, q, lax.rem(q + 16 - k, 16)).wait_recv()
    total = first[0]
    for k in range(1, 16):
        total = total + first[k]
    where = 2 * p + grid
    second[where] = total

    def share(k, slot, p_to, g_to):
        return send(second.at[slot], second.at[slot], m_send.at[15 + k], m_recv.at[15 + k], device(p_to, q, g_to))

    for k in range(1, 16):
        share(k, where, lax.rem(p + k // 2, 8), lax.rem(grid + k, 2)).start()
    for k in range(1, 16):
        p_, g_ = lax.rem(p + 8 - k // 2, 8), lax.rem(grid + k, 2)
        share(k, 2 * p_ + g_, p_, g_).wait_recv()
    total = second[0]
    for k in range(1, 16):
        total = total + second[k]
    matrix[block(q), :] = total

    def spread(k, to, slot):
        return send(
            matrix.at[block(slot), :], matrix.at[block(slot), :], m_send.at[30 + k], m_recv.at[30 + k],
            device(p, to, grid),
        )

    for k in range(1, 16):
        spread(k, lax.rem(q + k, 16), q).start()
    for k in range(1, 16):
        spread(k, q, lax.rem(q + 16 - k, 16)).wait_recv()

    for k in range(1, 16):
        scatter(k, lax.rem(q + k, 16), q).wait_send()
        share(k, where, lax.rem(p + k // 2, 8), lax.rem(grid + k, 2)).wait_send()
        spread(k, lax.rem(q + k, 16), q).wait_send()


def fock_kernel(
    owners, orb, tl, til, tr, tir, sq_rows, sq_pair, field, matrix,
    cols, whole, lent, blocks, picked, own_rows, lent_rows, work,
    given, kept, arrived, product, first, second,
    own_sem, w_send, w_recv, g_send, g_recv, t_send, t_recv, m_send, m_recv, *rest,
):
    near, far = rest[: len(rest) // 2], rest[len(rest) // 2 :]
    me = Place()
    partner = {"grid": 1 - me.grid}
    barrier = meet(me)
    from_plane(orb, work, 0)
    to_blocks(work, blocks, 0)
    pl.semaphore_wait(barrier, MET)

    same = me.core == me.grid
    differ = jnp.logical_not(same)
    middle_a, middle_b, finish, drain_near = exchange(me, blocks, near[0], near[1], cols, me.q, me.grid, near[2:])
    keep = pltpu.make_async_copy(orb, whole.at[me.grid], own_sem.at[0])
    to_twin = send(orb, whole.at[me.grid], w_send.at[0], w_recv.at[0], me.twin)
    to_partner = send(orb, whole.at[me.grid], w_send.at[0], w_recv.at[1], partner)
    from_partner = send(orb, whole.at[1 - me.grid], w_send.at[0], w_recv.at[1], partner)
    forward = send(whole.at[1 - me.grid], whole.at[1 - me.grid], w_send.at[1], w_recv.at[1], me.twin)

    @pl.when(same)
    def _():
        keep.start()
        to_twin.start()

    @pl.when(differ)
    def _():
        to_partner.start()

    middle_a()
    middle_b()
    finish()
    for r in range(2):
        owner = owners[r]
        picked[r : r + 1, :] = cols[pl.ds(lax.div(owner, 16), 1), pl.ds(lax.rem(owner, 16), 1), :].reshape(1, CELLS)

    @pl.when(same)
    def _():
        from_partner.wait_recv()
        forward.start()

    def meanwhile():
        @pl.when(same)
        def _():
            keep.wait()

        @pl.when(differ)
        def _():
            to_twin.wait_recv()
            forward.wait_recv()

        for s in range(2):
            from_plane(whole.at[s], own_rows, s)

    drain_gather = gather_lent(me, picked, lent, g_send, g_recv, own_sem.at[1], meanwhile)

    for s in range(2):
        from_blocks(lent.at[s], lent_rows, s)
    spectra(own_rows, lent_rows, work, tl, til, tr, sq_rows, sq_pair, 9, 9)
    potentials(own_rows, lent_rows, work, til, tir, 1 - me.core, 9)
    to_blocks(own_rows, given, 1 - me.core)
    give = send(given, arrived, t_send, t_recv, me.twin)
    give.start()
    potentials(own_rows, lent_rows, work, til, tir, me.core, 9)
    to_blocks(own_rows, kept, me.core)
    give.wait_recv()
    kept[...] = kept[...] + arrived[...]

    middle_a, middle_b, finish, drain_far = exchange(
        me, kept, far[0], far[1], field, 2 * me.z + me.grid, me.core, far[2:]
    )
    middle_a()
    middle_b()
    finish()
    oh, ol = halves(cols[...].reshape(BANDS, CELLS))
    fh, fl = halves(field[...].reshape(BANDS, CELLS))
    dot = lambda a, b: lax.dot_general(a, b, (((1,), (1,)), ((), ())), preferred_element_type=F32)
    product[...] = ((dot(oh, fl) + dot(ol, fh)) + dot(oh, fh)) * (1.0 / 373248.0)
    add_up(me, product, matrix, first, second, m_send, m_recv)

    @pl.when(same)
    def _():
        to_twin.wait_send()
        forward.wait_send()

    @pl.when(differ)
    def _():
        to_partner.wait_send()

    give.wait_send()
    drain_gather()
    drain_near()
    drain_far()


def fock_call(owners, orb):
    vm = pl.BlockSpec(memory_space=pltpu.VMEM)
    dma = pltpu.SemaphoreType.DMA
    v = lambda *shape: pltpu.VMEM(shape, F32)
    return pl.pallas_call(
        fock_kernel,
        out_shape=(
            jax.ShapeDtypeStruct((8, 16, CELLS), F32),
            jax.ShapeDtypeStruct((BANDS, BANDS), F32),
        ),
        in_specs=[pl.BlockSpec(memory_space=pltpu.SMEM)] + [vm] * 7,
        out_specs=(vm, vm),
        scratch_shapes=[
            v(8, 16, CELLS), v(2, 36, 5184), v(2, 2, 2, 32, CELLS), v(16, 8, CELLS), v(2, CELLS),
            v(5184, 128), v(5184, 128), v(5184, 128),
            v(16, 8, CELLS), v(16, 8, CELLS), v(16, 8, CELLS), v(BANDS, BANDS), v(16, 8, BANDS), v(16, 8, BANDS),
            dma((2,)), dma((2,)), dma((2,)), dma((56,)), dma((56,)), dma, dma, dma((46,)), dma((46,)),
        ] + exchange_scratch() + exchange_scratch(),
        compiler_params=pltpu.CompilerParams(collective_id=0, has_side_effects=True, vmem_limit_bytes=48 << 20),
    )(owners, orb, *tables())


def shards(orbitals, owners):
    field, matrix = fock_call(owners, orbitals[0])
    return (field.reshape(1, BANDS, CELLS), matrix)


def solution(mesh):
    in_specs = (P("band", "grid", None), P())
    out_specs = (P("grid", None, "band"), P())
    return jax.shard_map(shards, mesh=mesh, in_specs=in_specs, out_specs=out_specs, check_vma=False)
```

```python
import functools
import math

import jax
import jax.numpy as jnp
import numpy as np
from jax import lax
from jax.experimental import pallas as pl
from jax.experimental.pallas import tpu as pltpu
from jax.sharding import PartitionSpec as P

N = 72
PAD = 80
BF = jnp.bfloat16
F32 = jnp.float32

def tables():
    pos = np.arange(N)
    half = N // 2
    freq = np.where(pos <= half, pos, pos - half)
    ang = (freq[:, None] * pos[None, :] % N) * (2.0 * math.pi / N)
    w = np.where((pos == 0) | (pos == half), 1.0 / math.sqrt(N), math.sqrt(2.0 / N))
    basis = np.where((pos <= half)[:, None], np.cos(ang), np.sin(ang)) * w[:, None]
    sq = (freq * (2.0 * math.pi / N)) ** 2

    def split(t):
        hi = jnp.asarray(t, F32).astype(BF)
        lo = (jnp.asarray(t, F32) - hi.astype(F32)).astype(BF)
        return hi, lo

    def left(t):
        hi, lo = split(t)
        put = lambda a: jnp.pad(a, ((0, PAD - N), (0, PAD - N)))
        return jnp.concatenate([put(hi), put(hi), put(lo)], axis=1)

    def right(t):
        hi, lo = split(t)
        put = lambda a: jnp.pad(a, ((0, 128 - N), (0, 128 - N)))
        top = jnp.concatenate([put(hi), put(lo)], axis=1)
        low = jnp.concatenate([put(hi), jnp.zeros((128, 128), BF)], axis=1)
        return jnp.concatenate([top, low], axis=0)

    sq_rows = np.zeros((PAD, 128), np.float32); sq_rows[:N] = sq[:, None]
    sq_pair = np.zeros((N, 128), np.float32); sq_pair[:, :N] = sq[:, None] + sq[None, :]
    return (left(basis), left(basis.T), right(basis.T), right(basis), jnp.asarray(sq_rows), jnp.asarray(sq_pair))


def halves(v):
    hi = v.astype(BF)
    lo = (v - hi.astype(F32)).astype(BF)
    return hi, lo


def left_dot(table, planes):
    cols = []
    for v in planes:
        hi, lo = halves(v)
        cols.append(jnp.concatenate([hi, lo, hi], axis=0))
    out = jnp.dot(table, jnp.concatenate(cols, axis=1), preferred_element_type=F32)
    return [out[:, 128 * i : 128 * i + 128] for i in range(len(planes))]


def right_dot(v, table):
    hi, lo = halves(v)
    out = jnp.dot(jnp.concatenate([hi, lo], axis=1), table, preferred_element_type=F32)
    return out[:, :128] + out[:, 128:]


def pad_rows(v):
    return jnp.concatenate([v, jnp.zeros((PAD - N, 128), F32)], axis=0)


def fill_kernel(weight, sq_rows, sq_pair):
    def one(b, carry):
        total = sq_rows[...] + sq_pair[pl.ds(b, 1), :]
        positive = total > 0
        weight[b] = jnp.where(positive, (-0.25 * math.pi) / jnp.where(positive, total, 1.0), 0.0)
        return carry

    lax.fori_loop(0, N, one, 0)


def spectra(own, lent, work, tl, til, tr, weight, UA, UB):
    lane = lax.broadcasted_iota(jnp.int32, (1, 128), 1) < N

    def stage_a(step, carry):
        for u in range(UA):
            base = pl.multiple_of((step * UA + u) * 2 * N, 8)
            rows = pl.ds(base, 2 * N)
            d = jnp.where(lane, own[rows, :] * lent[rows, :], 0.0)
            z = right_dot(d, tr[...])
            a, b = left_dot(tl[...], [pad_rows(z[:N]), pad_rows(z[N:])])
            work[rows, :] = jnp.concatenate([a[:N], b[:N]], axis=0)
        return carry

    lax.fori_loop(0, 36 // UA, stage_a, 0)

    def stage_b(step, carry):
        for u in range(UB):
            b = (step * UB + u) * 2
            planes = [pad_rows(work[pl.ds(b + i, N, stride=N), :]) for i in range(2)]
            planes = left_dot(tl[...], planes)
            for i in range(2):
                planes[i] = planes[i] * weight[b + i]
            planes = left_dot(til[...], planes)
            for i in range(2):
                work[pl.ds(b + i, N, stride=N), :] = planes[i][:N]
        return carry

    lax.fori_loop(0, 36 // UB, stage_b, 0)


def potentials(own, lent, work, til, tir, slab, UC):
    def stage_c(step, carry):
        for u in range(UC):
            base = pl.multiple_of(slab * 2592 + (step * UC + u) * 2 * N, 8)
            rows = pl.ds(base, 2 * N)
            v = work[rows, :]
            a, b = left_dot(til[...], [pad_rows(v[:N]), pad_rows(v[N:])])
            z = right_dot(jnp.concatenate([a[:N], b[:N]], axis=0), tir[...])
            own[rows, :] = z * lent[rows, :]
        return carry

    lax.fori_loop(0, 18 // UC, stage_c, 0)


def from_plane(ref, dst, slab):
    for y in range(N):
        dst[pl.ds(slab * 2592 + y, 36, stride=N), :N] = ref[:, N * y : N * y + N]


def spans():
    for j in range(81):
        first, at = divmod(N * j, 1458)
        fit = min(N, 1458 - at)
        yield j, first, at, fit


def from_blocks(ref, dst, slab):
    for j, first, at, fit in spans():
        rows = pl.ds(slab * 2592 + j, 32, stride=81)
        v = ref[first // 2, first % 2, :, at : at + fit]
        if fit < N:
            v = jnp.concatenate([v, ref[(first + 1) // 2, (first + 1) % 2, :, : N - fit]], axis=1)
        dst[rows, :N] = v


def to_blocks(src, ref, slab):
    for h in range(4):
        for j, first, at, fit in spans():
            v = src[pl.ds(slab * 2592 + 81 * h + j, 8, stride=324), :]
            ref[4 * first + h, :, at : at + fit] = v[:, :fit]
            if fit < N:
                ref[4 * first + 4 + h, :, : N - fit] = v[:, fit:N]


MESH = pl.DeviceIdType.MESH
BANDS = 128
CELLS = 1458
CUT = 768


def send(src, dst, send_sem, recv_sem, device):
    return pltpu.make_async_remote_copy(
        src_ref=src, dst_ref=dst, send_sem=send_sem, recv_sem=recv_sem, device_id=device, device_id_type=MESH
    )


def greet(barrier, device):
    pl.semaphore_signal(barrier, inc=1, device_id=device, device_id_type=MESH)


class Place:
    def __init__(self):
        self.band, self.grid = lax.axis_index("band"), lax.axis_index("grid")
        self.p, self.q = lax.div(self.band, 16), lax.rem(self.band, 16)
        self.z, self.core = lax.div(self.q, 2), lax.rem(self.q, 2)
        self.xh, self.y = lax.div(self.p, 4), lax.rem(self.p, 4)
        self.twin = {"band": self.band + 1 - 2 * self.core}


def device(p, q, grid):
    return {"band": p * 16 + q, "grid": grid}


def meet(me):
    barrier = pltpu.get_barrier_semaphore()

    def near(k, carry):
        w = lax.rem(me.q * 2 + me.grid + k, 32)
        greet(barrier, device(me.p, lax.div(w, 2), lax.rem(w, 2)))
        return carry

    lax.fori_loop(1, 32, near, 0)

    def far(k, carry):
        p = lax.rem(me.p + k, 8)
        for n in range(4):
            greet(barrier, device(p, me.z * 2 + n // 2, n % 2))
        return carry

    lax.fori_loop(1, 8, far, 0)
    return barrier


MET = 31 + 28
FAR_Q = (8, 9, 7, 10, 6, 11, 5, 12, 4, 13, 3, 14, 2, 15, 1)
FAR_P = (6, 2, 4, 5, 3, 7, 1)


def lane_parts():
    return pl.ds(0, CUT), pl.ds(CUT, CELLS - CUT)


def exchange(me, blocks, via_a, via_b, cols, slot, grid_to, sems):
    s1, r1, s2, r2, s3, r3, s4, r4, local = sems
    low, high = lane_parts()
    stays = jnp.logical_and(slot == me.q, grid_to == me.grid)
    moves = jnp.logical_not(stays)

    def seat(q):
        return lax.rem(q, 4) * 4 + lax.div(q, 4)

    def a1(k, p_to, p_from):
        return send(blocks.at[:, p_to, low], via_a.at[p_from], s1.at[k], r1.at[k], device(p_to, slot, grid_to))

    def b1(k, q_to, q_from):
        return send(blocks.at[seat(q_to), :, high], via_b.at[q_from], s2.at[k], r2.at[q_from], device(me.p, q_to, grid_to))

    def a2(k, q_to, q_from):
        return send(via_a.at[:, seat(q_to), :], cols.at[:, q_from, low], s3.at[k], r3.at[k], device(me.p, q_to, me.grid))

    def b2(k, p_to, p_from):
        return send(via_b.at[:, p_to, :], cols.at[p_from, :, high], s4.at[k], r4.at[k], device(p_to, me.q, me.grid))

    keep_a1 = pltpu.make_async_copy(blocks.at[:, me.p, low], via_a.at[me.p], local.at[0])
    keep_b1 = pltpu.make_async_copy(blocks.at[seat(me.q), :, high], via_b.at[me.q], local.at[1])
    keep_a2 = pltpu.make_async_copy(via_a.at[:, seat(me.q), :], cols.at[:, me.q, low], local.at[2])
    keep_b2 = pltpu.make_async_copy(via_b.at[:, me.p, :], cols.at[me.p, :, high], local.at[3])

    for n in range(15):
        k = FAR_Q[n]
        b1(k, lax.rem(me.q + k, 16), slot).start()
        if n % 2 == 0 and n < 14:
            k = FAR_P[n // 2]
            a1(k, lax.rem(me.p + k, 8), me.p).start()

    @pl.when(stays)
    def _():
        keep_a1.start()
        keep_b1.start()

    @pl.when(moves)
    def _():
        a1(0, me.p, me.p).start()
        b1(0, me.q, slot).start()

    def middle_a():
        for k in range(1, 8):
            a1(k, me.p, lax.rem(me.p + 8 - k, 8)).wait_recv()

        @pl.when(stays)
        def _():
            keep_a1.wait()

        @pl.when(moves)
        def _():
            a1(0, me.p, me.p).wait_recv()

        for k in FAR_Q:
            a2(k, lax.rem(me.q + k, 16), me.q).start()
        keep_a2.start()

    def middle_b():
        for k in range(1, 16):
            b1(k, me.q, lax.rem(me.q + k, 16)).wait_recv()

        @pl.when(stays)
        def _():
            keep_b1.wait()

        @pl.when(moves)
        def _():
            b1(0, me.q, me.q).wait_recv()

        for k in FAR_P:
            b2(k, lax.rem(me.p + k, 8), me.p).start()
        keep_b2.start()

    def finish():
        for k in range(1, 16):
            a2(k, me.q, lax.rem(me.q + 16 - k, 16)).wait_recv()
        for k in range(1, 8):
            b2(k, me.p, lax.rem(me.p + 8 - k, 8)).wait_recv()
        keep_a2.wait()
        keep_b2.wait()

    def drain():
        for k in range(1, 8):
            a1(k, lax.rem(me.p + k, 8), me.p).wait_send()
            b2(k, lax.rem(me.p + k, 8), me.p).wait_send()
        for k in range(1, 16):
            b1(k, lax.rem(me.q + k, 16), slot).wait_send()
            a2(k, lax.rem(me.q + k, 16), me.q).wait_send()

        @pl.when(moves)
        def _():
            a1(0, me.p, me.p).wait_send()
            b1(0, me.q, slot).wait_send()

    return middle_a, middle_b, finish, drain


def exchange_scratch():
    dma = pltpu.SemaphoreType.DMA
    return [
        pltpu.VMEM((8, 16, CUT), F32), pltpu.VMEM((16, 8, CELLS - CUT), F32),
        dma((8,)), dma((8,)), dma((16,)), dma((16,)), dma((16,)), dma((16,)), dma((8,)), dma((8,)), dma((4,)),
    ]


def gather_lent(me, picked, lent, send_sem, recv_sem, local, meanwhile):
    zlo, zhi = lax.rem(me.z, 2), lax.div(me.z, 2)

    def cell(q):
        z = lax.div(q, 2)
        return lent.at[me.grid, lax.rem(z, 2), lax.rem(q, 2), pl.ds(4 * me.p + lax.div(z, 2), 1), :]

    def over_q(k, q_to, q_from):
        return send(
            picked.at[pl.ds(lax.rem(q_to, 2), 1), :], cell(q_from), send_sem.at[k], recv_sem.at[k],
            device(me.p, q_to, me.grid),
        )

    keep = pltpu.make_async_copy(picked.at[pl.ds(me.core, 1), :], cell(me.q), local)
    for k in FAR_Q:
        over_q(k, lax.rem(me.q + k, 16), me.q).start()
    keep.start()
    for k in range(1, 16):
        over_q(k, me.q, lax.rem(me.q + 16 - k, 16)).wait_recv()
    keep.wait()

    def piece(half, grid, xh, y):
        return lent.at[grid, :, half, pl.ds(16 * xh + 4 * y, 4), :]

    started = []

    def x_peer(n):
        return lax.rem(me.xh + n // 2, 2), lax.rem(me.grid + n, 2)

    def along_x(slot, half, y, n):
        xh, grid = x_peer(n)
        part = piece(half, me.grid, me.xh, y)
        return send(part, part, send_sem.at[slot + n], recv_sem.at[slot + n], device(4 * xh + me.y, me.q, grid))

    def from_x(slot, half, y, n):
        xh, grid = x_peer(n)
        part = piece(half, grid, xh, y)
        return send(part, part, send_sem.at[slot + n], recv_sem.at[slot + n], device(4 * xh + me.y, me.q, grid))

    def along_y(slot, half, xh, grid, n):
        part = piece(half, grid, xh, me.y)
        return send(part, part, send_sem.at[slot + n], recv_sem.at[slot + n], device(4 * me.xh + lax.rem(me.y + n, 4), me.q, me.grid))

    def from_y(slot, half, xh, grid, n):
        part = piece(half, grid, xh, lax.rem(me.y + 4 - n, 4))
        return send(part, part, send_sem.at[slot + n], recv_sem.at[slot + n], device(4 * me.xh + lax.rem(me.y + n, 4), me.q, me.grid))

    def go(copy):
        copy.start()
        started.append(copy)

    for n in range(1, 4):
        go(along_x(16, 0, me.y, n))
        go(along_y(20, 1, me.xh, me.grid, n))
    for n in range(1, 4):
        go(along_y(24, 0, me.xh, me.grid, n))
        go(along_x(40, 1, me.y, n))
    for m in range(1, 4):
        from_x(16, 0, me.y, m).wait_recv()
        xh, grid = x_peer(m)
        for n in range(1, 4):
            go(along_y(24 + 4 * m, 0, xh, grid, n))
        from_y(20, 1, me.xh, me.grid, m).wait_recv()
        for n in range(1, 4):
            go(along_x(40 + 4 * m, 1, lax.rem(me.y + 4 - m, 4), n))
    meanwhile()
    for m in range(4):
        xh, grid = x_peer(m)
        for n in range(1, 4):
            from_y(24 + 4 * m, 0, xh, grid, n).wait_recv()
            from_x(40 + 4 * m, 1, lax.rem(me.y + 4 - m, 4), n).wait_recv()

    def drain():
        for k in range(1, 16):
            over_q(k, lax.rem(me.q + k, 16), me.q).wait_send()
        for c in started:
            c.wait_send()

    return drain


def add_up(me, product, matrix, first, second, m_send, m_recv, meanwhile):
    p, q, grid = me.p, me.q, me.grid
    where = 2 * p + grid
    far = (12, 4, 13, 5, 8, 9, 10, 6, 11, 7, 14, 2, 15, 3, 1)

    def block(c):
        return pl.ds(pl.multiple_of(8 * c, 8), 8)

    def ahead(k):
        return lax.rem(p + k // 2, 8), lax.rem(grid + k, 2)

    def behind(k):
        return lax.rem(p + 8 - k // 2, 8), lax.rem(grid + k, 2)

    def scatter(k, to, slot):
        return send(
            product.at[block(2 * to[0] + to[1]), :], first.at[slot], m_send.at[k], m_recv.at[k], device(to[0], q, to[1])
        )

    for k in far:
        scatter(k, ahead(k), where).start()
    first[where] = product[block(where), :]
    meanwhile()
    for k in range(1, 16):
        b = behind(k)
        scatter(k, (p, grid), 2 * b[0] + b[1]).wait_recv()
    total = first[0]
    for k in range(1, 16):
        total = total + first[k]
    second[q] = total

    def share(k, slot, to):
        return send(second.at[slot], second.at[slot], m_send.at[15 + k], m_recv.at[15 + k], device(p, to, grid))

    for k in FAR_Q:
        share(k, q, lax.rem(q + k, 16)).start()
    for k in range(1, 16):
        scatter(k, ahead(k), where).wait_send()
    for k in range(1, 16):
        share(k, lax.rem(q + 16 - k, 16), q).wait_recv()
    total = second[0]
    for k in range(1, 16):
        total = total + second[k]
    matrix[block(where), :] = total

    def spread(k, slot, to):
        return send(
            matrix.at[block(slot), :], matrix.at[block(slot), :], m_send.at[30 + k], m_recv.at[30 + k],
            device(to[0], q, to[1]),
        )

    for k in far:
        spread(k, where, ahead(k)).start()
    for k in range(1, 16):
        share(k, q, lax.rem(q + k, 16)).wait_send()
    for k in range(1, 16):
        b = behind(k)
        spread(k, 2 * b[0] + b[1], (p, grid)).wait_recv()
    for k in range(1, 16):
        spread(k, where, ahead(k)).wait_send()


def fock_kernel(
    owners, orb_hbm, tl, til, tr, tir, sq_rows, sq_pair, field_out, matrix,
    orb, weight, cols, whole, lent, blocks, picked, own_rows, lent_rows, work,
    given, kept, arrived, field, turned, product, first, second,
    own_sem, w_send, w_recv, g_send, g_recv, t_send, t_recv, m_send, m_recv, *rest,
):
    near, far = rest[: len(rest) // 2], rest[len(rest) // 2 :]
    me = Place()
    partner = {"grid": 1 - me.grid}
    load = pltpu.make_async_copy(orb_hbm.at[:, 0, :], orb, own_sem.at[0])
    load.start()
    barrier = meet(me)
    load.wait()
    from_plane(orb, work, 0)
    to_blocks(work, blocks, 0)
    pl.semaphore_wait(barrier, MET)

    same = me.core == me.grid
    differ = jnp.logical_not(same)
    middle_a, middle_b, finish, drain_near = exchange(me, blocks, near[0], near[1], cols, me.q, me.grid, near[2:])
    keep = pltpu.make_async_copy(orb, whole.at[me.grid], own_sem.at[0])
    to_twin = send(orb, whole.at[me.grid], w_send.at[0], w_recv.at[0], me.twin)
    to_partner = send(orb, whole.at[me.grid], w_send.at[0], w_recv.at[1], partner)
    from_partner = send(orb, whole.at[1 - me.grid], w_send.at[0], w_recv.at[1], partner)
    forward = send(whole.at[1 - me.grid], whole.at[1 - me.grid], w_send.at[1], w_recv.at[1], me.twin)

    @pl.when(same)
    def _():
        keep.start()
        to_twin.start()

    @pl.when(differ)
    def _():
        to_partner.start()

    fill_kernel(weight, sq_rows, sq_pair)
    middle_a()
    middle_b()
    finish()
    for r in range(2):
        owner = owners[r]
        picked[r : r + 1, :] = cols[pl.ds(lax.div(owner, 16), 1), pl.ds(lax.rem(owner, 16), 1), :].reshape(1, CELLS)

    @pl.when(same)
    def _():
        from_partner.wait_recv()
        forward.start()

    def meanwhile():
        @pl.when(same)
        def _():
            keep.wait()

        @pl.when(differ)
        def _():
            to_twin.wait_recv()
            forward.wait_recv()

        for s in range(2):
            from_plane(whole.at[s], own_rows, s)

    drain_gather = gather_lent(me, picked, lent, g_send, g_recv, own_sem.at[1], meanwhile)

    for s in range(2):
        from_blocks(lent.at[s], lent_rows, s)
    spectra(own_rows, lent_rows, work, tl, til, tr, weight, 9, 9)
    potentials(own_rows, lent_rows, work, til, tir, 1 - me.core, 9)
    to_blocks(own_rows, given, 1 - me.core)
    give = send(given, arrived, t_send, t_recv, me.twin)
    give.start()
    potentials(own_rows, lent_rows, work, til, tir, me.core, 9)
    to_blocks(own_rows, kept, me.core)
    give.wait_recv()
    kept[...] = kept[...] + arrived[...]

    middle_a, middle_b, finish, drain_far = exchange(
        me, kept, far[0], far[1], field, 2 * me.z + me.grid, me.core, far[2:]
    )

    @pl.when(same)
    def _():
        to_twin.wait_send()
        forward.wait_send()

    @pl.when(differ)
    def _():
        to_partner.wait_send()

    give.wait_send()
    drain_gather()
    drain_near()
    middle_a()
    middle_b()
    finish()
    oh, ol = halves(cols[...].reshape(BANDS, CELLS))
    fh, fl = halves(field[...].reshape(BANDS, CELLS))
    dot = lambda a, b: lax.dot_general(a, b, (((1,), (1,)), ((), ())), preferred_element_type=F32)
    product[...] = ((dot(oh, fl) + dot(ol, fh)) + dot(oh, fh)) * (1.0 / 373248.0)

    store = pltpu.make_async_copy(turned, field_out.at[:, 0, :], own_sem.at[1])

    def turn():
        drain_far()
        for n in range(12):
            width = min(128, CELLS - 128 * n)
            tile = field[:, :, pl.ds(128 * n, width)].reshape(BANDS, width)
            turned[pl.ds(128 * n, width), :] = tile.T
        store.start()

    add_up(me, product, matrix, first, second, m_send, m_recv, turn)
    store.wait()


def fock_call(owners, orb):
    vm = pl.BlockSpec(memory_space=pltpu.VMEM)
    dma = pltpu.SemaphoreType.DMA
    v = lambda *shape: pltpu.VMEM(shape, F32)
    return pl.pallas_call(
        fock_kernel,
        out_shape=(
            jax.ShapeDtypeStruct((CELLS, 1, BANDS), F32),
            jax.ShapeDtypeStruct((BANDS, BANDS), F32),
        ),
        in_specs=[pl.BlockSpec(memory_space=pltpu.SMEM), pl.BlockSpec(memory_space=pl.ANY)] + [vm] * 6,
        out_specs=(pl.BlockSpec(memory_space=pl.ANY), vm),
        scratch_shapes=[
            v(36, 5184), v(N, PAD, 128), v(8, 16, CELLS), v(2, 36, 5184), v(2, 2, 2, 32, CELLS), v(16, 8, CELLS), v(2, CELLS),
            v(5184, 128), v(5184, 128), v(5184, 128),
            v(16, 8, CELLS), v(16, 8, CELLS), v(16, 8, CELLS), v(8, 16, CELLS), v(CELLS, BANDS), v(BANDS, BANDS), v(16, 8, BANDS), v(16, 8, BANDS),
            dma((2,)), dma((2,)), dma((2,)), dma((56,)), dma((56,)), dma, dma, dma((46,)), dma((46,)),
        ] + exchange_scratch() + exchange_scratch(),
        compiler_params=pltpu.CompilerParams(collective_id=0, has_side_effects=True, vmem_limit_bytes=60 << 20),
    )(owners, orb, *tables())


def shards(orbitals, owners):
    field, matrix = fock_call(owners, orbitals.transpose(1, 0, 2))
    return (field.transpose(1, 2, 0), matrix)


def solution(mesh):
    in_specs = (P("band", "grid", None), P())
    out_specs = (P("grid", None, "band"), P())
    return jax.shard_map(shards, mesh=mesh, in_specs=in_specs, out_specs=out_specs, check_vma=False)
```

```python
import functools
import math

import jax
import jax.numpy as jnp
import numpy as np
from jax import lax
from jax.experimental import pallas as pl
from jax.experimental.pallas import tpu as pltpu
from jax.sharding import PartitionSpec as P

N = 72
PAD = 80
GROUP = 9
BF = jnp.bfloat16
F32 = jnp.float32

def tables():
    pos = np.arange(N)
    half = N // 2
    freq = np.where(pos <= half, pos, pos - half)
    ang = (freq[:, None] * pos[None, :] % N) * (2.0 * math.pi / N)
    w = np.where((pos == 0) | (pos == half), 1.0 / math.sqrt(N), math.sqrt(2.0 / N))
    basis = np.where((pos <= half)[:, None], np.cos(ang), np.sin(ang)) * w[:, None]
    sq = (freq * (2.0 * math.pi / N)) ** 2

    def split(t):
        hi = jnp.asarray(t, F32).astype(BF)
        lo = (jnp.asarray(t, F32) - hi.astype(F32)).astype(BF)
        return hi, lo

    def left(t):
        hi, lo = split(t)
        put = lambda a: jnp.pad(a, ((0, PAD - N), (0, PAD - N)))
        return jnp.concatenate([put(hi), put(hi), put(lo)], axis=1)

    def right(t):
        hi, lo = split(t)
        put = lambda a: jnp.pad(a, ((0, 128 - N), (0, 128 - N)))
        top = jnp.concatenate([put(hi), put(lo)], axis=1)
        low = jnp.concatenate([put(hi), jnp.zeros((128, 128), BF)], axis=1)
        return jnp.concatenate([top, low], axis=0)

    sq_rows = np.zeros((PAD, 128), np.float32); sq_rows[:N] = sq[:, None]
    sq_pair = np.zeros((N, 128), np.float32); sq_pair[:, :N] = sq[:, None] + sq[None, :]
    return (left(basis), left(basis.T), right(basis.T), right(basis), jnp.asarray(sq_rows), jnp.asarray(sq_pair))


def halves(v):
    hi = v.astype(BF)
    lo = (v - hi.astype(F32)).astype(BF)
    return hi, lo


def left_dot(table, planes):
    cols = []
    for v in planes:
        hi, lo = halves(v)
        cols.append(jnp.concatenate([hi, lo, hi], axis=0))
    out = jnp.dot(table, jnp.concatenate(cols, axis=1), preferred_element_type=F32)
    return [out[:, 128 * i : 128 * i + 128] for i in range(len(planes))]


def right_dot(v, table):
    hi, lo = halves(v)
    out = jnp.dot(jnp.concatenate([hi, lo], axis=1), table, preferred_element_type=F32)
    return out[:, :128] + out[:, 128:]


def pad_rows(v):
    return jnp.concatenate([v, jnp.zeros((PAD - N, 128), F32)], axis=0)


def fill_kernel(weight, sq_rows, sq_pair):
    def one(b, carry):
        total = sq_rows[...] + sq_pair[pl.ds(b, 1), :]
        positive = total > 0
        weight[b] = jnp.where(positive, (-0.25 * math.pi) / jnp.where(positive, total, 1.0), 0.0)
        return carry

    lax.fori_loop(0, N, one, 0)


def spectra(own, lent, work, tl, til, tr, weight, UA, UB):
    lane = lax.broadcasted_iota(jnp.int32, (1, 128), 1) < N

    def stage_a(step, carry):
        span = 2 * N * GROUP
        for u in range(UA // GROUP):
            base = pl.multiple_of((step * (UA // GROUP) + u) * span, 8)
            rows = pl.ds(base, span)
            d = jnp.where(lane, own[rows, :] * lent[rows, :], 0.0)
            z = right_dot(d, tr[...])
            for n in range(GROUP):
                at = 2 * N * n
                planes = left_dot(tl[...], [pad_rows(z[at : at + N]), pad_rows(z[at + N : at + 2 * N])])
                work[pl.ds(base + at, 2 * N), :] = jnp.concatenate([v[:N] for v in planes], axis=0)
        return carry

    lax.fori_loop(0, 36 // UA, stage_a, 0)

    def stage_b(step, carry):
        for u in range(UB):
            b = (step * UB + u) * 2
            planes = [pad_rows(work[pl.ds(b + i, N, stride=N), :]) for i in range(2)]
            planes = left_dot(tl[...], planes)
            for i in range(2):
                planes[i] = planes[i] * weight[b + i]
            planes = left_dot(til[...], planes)
            for i in range(2):
                work[pl.ds(b + i, N, stride=N), :] = planes[i][:N]
        return carry

    lax.fori_loop(0, 36 // UB, stage_b, 0)


def potentials(own, lent, work, til, tir, slab, UC):
    def stage_c(step, carry):
        span = 2 * N * GROUP
        for u in range(UC // GROUP):
            base = pl.multiple_of(slab * 2592 + (step * (UC // GROUP) + u) * span, 8)
            planes = []
            for n in range(GROUP):
                v = work[pl.ds(base + 2 * N * n, 2 * N), :]
                planes += left_dot(til[...], [pad_rows(v[:N]), pad_rows(v[N:])])
            rows = pl.ds(base, span)
            own[rows, :] = right_dot(jnp.concatenate([v[:N] for v in planes], axis=0), tir[...]) * lent[rows, :]
        return carry

    lax.fori_loop(0, 18 // UC, stage_c, 0)


def from_plane(ref, dst, slab):
    for y in range(N):
        dst[pl.ds(slab * 2592 + y, 36, stride=N), :N] = ref[:, N * y : N * y + N]


def spans():
    for j in range(81):
        first, at = divmod(N * j, 1458)
        fit = min(N, 1458 - at)
        yield j, first, at, fit


def from_blocks(ref, dst, slab):
    for j, first, at, fit in spans():
        rows = pl.ds(slab * 2592 + j, 32, stride=81)
        v = ref[first // 2, first % 2, :, at : at + fit]
        if fit < N:
            v = jnp.concatenate([v, ref[(first + 1) // 2, (first + 1) % 2, :, : N - fit]], axis=1)
        dst[rows, :N] = v


def to_blocks(src, ref, slab):
    for h in range(4):
        for j, first, at, fit in spans():
            v = src[pl.ds(slab * 2592 + 81 * h + j, 8, stride=324), :]
            ref[4 * first + h, :, at : at + fit] = v[:, :fit]
            if fit < N:
                ref[4 * first + 4 + h, :, : N - fit] = v[:, fit:N]


MESH = pl.DeviceIdType.MESH
BANDS = 128
CELLS = 1458
CUT = 768


def send(src, dst, send_sem, recv_sem, device):
    return pltpu.make_async_remote_copy(
        src_ref=src, dst_ref=dst, send_sem=send_sem, recv_sem=recv_sem, device_id=device, device_id_type=MESH
    )


def greet(barrier, device):
    pl.semaphore_signal(barrier, inc=1, device_id=device, device_id_type=MESH)


class Place:
    def __init__(self):
        self.band, self.grid = lax.axis_index("band"), lax.axis_index("grid")
        self.p, self.q = lax.div(self.band, 16), lax.rem(self.band, 16)
        self.z, self.core = lax.div(self.q, 2), lax.rem(self.q, 2)
        self.xh, self.y = lax.div(self.p, 4), lax.rem(self.p, 4)
        self.twin = {"band": self.band + 1 - 2 * self.core}


def device(p, q, grid):
    return {"band": p * 16 + q, "grid": grid}


def meet(me):
    barrier = pltpu.get_barrier_semaphore()

    def near(k, carry):
        w = lax.rem(me.q * 2 + me.grid + k, 32)
        greet(barrier, device(me.p, lax.div(w, 2), lax.rem(w, 2)))
        return carry

    lax.fori_loop(1, 32, near, 0)

    def far(k, carry):
        p = lax.rem(me.p + k, 8)
        for n in range(4):
            greet(barrier, device(p, me.z * 2 + n // 2, n % 2))
        return carry

    lax.fori_loop(1, 8, far, 0)
    return barrier


MET = 31 + 28
FAR_Q = (8, 9, 7, 10, 6, 11, 5, 12, 4, 13, 3, 14, 2, 15, 1)
FAR_P = (6, 2, 4, 5, 3, 7, 1)


def lane_parts():
    return pl.ds(0, CUT), pl.ds(CUT, CELLS - CUT)


def exchange(me, blocks, via_a, via_b, cols, slot, grid_to, sems):
    s1, r1, s2, r2, s3, r3, s4, r4, local = sems
    low, high = lane_parts()
    stays = jnp.logical_and(slot == me.q, grid_to == me.grid)
    moves = jnp.logical_not(stays)

    def seat(q):
        return lax.rem(q, 4) * 4 + lax.div(q, 4)

    def a1(k, p_to, p_from):
        return send(blocks.at[:, p_to, low], via_a.at[p_from], s1.at[k], r1.at[k], device(p_to, slot, grid_to))

    def b1(k, q_to, q_from):
        return send(blocks.at[seat(q_to), :, high], via_b.at[q_from], s2.at[k], r2.at[q_from], device(me.p, q_to, grid_to))

    def a2(k, q_to, q_from):
        return send(via_a.at[:, seat(q_to), :], cols.at[:, q_from, low], s3.at[k], r3.at[k], device(me.p, q_to, me.grid))

    def b2(k, p_to, p_from):
        return send(via_b.at[:, p_to, :], cols.at[p_from, :, high], s4.at[k], r4.at[k], device(p_to, me.q, me.grid))

    keep_a1 = pltpu.make_async_copy(blocks.at[:, me.p, low], via_a.at[me.p], local.at[0])
    keep_b1 = pltpu.make_async_copy(blocks.at[seat(me.q), :, high], via_b.at[me.q], local.at[1])
    keep_a2 = pltpu.make_async_copy(via_a.at[:, seat(me.q), :], cols.at[:, me.q, low], local.at[2])
    keep_b2 = pltpu.make_async_copy(via_b.at[:, me.p, :], cols.at[me.p, :, high], local.at[3])

    for n in range(15):
        k = FAR_Q[n]
        b1(k, lax.rem(me.q + k, 16), slot).start()
        if n % 2 == 0 and n < 14:
            k = FAR_P[n // 2]
            a1(k, lax.rem(me.p + k, 8), me.p).start()

    @pl.when(stays)
    def _():
        keep_a1.start()
        keep_b1.start()

    @pl.when(moves)
    def _():
        a1(0, me.p, me.p).start()
        b1(0, me.q, slot).start()

    def middle_a():
        for k in range(1, 8):
            a1(k, me.p, lax.rem(me.p + 8 - k, 8)).wait_recv()

        @pl.when(stays)
        def _():
            keep_a1.wait()

        @pl.when(moves)
        def _():
            a1(0, me.p, me.p).wait_recv()

        for k in FAR_Q:
            a2(k, lax.rem(me.q + k, 16), me.q).start()
        keep_a2.start()

    def middle_b():
        for k in range(1, 16):
            b1(k, me.q, lax.rem(me.q + k, 16)).wait_recv()

        @pl.when(stays)
        def _():
            keep_b1.wait()

        @pl.when(moves)
        def _():
            b1(0, me.q, me.q).wait_recv()

        for k in FAR_P:
            b2(k, lax.rem(me.p + k, 8), me.p).start()
        keep_b2.start()

    def finish_a():
        for k in range(1, 16):
            a2(k, me.q, lax.rem(me.q + 16 - k, 16)).wait_recv()
        keep_a2.wait()

    def finish_b():
        for k in range(1, 8):
            b2(k, me.p, lax.rem(me.p + 8 - k, 8)).wait_recv()
        keep_b2.wait()

    def drain():
        for k in range(1, 8):
            a1(k, lax.rem(me.p + k, 8), me.p).wait_send()
            b2(k, lax.rem(me.p + k, 8), me.p).wait_send()
        for k in range(1, 16):
            b1(k, lax.rem(me.q + k, 16), slot).wait_send()
            a2(k, lax.rem(me.q + k, 16), me.q).wait_send()

        @pl.when(moves)
        def _():
            a1(0, me.p, me.p).wait_send()
            b1(0, me.q, slot).wait_send()

    return middle_a, middle_b, finish_a, finish_b, drain


def exchange_scratch():
    dma = pltpu.SemaphoreType.DMA
    return [
        pltpu.VMEM((8, 16, CUT), F32), pltpu.VMEM((16, 8, CELLS - CUT), F32),
        dma((8,)), dma((8,)), dma((16,)), dma((16,)), dma((16,)), dma((16,)), dma((8,)), dma((8,)), dma((4,)),
    ]


def gather_lent(me, picked, lent, send_sem, recv_sem, local, meanwhile):
    zlo, zhi = lax.rem(me.z, 2), lax.div(me.z, 2)

    def cell(q):
        z = lax.div(q, 2)
        return lent.at[me.grid, lax.rem(z, 2), lax.rem(q, 2), pl.ds(4 * me.p + lax.div(z, 2), 1), :]

    def over_q(k, q_to, q_from):
        return send(
            picked.at[pl.ds(lax.rem(q_to, 2), 1), :], cell(q_from), send_sem.at[k], recv_sem.at[k],
            device(me.p, q_to, me.grid),
        )

    keep = pltpu.make_async_copy(picked.at[pl.ds(me.core, 1), :], cell(me.q), local)
    for k in FAR_Q:
        over_q(k, lax.rem(me.q + k, 16), me.q).start()
    keep.start()
    for k in range(1, 16):
        over_q(k, me.q, lax.rem(me.q + 16 - k, 16)).wait_recv()
    keep.wait()

    def piece(half, grid, xh, y):
        return lent.at[grid, :, half, pl.ds(16 * xh + 4 * y, 4), :]

    started = []

    def x_peer(n):
        return lax.rem(me.xh + n // 2, 2), lax.rem(me.grid + n, 2)

    def along_x(slot, half, y, n):
        xh, grid = x_peer(n)
        part = piece(half, me.grid, me.xh, y)
        return send(part, part, send_sem.at[slot + n], recv_sem.at[slot + n], device(4 * xh + me.y, me.q, grid))

    def from_x(slot, half, y, n):
        xh, grid = x_peer(n)
        part = piece(half, grid, xh, y)
        return send(part, part, send_sem.at[slot + n], recv_sem.at[slot + n], device(4 * xh + me.y, me.q, grid))

    def along_y(slot, half, xh, grid, n):
        part = piece(half, grid, xh, me.y)
        return send(part, part, send_sem.at[slot + n], recv_sem.at[slot + n], device(4 * me.xh + lax.rem(me.y + n, 4), me.q, me.grid))

    def from_y(slot, half, xh, grid, n):
        part = piece(half, grid, xh, lax.rem(me.y + 4 - n, 4))
        return send(part, part, send_sem.at[slot + n], recv_sem.at[slot + n], device(4 * me.xh + lax.rem(me.y + n, 4), me.q, me.grid))

    def go(copy):
        copy.start()
        started.append(copy)

    for n in range(1, 4):
        go(along_x(16, 0, me.y, n))
        go(along_y(20, 1, me.xh, me.grid, n))
    for n in range(1, 4):
        go(along_y(24, 0, me.xh, me.grid, n))
        go(along_x(40, 1, me.y, n))
    for m in range(1, 4):
        from_x(16, 0, me.y, m).wait_recv()
        xh, grid = x_peer(m)
        for n in range(1, 4):
            go(along_y(24 + 4 * m, 0, xh, grid, n))
        from_y(20, 1, me.xh, me.grid, m).wait_recv()
        for n in range(1, 4):
            go(along_x(40 + 4 * m, 1, lax.rem(me.y + 4 - m, 4), n))
    meanwhile()
    for m in range(4):
        xh, grid = x_peer(m)
        for n in range(1, 4):
            from_y(24 + 4 * m, 0, xh, grid, n).wait_recv()
            from_x(40 + 4 * m, 1, lax.rem(me.y + 4 - m, 4), n).wait_recv()

    def drain():
        for k in range(1, 16):
            over_q(k, lax.rem(me.q + k, 16), me.q).wait_send()
        for c in started:
            c.wait_send()

    return drain


def add_up(me, product, matrix, first, second, m_send, m_recv, meanwhile):
    p, q, grid = me.p, me.q, me.grid
    where = 2 * p + grid
    far = (12, 4, 13, 5, 8, 9, 10, 6, 11, 7, 14, 2, 15, 3, 1)

    def block(c):
        return pl.ds(pl.multiple_of(8 * c, 8), 8)

    def ahead(k):
        return lax.rem(p + k // 2, 8), lax.rem(grid + k, 2)

    def behind(k):
        return lax.rem(p + 8 - k // 2, 8), lax.rem(grid + k, 2)

    def scatter(k, to, slot):
        return send(
            product.at[block(2 * to[0] + to[1]), :], first.at[slot], m_send.at[k], m_recv.at[k], device(to[0], q, to[1])
        )

    for k in far:
        scatter(k, ahead(k), where).start()
    first[where] = product[block(where), :]
    meanwhile()
    for k in range(1, 16):
        b = behind(k)
        scatter(k, (p, grid), 2 * b[0] + b[1]).wait_recv()
    total = first[0]
    for k in range(1, 16):
        total = total + first[k]
    second[q] = total

    def share(k, slot, to):
        return send(second.at[slot], second.at[slot], m_send.at[15 + k], m_recv.at[15 + k], device(p, to, grid))

    for k in FAR_Q:
        share(k, q, lax.rem(q + k, 16)).start()
    for k in range(1, 16):
        scatter(k, ahead(k), where).wait_send()
    for k in range(1, 16):
        share(k, lax.rem(q + 16 - k, 16), q).wait_recv()
    total = second[0]
    for k in range(1, 16):
        total = total + second[k]
    matrix[block(where), :] = total

    def spread(k, slot, to):
        return send(
            matrix.at[block(slot), :], matrix.at[block(slot), :], m_send.at[30 + k], m_recv.at[30 + k],
            device(to[0], q, to[1]),
        )

    for k in far:
        spread(k, where, ahead(k)).start()
    for k in range(1, 16):
        share(k, q, lax.rem(q + k, 16)).wait_send()
    for k in range(1, 16):
        b = behind(k)
        spread(k, 2 * b[0] + b[1], (p, grid)).wait_recv()
    for k in range(1, 16):
        spread(k, where, ahead(k)).wait_send()


def fock_kernel(
    owners, orb_hbm, tl, til, tr, tir, sq_rows, sq_pair, field_out, matrix,
    orb, weight, cols, whole, lent, blocks, picked, own_rows, lent_rows, work,
    given, kept, arrived, field, turned, product, first, second,
    own_sem, w_send, w_recv, g_send, g_recv, t_send, t_recv, m_send, m_recv, *rest,
):
    near, far = rest[: len(rest) // 2], rest[len(rest) // 2 :]
    me = Place()
    partner = {"grid": 1 - me.grid}
    load = pltpu.make_async_copy(orb_hbm.at[:, 0, :], orb, own_sem.at[0])
    load.start()
    barrier = meet(me)
    load.wait()
    from_plane(orb, work, 0)
    to_blocks(work, blocks, 0)
    pl.semaphore_wait(barrier, MET)

    same = me.core == me.grid
    differ = jnp.logical_not(same)
    middle_a, middle_b, finish_a, finish_b, drain_near = exchange(me, blocks, near[0], near[1], cols, me.q, me.grid, near[2:])
    keep = pltpu.make_async_copy(orb, whole.at[me.grid], own_sem.at[0])
    to_twin = send(orb, whole.at[me.grid], w_send.at[0], w_recv.at[0], me.twin)
    to_partner = send(orb, whole.at[me.grid], w_send.at[0], w_recv.at[1], partner)
    from_partner = send(orb, whole.at[1 - me.grid], w_send.at[0], w_recv.at[1], partner)
    forward = send(whole.at[1 - me.grid], whole.at[1 - me.grid], w_send.at[1], w_recv.at[1], me.twin)

    @pl.when(same)
    def _():
        keep.start()
        to_twin.start()

    @pl.when(differ)
    def _():
        to_partner.start()

    fill_kernel(weight, sq_rows, sq_pair)
    middle_a()
    middle_b()
    finish_a()
    finish_b()
    for r in range(2):
        owner = owners[r]
        picked[r : r + 1, :] = cols[pl.ds(lax.div(owner, 16), 1), pl.ds(lax.rem(owner, 16), 1), :].reshape(1, CELLS)

    @pl.when(same)
    def _():
        from_partner.wait_recv()
        forward.start()

    def meanwhile():
        @pl.when(same)
        def _():
            keep.wait()

        @pl.when(differ)
        def _():
            to_twin.wait_recv()
            forward.wait_recv()

        for s in range(2):
            from_plane(whole.at[s], own_rows, s)

    drain_gather = gather_lent(me, picked, lent, g_send, g_recv, own_sem.at[1], meanwhile)

    for s in range(2):
        from_blocks(lent.at[s], lent_rows, s)
    spectra(own_rows, lent_rows, work, tl, til, tr, weight, 36, 36)
    potentials(own_rows, lent_rows, work, til, tir, 1 - me.core, 18)
    to_blocks(own_rows, given, 1 - me.core)
    give = send(given, arrived, t_send, t_recv, me.twin)
    give.start()
    potentials(own_rows, lent_rows, work, til, tir, me.core, 18)
    to_blocks(own_rows, kept, me.core)
    give.wait_recv()
    kept[...] = kept[...] + arrived[...]

    middle_a, middle_b, finish_a, finish_b, drain_far = exchange(
        me, kept, far[0], far[1], field, 2 * me.z + me.grid, me.core, far[2:]
    )

    @pl.when(same)
    def _():
        to_twin.wait_send()
        forward.wait_send()

    @pl.when(differ)
    def _():
        to_partner.wait_send()

    give.wait_send()
    drain_gather()
    drain_near()
    middle_a()
    middle_b()
    dot = lambda a, b: lax.dot_general(a, b, (((1,), (1,)), ((), ())), preferred_element_type=F32)

    def overlap(lanes, width):
        oh, ol = halves(cols[:, :, lanes].reshape(BANDS, width))
        fh, fl = halves(field[:, :, lanes].reshape(BANDS, width))
        return (dot(oh, fl) + dot(ol, fh)) + dot(oh, fh)

    low, high = lane_parts()
    finish_b()
    product[...] = overlap(high, CELLS - CUT)
    finish_a()
    product[...] = (product[...] + overlap(low, CUT)) * (1.0 / 373248.0)
    store = pltpu.make_async_copy(turned, field_out.at[:, 0, :], own_sem.at[1])

    def turn():
        drain_far()
        for n in range(12):
            width = min(128, CELLS - 128 * n)
            tile = field[:, :, pl.ds(128 * n, width)].reshape(BANDS, width)
            turned[pl.ds(128 * n, width), :] = tile.T
        store.start()

    add_up(me, product, matrix, first, second, m_send, m_recv, turn)
    store.wait()


def fock_call(owners, orb):
    vm = pl.BlockSpec(memory_space=pltpu.VMEM)
    dma = pltpu.SemaphoreType.DMA
    v = lambda *shape: pltpu.VMEM(shape, F32)
    return pl.pallas_call(
        fock_kernel,
        out_shape=(
            jax.ShapeDtypeStruct((CELLS, 1, BANDS), F32),
            jax.ShapeDtypeStruct((BANDS, BANDS), F32),
        ),
        in_specs=[pl.BlockSpec(memory_space=pltpu.SMEM), pl.BlockSpec(memory_space=pl.ANY)] + [vm] * 6,
        out_specs=(pl.BlockSpec(memory_space=pl.ANY), vm),
        scratch_shapes=[
            v(36, 5184), v(N, PAD, 128), v(8, 16, CELLS), v(2, 36, 5184), v(2, 2, 2, 32, CELLS), v(16, 8, CELLS), v(2, CELLS),
            v(5184, 128), v(5184, 128), v(5184, 128),
            v(16, 8, CELLS), v(16, 8, CELLS), v(16, 8, CELLS), v(8, 16, CELLS), v(CELLS, BANDS), v(BANDS, BANDS), v(16, 8, BANDS), v(16, 8, BANDS),
            dma((2,)), dma((2,)), dma((2,)), dma((56,)), dma((56,)), dma, dma, dma((46,)), dma((46,)),
        ] + exchange_scratch() + exchange_scratch(),
        compiler_params=pltpu.CompilerParams(collective_id=0, has_side_effects=True, vmem_limit_bytes=60 << 20),
    )(owners, orb, *tables())


def shards(orbitals, owners):
    field, matrix = fock_call(owners, orbitals.transpose(1, 0, 2))
    return (field.transpose(1, 2, 0), matrix)


def solution(mesh):
    in_specs = (P("band", "grid", None), P())
    out_specs = (P("grid", None, "band"), P())
    return jax.shard_map(shards, mesh=mesh, in_specs=in_specs, out_specs=out_specs, check_vma=False)
```

```python
import functools
import math

import jax
import jax.numpy as jnp
import numpy as np
from jax import lax
from jax.experimental import pallas as pl
from jax.experimental.pallas import tpu as pltpu
from jax.sharding import PartitionSpec as P

N = 72
PAD = 80
GROUP = 9
BF = jnp.bfloat16
F32 = jnp.float32

def tables():
    pos = np.arange(N)
    half = N // 2
    freq = np.where(pos <= half, pos, pos - half)
    ang = (freq[:, None] * pos[None, :] % N) * (2.0 * math.pi / N)
    w = np.where((pos == 0) | (pos == half), 1.0 / math.sqrt(N), math.sqrt(2.0 / N))
    basis = np.where((pos <= half)[:, None], np.cos(ang), np.sin(ang)) * w[:, None]
    sq = (freq * (2.0 * math.pi / N)) ** 2

    def split(t):
        hi = jnp.asarray(t, F32).astype(BF)
        lo = (jnp.asarray(t, F32) - hi.astype(F32)).astype(BF)
        return hi, lo

    def left(t):
        hi, lo = split(t)
        put = lambda a: jnp.pad(a, ((0, PAD - N), (0, PAD - N)))
        return jnp.concatenate([put(hi), put(hi), put(lo)], axis=1)

    def right(t):
        hi, lo = split(t)
        put = lambda a: jnp.pad(a, ((0, 128 - N), (0, 128 - N)))
        top = jnp.concatenate([put(hi), put(lo)], axis=1)
        low = jnp.concatenate([put(hi), jnp.zeros((128, 128), BF)], axis=1)
        return jnp.concatenate([top, low], axis=0)

    sq_rows = np.zeros((PAD, 128), np.float32); sq_rows[:N] = sq[:, None]
    sq_pair = np.zeros((N, 128), np.float32); sq_pair[:, :N] = sq[:, None] + sq[None, :]
    return (left(basis), left(basis.T), right(basis.T), right(basis), jnp.asarray(sq_rows), jnp.asarray(sq_pair))


def halves(v):
    hi = v.astype(BF)
    lo = (v - hi.astype(F32)).astype(BF)
    return hi, lo


def left_dot(table, planes):
    cols = []
    for v in planes:
        hi, lo = halves(v)
        cols.append(jnp.concatenate([hi, lo, hi], axis=0))
    out = jnp.dot(table, jnp.concatenate(cols, axis=1), preferred_element_type=F32)
    return [out[:, 128 * i : 128 * i + 128] for i in range(len(planes))]


def right_dot(v, table):
    hi, lo = halves(v)
    out = jnp.dot(jnp.concatenate([hi, lo], axis=1), table, preferred_element_type=F32)
    return out[:, :128] + out[:, 128:]


def pad_rows(v):
    return jnp.concatenate([v, jnp.zeros((PAD - N, 128), F32)], axis=0)


def fill_kernel(weight, sq_rows, sq_pair):
    def one(b, carry):
        total = sq_rows[...] + sq_pair[pl.ds(b, 1), :]
        positive = total > 0
        weight[b] = jnp.where(positive, (-0.25 * math.pi) / jnp.where(positive, total, 1.0), 0.0)
        return carry

    lax.fori_loop(0, N, one, 0)


def spectra(own, lent, work, tl, til, tr, weight, UA, UB):
    lane = lax.broadcasted_iota(jnp.int32, (1, 128), 1) < N

    def stage_a(step, carry):
        span = 2 * N * GROUP
        for u in range(UA // GROUP):
            base = pl.multiple_of((step * (UA // GROUP) + u) * span, 8)
            rows = pl.ds(base, span)
            d = jnp.where(lane, own[rows, :] * lent[rows, :], 0.0)
            z = right_dot(d, tr[...])
            for n in range(GROUP):
                at = 2 * N * n
                planes = left_dot(tl[...], [pad_rows(z[at : at + N]), pad_rows(z[at + N : at + 2 * N])])
                work[pl.ds(base + at, 2 * N), :] = jnp.concatenate([v[:N] for v in planes], axis=0)
        return carry

    lax.fori_loop(0, 36 // UA, stage_a, 0)

    def stage_b(step, carry):
        for u in range(UB):
            b = (step * UB + u) * 2
            planes = [pad_rows(work[pl.ds(b + i, N, stride=N), :]) for i in range(2)]
            planes = left_dot(tl[...], planes)
            for i in range(2):
                planes[i] = planes[i] * weight[b + i]
            planes = left_dot(til[...], planes)
            for i in range(2):
                work[pl.ds(b + i, N, stride=N), :] = planes[i][:N]
        return carry

    lax.fori_loop(0, 36 // UB, stage_b, 0)


def potentials(own, lent, work, til, tir, slab, UC):
    def stage_c(step, carry):
        span = 2 * N * GROUP
        for u in range(UC // GROUP):
            base = pl.multiple_of(slab * 2592 + (step * (UC // GROUP) + u) * span, 8)
            planes = []
            for n in range(GROUP):
                v = work[pl.ds(base + 2 * N * n, 2 * N), :]
                planes += left_dot(til[...], [pad_rows(v[:N]), pad_rows(v[N:])])
            rows = pl.ds(base, span)
            own[rows, :] = right_dot(jnp.concatenate([v[:N] for v in planes], axis=0), tir[...]) * lent[rows, :]
        return carry

    lax.fori_loop(0, 18 // UC, stage_c, 0)


def from_plane(ref, dst, slab):
    for y in range(N):
        dst[pl.ds(slab * 2592 + y, 36, stride=N), :N] = ref[:, N * y : N * y + N]


def spans():
    for j in range(81):
        first, at = divmod(N * j, 1458)
        fit = min(N, 1458 - at)
        yield j, first, at, fit


def from_blocks(ref, dst, slab):
    for j, first, at, fit in spans():
        rows = pl.ds(slab * 2592 + j, 32, stride=81)
        v = ref[first // 2, first % 2, :, at : at + fit]
        if fit < N:
            v = jnp.concatenate([v, ref[(first + 1) // 2, (first + 1) % 2, :, : N - fit]], axis=1)
        dst[rows, :N] = v


def to_blocks(src, ref, slab):
    for h in range(4):
        for j, first, at, fit in spans():
            v = src[pl.ds(slab * 2592 + 81 * h + j, 8, stride=324), :]
            ref[4 * first + h, :, at : at + fit] = v[:, :fit]
            if fit < N:
                ref[4 * first + 4 + h, :, : N - fit] = v[:, fit:N]


MESH = pl.DeviceIdType.MESH
BANDS = 128
CELLS = 1458
CUT = 768


def send(src, dst, send_sem, recv_sem, device):
    return pltpu.make_async_remote_copy(
        src_ref=src, dst_ref=dst, send_sem=send_sem, recv_sem=recv_sem, device_id=device, device_id_type=MESH
    )


def greet(barrier, device):
    pl.semaphore_signal(barrier, inc=1, device_id=device, device_id_type=MESH)


class Place:
    def __init__(self):
        self.band, self.grid = lax.axis_index("band"), lax.axis_index("grid")
        self.p, self.q = lax.div(self.band, 16), lax.rem(self.band, 16)
        self.z, self.core = lax.div(self.q, 2), lax.rem(self.q, 2)
        self.xh, self.y = lax.div(self.p, 4), lax.rem(self.p, 4)
        self.twin = {"band": self.band + 1 - 2 * self.core}


def device(p, q, grid):
    return {"band": p * 16 + q, "grid": grid}


def meet(me):
    barrier = pltpu.get_barrier_semaphore()

    def near(k, carry):
        w = lax.rem(me.q * 2 + me.grid + k, 32)
        greet(barrier, device(me.p, lax.div(w, 2), lax.rem(w, 2)))
        return carry

    lax.fori_loop(1, 32, near, 0)

    def far(k, carry):
        p = lax.rem(me.p + k, 8)
        for n in range(4):
            greet(barrier, device(p, me.z * 2 + n // 2, n % 2))
        return carry

    lax.fori_loop(1, 8, far, 0)
    return barrier


MET = 31 + 28
FAR_Q = (8, 9, 7, 10, 6, 11, 5, 12, 4, 13, 3, 14, 2, 15, 1)
FAR_P = (6, 2, 4, 5, 3, 7, 1)


def lane_parts():
    return pl.ds(0, CUT), pl.ds(CUT, CELLS - CUT)


def exchange(me, blocks, via_a, via_b, cols, slot, grid_to, sems):
    s1, r1, s2, r2, s3, r3, s4, r4, local = sems
    low, high = lane_parts()
    stays = jnp.logical_and(slot == me.q, grid_to == me.grid)
    moves = jnp.logical_not(stays)

    def seat(q):
        return lax.rem(q, 4) * 4 + lax.div(q, 4)

    def a1(k, p_to, p_from):
        return send(blocks.at[:, p_to, low], via_a.at[p_from], s1.at[k], r1.at[k], device(p_to, slot, grid_to))

    def b1(k, q_to, q_from):
        return send(blocks.at[seat(q_to), :, high], via_b.at[q_from], s2.at[k], r2.at[q_from], device(me.p, q_to, grid_to))

    def a2(k, q_to, q_from):
        return send(via_a.at[:, seat(q_to), :], cols.at[:, q_from, low], s3.at[k], r3.at[k], device(me.p, q_to, me.grid))

    def b2(k, p_to, p_from):
        return send(via_b.at[:, p_to, :], cols.at[p_from, :, high], s4.at[k], r4.at[k], device(p_to, me.q, me.grid))

    keep_a1 = pltpu.make_async_copy(blocks.at[:, me.p, low], via_a.at[me.p], local.at[0])
    keep_b1 = pltpu.make_async_copy(blocks.at[seat(me.q), :, high], via_b.at[me.q], local.at[1])
    keep_a2 = pltpu.make_async_copy(via_a.at[:, seat(me.q), :], cols.at[:, me.q, low], local.at[2])
    keep_b2 = pltpu.make_async_copy(via_b.at[:, me.p, :], cols.at[me.p, :, high], local.at[3])

    for n in range(15):
        k = FAR_Q[n]
        b1(k, lax.rem(me.q + k, 16), slot).start()
        if n % 2 == 0 and n < 14:
            k = FAR_P[n // 2]
            a1(k, lax.rem(me.p + k, 8), me.p).start()

    @pl.when(stays)
    def _():
        keep_a1.start()
        keep_b1.start()

    @pl.when(moves)
    def _():
        a1(0, me.p, me.p).start()
        b1(0, me.q, slot).start()

    def middle_a():
        for k in range(1, 8):
            a1(k, me.p, lax.rem(me.p + 8 - k, 8)).wait_recv()

        @pl.when(stays)
        def _():
            keep_a1.wait()

        @pl.when(moves)
        def _():
            a1(0, me.p, me.p).wait_recv()

        for k in FAR_Q:
            a2(k, lax.rem(me.q + k, 16), me.q).start()
        keep_a2.start()

    def middle_b():
        for k in range(1, 16):
            b1(k, me.q, lax.rem(me.q + k, 16)).wait_recv()

        @pl.when(stays)
        def _():
            keep_b1.wait()

        @pl.when(moves)
        def _():
            b1(0, me.q, me.q).wait_recv()

        for k in FAR_P:
            b2(k, lax.rem(me.p + k, 8), me.p).start()
        keep_b2.start()

    def finish_a():
        for k in range(1, 16):
            a2(k, me.q, lax.rem(me.q + 16 - k, 16)).wait_recv()
        keep_a2.wait()

    def finish_b():
        for k in range(1, 8):
            b2(k, me.p, lax.rem(me.p + 8 - k, 8)).wait_recv()
        keep_b2.wait()

    def drain():
        for k in range(1, 8):
            a1(k, lax.rem(me.p + k, 8), me.p).wait_send()
            b2(k, lax.rem(me.p + k, 8), me.p).wait_send()
        for k in range(1, 16):
            b1(k, lax.rem(me.q + k, 16), slot).wait_send()
            a2(k, lax.rem(me.q + k, 16), me.q).wait_send()

        @pl.when(moves)
        def _():
            a1(0, me.p, me.p).wait_send()
            b1(0, me.q, slot).wait_send()

    return middle_a, middle_b, finish_a, finish_b, drain


def exchange_scratch():
    dma = pltpu.SemaphoreType.DMA
    return [
        pltpu.VMEM((8, 16, CUT), F32), pltpu.VMEM((16, 8, CELLS - CUT), F32),
        dma((8,)), dma((8,)), dma((16,)), dma((16,)), dma((16,)), dma((16,)), dma((8,)), dma((8,)), dma((4,)),
    ]


def gather_lent(me, picked, lent, send_sem, recv_sem, local, meanwhile):
    zlo, zhi = lax.rem(me.z, 2), lax.div(me.z, 2)

    def cell(q):
        z = lax.div(q, 2)
        return lent.at[me.grid, lax.rem(z, 2), lax.rem(q, 2), pl.ds(4 * me.p + lax.div(z, 2), 1), :]

    def over_q(k, q_to, q_from):
        return send(
            picked.at[pl.ds(lax.rem(q_to, 2), 1), :], cell(q_from), send_sem.at[k], recv_sem.at[k],
            device(me.p, q_to, me.grid),
        )

    keep = pltpu.make_async_copy(picked.at[pl.ds(me.core, 1), :], cell(me.q), local)
    for k in FAR_Q:
        over_q(k, lax.rem(me.q + k, 16), me.q).start()
    keep.start()
    for k in range(1, 16):
        over_q(k, me.q, lax.rem(me.q + 16 - k, 16)).wait_recv()
    keep.wait()

    def piece(half, grid, xh, y):
        return lent.at[grid, :, half, pl.ds(16 * xh + 4 * y, 4), :]

    started = []

    def x_peer(n):
        return lax.rem(me.xh + n // 2, 2), lax.rem(me.grid + n, 2)

    def along_x(slot, half, y, n):
        xh, grid = x_peer(n)
        part = piece(half, me.grid, me.xh, y)
        return send(part, part, send_sem.at[slot + n], recv_sem.at[slot + n], device(4 * xh + me.y, me.q, grid))

    def from_x(slot, half, y, n):
        xh, grid = x_peer(n)
        part = piece(half, grid, xh, y)
        return send(part, part, send_sem.at[slot + n], recv_sem.at[slot + n], device(4 * xh + me.y, me.q, grid))

    def along_y(slot, half, xh, grid, n):
        part = piece(half, grid, xh, me.y)
        return send(part, part, send_sem.at[slot + n], recv_sem.at[slot + n], device(4 * me.xh + lax.rem(me.y + n, 4), me.q, me.grid))

    def from_y(slot, half, xh, grid, n):
        part = piece(half, grid, xh, lax.rem(me.y + 4 - n, 4))
        return send(part, part, send_sem.at[slot + n], recv_sem.at[slot + n], device(4 * me.xh + lax.rem(me.y + n, 4), me.q, me.grid))

    def go(copy):
        copy.start()
        started.append(copy)

    def second(m, xh, grid):
        for n in (2, 1, 3) if m == 3 else (1, 3):
            go(along_y(24 + 4 * m, 0, xh, grid, n))
            go(along_x(40 + 4 * m, 1, lax.rem(me.y + 4 - m, 4), n))

    for n in (2, 1, 3):
        go(along_x(16, 0, me.y, n))
        go(along_y(20, 1, me.xh, me.grid, n))
    second(0, me.xh, me.grid)
    for m in range(1, 4):
        from_x(16, 0, me.y, m).wait_recv()
        from_y(20, 1, me.xh, me.grid, m).wait_recv()
        second(m, *x_peer(m))
    for m in range(3):
        near, away = (1, 3) if m % 2 == 0 else (3, 1)
        xh, grid = x_peer(m)
        y_m = lax.rem(me.y + 4 - m, 4)
        from_y(24 + 4 * m, 0, xh, grid, near).wait_recv()
        part = piece(0, grid, xh, lax.rem(me.y + 4 - near, 4))
        go(send(part, part, send_sem.at[26 + 4 * m], recv_sem.at[26 + 4 * m],
                device(4 * me.xh + lax.rem(me.y + near, 4), me.q, me.grid)))
        from_x(40 + 4 * m, 1, y_m, near).wait_recv()
        xh_near, grid_near = x_peer(near)
        xh_away, grid_away = x_peer(away)
        part = piece(1, grid_near, xh_near, y_m)
        go(send(part, part, send_sem.at[42 + 4 * m], recv_sem.at[42 + 4 * m], device(4 * xh_away + me.y, me.q, grid_away)))
    meanwhile()
    for m in range(4):
        xh, grid = x_peer(m)
        y_m = lax.rem(me.y + 4 - m, 4)
        for n in (1, 3, 2) if m == 3 else ((3, 2) if m % 2 == 0 else (1, 2)):
            from_y(24 + 4 * m, 0, xh, grid, n).wait_recv()
            from_x(40 + 4 * m, 1, y_m, n).wait_recv()

    def drain():
        for k in range(1, 16):
            over_q(k, lax.rem(me.q + k, 16), me.q).wait_send()
        for c in started:
            c.wait_send()

    return drain


def add_up(me, product, matrix, first, second, m_send, m_recv, meanwhile):
    p, q, grid = me.p, me.q, me.grid
    where = 2 * p + grid
    far = (12, 4, 13, 5, 8, 9, 10, 6, 11, 7, 14, 2, 15, 3, 1)

    def block(c):
        return pl.ds(pl.multiple_of(8 * c, 8), 8)

    def ahead(k):
        return lax.rem(p + k // 2, 8), lax.rem(grid + k, 2)

    def behind(k):
        return lax.rem(p + 8 - k // 2, 8), lax.rem(grid + k, 2)

    def scatter(k, to, slot):
        return send(
            product.at[block(2 * to[0] + to[1]), :], first.at[slot], m_send.at[k], m_recv.at[k], device(to[0], q, to[1])
        )

    for k in far:
        scatter(k, ahead(k), where).start()
    first[where] = product[block(where), :]
    meanwhile()
    for k in range(1, 16):
        b = behind(k)
        scatter(k, (p, grid), 2 * b[0] + b[1]).wait_recv()
    total = first[0]
    for k in range(1, 16):
        total = total + first[k]
    second[q] = total

    def share(k, slot, to):
        return send(second.at[slot], second.at[slot], m_send.at[15 + k], m_recv.at[15 + k], device(p, to, grid))

    for k in FAR_Q:
        share(k, q, lax.rem(q + k, 16)).start()
    for k in range(1, 16):
        scatter(k, ahead(k), where).wait_send()
    for k in range(1, 16):
        share(k, lax.rem(q + 16 - k, 16), q).wait_recv()
    total = second[0]
    for k in range(1, 16):
        total = total + second[k]
    matrix[block(where), :] = total

    def spread(k, slot, to):
        return send(
            matrix.at[block(slot), :], matrix.at[block(slot), :], m_send.at[30 + k], m_recv.at[30 + k],
            device(to[0], q, to[1]),
        )

    for k in far:
        spread(k, where, ahead(k)).start()
    for k in range(1, 16):
        share(k, q, lax.rem(q + k, 16)).wait_send()
    for k in range(1, 16):
        b = behind(k)
        spread(k, 2 * b[0] + b[1], (p, grid)).wait_recv()
    for k in range(1, 16):
        spread(k, where, ahead(k)).wait_send()


def fock_kernel(
    owners, orb_hbm, tl, til, tr, tir, sq_rows, sq_pair, field_out, matrix,
    orb, weight, cols, whole, lent, blocks, picked, own_rows, lent_rows, work,
    given, kept, arrived, field, turned, product, first, second,
    own_sem, w_send, w_recv, g_send, g_recv, t_send, t_recv, m_send, m_recv, *rest,
):
    near, far = rest[: len(rest) // 2], rest[len(rest) // 2 :]
    me = Place()
    partner = {"grid": 1 - me.grid}
    load = pltpu.make_async_copy(orb_hbm.at[:, 0, :], orb, own_sem.at[0])
    load.start()
    barrier = meet(me)
    load.wait()
    from_plane(orb, work, 0)
    to_blocks(work, blocks, 0)
    pl.semaphore_wait(barrier, MET)

    same = me.core == me.grid
    differ = jnp.logical_not(same)
    middle_a, middle_b, finish_a, finish_b, drain_near = exchange(me, blocks, near[0], near[1], cols, me.q, me.grid, near[2:])
    keep = pltpu.make_async_copy(orb, whole.at[me.grid], own_sem.at[0])
    to_twin = send(orb, whole.at[me.grid], w_send.at[0], w_recv.at[0], me.twin)
    to_partner = send(orb, whole.at[me.grid], w_send.at[0], w_recv.at[1], partner)
    from_partner = send(orb, whole.at[1 - me.grid], w_send.at[0], w_recv.at[1], partner)
    forward = send(whole.at[1 - me.grid], whole.at[1 - me.grid], w_send.at[1], w_recv.at[1], me.twin)

    @pl.when(same)
    def _():
        keep.start()
        to_twin.start()

    @pl.when(differ)
    def _():
        to_partner.start()

    fill_kernel(weight, sq_rows, sq_pair)
    middle_a()
    middle_b()
    finish_a()
    finish_b()
    for r in range(2):
        owner = owners[r]
        picked[r : r + 1, :] = cols[pl.ds(lax.div(owner, 16), 1), pl.ds(lax.rem(owner, 16), 1), :].reshape(1, CELLS)

    @pl.when(same)
    def _():
        from_partner.wait_recv()
        forward.start()

    def meanwhile():
        @pl.when(same)
        def _():
            keep.wait()

        @pl.when(differ)
        def _():
            to_twin.wait_recv()
            forward.wait_recv()

        for s in range(2):
            from_plane(whole.at[s], own_rows, s)

    drain_gather = gather_lent(me, picked, lent, g_send, g_recv, own_sem.at[1], meanwhile)

    for s in range(2):
        from_blocks(lent.at[s], lent_rows, s)
    spectra(own_rows, lent_rows, work, tl, til, tr, weight, 36, 36)
    potentials(own_rows, lent_rows, work, til, tir, 1 - me.core, 18)
    to_blocks(own_rows, given, 1 - me.core)
    give = send(given, arrived, t_send, t_recv, me.twin)
    give.start()
    potentials(own_rows, lent_rows, work, til, tir, me.core, 18)
    to_blocks(own_rows, kept, me.core)
    give.wait_recv()
    kept[...] = kept[...] + arrived[...]

    middle_a, middle_b, finish_a, finish_b, drain_far = exchange(
        me, kept, far[0], far[1], field, 2 * me.z + me.grid, me.core, far[2:]
    )

    @pl.when(same)
    def _():
        to_twin.wait_send()
        forward.wait_send()

    @pl.when(differ)
    def _():
        to_partner.wait_send()

    give.wait_send()
    drain_gather()
    drain_near()
    middle_a()
    middle_b()
    dot = lambda a, b: lax.dot_general(a, b, (((1,), (1,)), ((), ())), preferred_element_type=F32)

    def overlap(lanes, width):
        oh, ol = halves(cols[:, :, lanes].reshape(BANDS, width))
        fh, fl = halves(field[:, :, lanes].reshape(BANDS, width))
        return (dot(oh, fl) + dot(ol, fh)) + dot(oh, fh)

    low, high = lane_parts()
    finish_b()
    product[...] = overlap(high, CELLS - CUT)
    finish_a()
    product[...] = (product[...] + overlap(low, CUT)) * (1.0 / 373248.0)
    store = pltpu.make_async_copy(turned, field_out.at[:, 0, :], own_sem.at[1])

    def turn():
        drain_far()
        for n in range(12):
            width = min(128, CELLS - 128 * n)
            tile = field[:, :, pl.ds(128 * n, width)].reshape(BANDS, width)
            turned[pl.ds(128 * n, width), :] = tile.T
        store.start()

    add_up(me, product, matrix, first, second, m_send, m_recv, turn)
    store.wait()


def fock_call(owners, orb):
    vm = pl.BlockSpec(memory_space=pltpu.VMEM)
    dma = pltpu.SemaphoreType.DMA
    v = lambda *shape: pltpu.VMEM(shape, F32)
    return pl.pallas_call(
        fock_kernel,
        out_shape=(
            jax.ShapeDtypeStruct((CELLS, 1, BANDS), F32),
            jax.ShapeDtypeStruct((BANDS, BANDS), F32),
        ),
        in_specs=[pl.BlockSpec(memory_space=pltpu.SMEM), pl.BlockSpec(memory_space=pl.ANY)] + [vm] * 6,
        out_specs=(pl.BlockSpec(memory_space=pl.ANY), vm),
        scratch_shapes=[
            v(36, 5184), v(N, PAD, 128), v(8, 16, CELLS), v(2, 36, 5184), v(2, 2, 2, 32, CELLS), v(16, 8, CELLS), v(2, CELLS),
            v(5184, 128), v(5184, 128), v(5184, 128),
            v(16, 8, CELLS), v(16, 8, CELLS), v(16, 8, CELLS), v(8, 16, CELLS), v(CELLS, BANDS), v(BANDS, BANDS), v(16, 8, BANDS), v(16, 8, BANDS),
            dma((2,)), dma((2,)), dma((2,)), dma((56,)), dma((56,)), dma, dma, dma((46,)), dma((46,)),
        ] + exchange_scratch() + exchange_scratch(),
        compiler_params=pltpu.CompilerParams(collective_id=0, has_side_effects=True, vmem_limit_bytes=60 << 20),
    )(owners, orb, *tables())


def result_kernel(field, matrix, field_out, matrix_out, sems):
    copies = [pltpu.make_async_copy(matrix, matrix_out, sems.at[6])]
    for n in range(6):
        rows = pl.ds(243 * n, 243)
        copies.append(pltpu.make_async_copy(field.at[rows], field_out.at[rows], sems.at[n]))
    for c in copies:
        c.start()
    for c in copies:
        c.wait()


def result_call(field, matrix):
    hbm = pl.BlockSpec(memory_space=pl.ANY)
    return pl.pallas_call(
        result_kernel,
        out_shape=(jax.ShapeDtypeStruct(field.shape, F32), jax.ShapeDtypeStruct(matrix.shape, F32)),
        in_specs=[hbm, hbm],
        out_specs=(hbm, hbm),
        scratch_shapes=[pltpu.SemaphoreType.DMA((7,))],
    )(field, matrix)


def shards(orbitals, owners):
    field, matrix = fock_call(owners, orbitals.transpose(1, 0, 2))
    field, matrix = result_call(field, matrix)
    return (field.transpose(1, 2, 0), matrix)


def solution(mesh):
    in_specs = (P("band", "grid", None), P())
    out_specs = (P("grid", None, "band"), P())
    return jax.shard_map(shards, mesh=mesh, in_specs=in_specs, out_specs=out_specs, check_vma=False)
```

```python
import functools
import math

import jax
import jax.numpy as jnp
import numpy as np
from jax import lax
from jax.experimental import pallas as pl
from jax.experimental.pallas import tpu as pltpu
from jax.sharding import PartitionSpec as P

N = 72
PAD = 80
GROUP = 9
BF = jnp.bfloat16
F32 = jnp.float32

def tables():
    pos = np.arange(N)
    half = N // 2
    freq = np.where(pos <= half, pos, pos - half)
    ang = (freq[:, None] * pos[None, :] % N) * (2.0 * math.pi / N)
    w = np.where((pos == 0) | (pos == half), 1.0 / math.sqrt(N), math.sqrt(2.0 / N))
    basis = np.where((pos <= half)[:, None], np.cos(ang), np.sin(ang)) * w[:, None]
    sq = (freq * (2.0 * math.pi / N)) ** 2

    def split(t):
        hi = jnp.asarray(t, F32).astype(BF)
        lo = (jnp.asarray(t, F32) - hi.astype(F32)).astype(BF)
        return hi, lo

    def left(t):
        hi, lo = split(t)
        put = lambda a: jnp.pad(a, ((0, PAD - N), (0, PAD - N)))
        return jnp.concatenate([put(hi), put(hi), put(lo)], axis=1)

    def right(t):
        hi, lo = split(t)
        put = lambda a: jnp.pad(a, ((0, 128 - N), (0, 128 - N)))
        top = jnp.concatenate([put(hi), put(lo)], axis=1)
        low = jnp.concatenate([put(hi), jnp.zeros((128, 128), BF)], axis=1)
        return jnp.concatenate([top, low], axis=0)

    sq_rows = np.zeros((PAD, 128), np.float32); sq_rows[:N] = sq[:, None]
    sq_pair = np.zeros((N, 128), np.float32); sq_pair[:, :N] = sq[:, None] + sq[None, :]
    return (left(basis), left(basis.T), right(basis.T), right(basis), jnp.asarray(sq_rows), jnp.asarray(sq_pair))


def halves(v):
    hi = v.astype(BF)
    lo = (v - hi.astype(F32)).astype(BF)
    return hi, lo


def left_dot(table, planes):
    cols = []
    for v in planes:
        hi, lo = halves(v)
        cols.append(jnp.concatenate([hi, lo, hi], axis=0))
    out = jnp.dot(table, jnp.concatenate(cols, axis=1), preferred_element_type=F32)
    return [out[:, 128 * i : 128 * i + 128] for i in range(len(planes))]


def right_dot(v, table):
    hi, lo = halves(v)
    out = jnp.dot(jnp.concatenate([hi, lo], axis=1), table, preferred_element_type=F32)
    return out[:, :128] + out[:, 128:]


def pad_rows(v):
    return jnp.concatenate([v, jnp.zeros((PAD - N, 128), F32)], axis=0)


def fill_kernel(weight, sq_rows, sq_pair):
    def one(b, carry):
        total = sq_rows[...] + sq_pair[pl.ds(b, 1), :]
        positive = total > 0
        weight[b] = jnp.where(positive, (-0.25 * math.pi) / jnp.where(positive, total, 1.0), 0.0)
        return carry

    lax.fori_loop(0, N, one, 0)


def spectra(own, lent, work, tl, til, tr, weight, UA, UB):
    lane = lax.broadcasted_iota(jnp.int32, (1, 128), 1) < N

    def stage_a(step, carry):
        span = 2 * N * GROUP
        for u in range(UA // GROUP):
            base = pl.multiple_of((step * (UA // GROUP) + u) * span, 8)
            rows = pl.ds(base, span)
            d = jnp.where(lane, own[rows, :] * lent[rows, :], 0.0)
            z = right_dot(d, tr[...])
            for n in range(GROUP):
                at = 2 * N * n
                planes = left_dot(tl[...], [pad_rows(z[at : at + N]), pad_rows(z[at + N : at + 2 * N])])
                work[pl.ds(base + at, 2 * N), :] = jnp.concatenate([v[:N] for v in planes], axis=0)
        return carry

    lax.fori_loop(0, 36 // UA, stage_a, 0)

    def stage_b(step, carry):
        for u in range(UB):
            b = (step * UB + u) * 2
            planes = [pad_rows(work[pl.ds(b + i, N, stride=N), :]) for i in range(2)]
            planes = left_dot(tl[...], planes)
            for i in range(2):
                planes[i] = planes[i] * weight[b + i]
            planes = left_dot(til[...], planes)
            for i in range(2):
                work[pl.ds(b + i, N, stride=N), :] = planes[i][:N]
        return carry

    lax.fori_loop(0, 36 // UB, stage_b, 0)


def potentials(own, lent, work, til, tir, row, UC, pairs):
    def stage_c(step, carry):
        span = 2 * N * GROUP
        for u in range(UC // GROUP):
            base = pl.multiple_of(row + (step * (UC // GROUP) + u) * span, 8)
            planes = []
            for n in range(GROUP):
                v = work[pl.ds(base + 2 * N * n, 2 * N), :]
                planes += left_dot(til[...], [pad_rows(v[:N]), pad_rows(v[N:])])
            rows = pl.ds(base, span)
            own[rows, :] = right_dot(jnp.concatenate([v[:N] for v in planes], axis=0), tir[...]) * lent[rows, :]
        return carry

    lax.fori_loop(0, pairs // UC, stage_c, 0)


def from_plane(ref, dst, slab):
    for y in range(N):
        dst[pl.ds(slab * 2592 + y, 36, stride=N), :N] = ref[:, N * y : N * y + N]


def spans():
    for j in range(81):
        first, at = divmod(N * j, 1458)
        fit = min(N, 1458 - at)
        yield j, first, at, fit


def from_blocks(ref, dst, slab):
    for j, first, at, fit in spans():
        rows = pl.ds(slab * 2592 + j, 32, stride=81)
        v = ref[first // 2, first % 2, :, at : at + fit]
        if fit < N:
            v = jnp.concatenate([v, ref[(first + 1) // 2, (first + 1) % 2, :, : N - fit]], axis=1)
        dst[rows, :N] = v


def to_blocks(src, ref, row, count, place):
    for h in range(4):
        for j, first, at, fit in spans():
            v = src[pl.ds(row + 81 * h + j, count, stride=324), :]
            ref[4 * first + h, place : place + count, at : at + fit] = v[:, :fit]
            if fit < N:
                ref[4 * first + 4 + h, place : place + count, : N - fit] = v[:, fit:N]


MESH = pl.DeviceIdType.MESH
BANDS = 128
CELLS = 1458
CUT = 768


def send(src, dst, send_sem, recv_sem, device):
    return pltpu.make_async_remote_copy(
        src_ref=src, dst_ref=dst, send_sem=send_sem, recv_sem=recv_sem, device_id=device, device_id_type=MESH
    )


def greet(barrier, device):
    pl.semaphore_signal(barrier, inc=1, device_id=device, device_id_type=MESH)


class Place:
    def __init__(self):
        self.band, self.grid = lax.axis_index("band"), lax.axis_index("grid")
        self.p, self.q = lax.div(self.band, 16), lax.rem(self.band, 16)
        self.z, self.core = lax.div(self.q, 2), lax.rem(self.q, 2)
        self.xh, self.y = lax.div(self.p, 4), lax.rem(self.p, 4)
        self.twin = {"band": self.band + 1 - 2 * self.core}


def device(p, q, grid):
    return {"band": p * 16 + q, "grid": grid}


def meet(me):
    barrier = pltpu.get_barrier_semaphore()

    def near(k, carry):
        w = lax.rem(me.q * 2 + me.grid + k, 32)
        greet(barrier, device(me.p, lax.div(w, 2), lax.rem(w, 2)))
        return carry

    lax.fori_loop(1, 32, near, 0)

    def far(k, carry):
        p = lax.rem(me.p + k, 8)
        for n in range(4):
            greet(barrier, device(p, me.z * 2 + n // 2, n % 2))
        return carry

    lax.fori_loop(1, 8, far, 0)
    return barrier


MET = 31 + 28
FAR_Q = (8, 9, 7, 10, 6, 11, 5, 12, 4, 13, 3, 14, 2, 15, 1)
FAR_P = (6, 2, 4, 5, 3, 7, 1)


def lane_parts():
    return pl.ds(0, CUT), pl.ds(CUT, CELLS - CUT)


def exchange(me, blocks, via_a, via_b, cols, slot, grid_to, sems, parts):
    s1, r1, s2, r2, s3, r3, s4, r4, local = sems
    low, high = lane_parts()
    stays = jnp.logical_and(slot == me.q, grid_to == me.grid)
    moves = jnp.logical_not(stays)

    def seat(q):
        return lax.rem(q, 4) * 4 + lax.div(q, 4)

    def a1(k, p_to, p_from):
        return send(blocks.at[:, p_to, low], via_a.at[p_from], s1.at[k], r1.at[k], device(p_to, slot, grid_to))

    def rows(part):
        return pl.ds(8 // parts * part, 8 // parts)

    def b1(part, k, q_to, q_from):
        return send(
            blocks.at[seat(q_to), rows(part), high], via_b.at[q_from, rows(part), :],
            s2.at[16 * part + k], r2.at[16 * part + q_from], device(me.p, q_to, grid_to),
        )

    def a2(k, q_to, q_from):
        return send(via_a.at[:, seat(q_to), :], cols.at[:, q_from, low], s3.at[k], r3.at[k], device(me.p, q_to, me.grid))

    def b2(k, p_to, p_from):
        return send(via_b.at[:, p_to, :], cols.at[p_from, :, high], s4.at[k], r4.at[k], device(p_to, me.q, me.grid))

    keep_a1 = pltpu.make_async_copy(blocks.at[:, me.p, low], via_a.at[me.p], local.at[0])
    def keep_b1(part):
        return pltpu.make_async_copy(
            blocks.at[seat(me.q), rows(part), high], via_b.at[me.q, rows(part), :], local.at[4 * part + 1]
        )

    keep_a2 = pltpu.make_async_copy(via_a.at[:, seat(me.q), :], cols.at[:, me.q, low], local.at[2])
    keep_b2 = pltpu.make_async_copy(via_b.at[:, me.p, :], cols.at[me.p, :, high], local.at[3])

    def begin(part):
        for n in range(15):
            k = FAR_Q[n]
            b1(part, k, lax.rem(me.q + k, 16), slot).start()
            if parts == 1 and n % 2 == 0 and n < 14:
                k = FAR_P[n // 2]
                a1(k, lax.rem(me.p + k, 8), me.p).start()
            if parts == 2 and n % 4 == 1 and n < 10:
                p_to = 4 * part + lax.rem(me.y + (2, 1, 3)[n // 4], 4)
                a1(lax.rem(p_to + 8 - me.p, 8), p_to, me.p).start()

        @pl.when(stays)
        def _():
            keep_b1(part).start()

        @pl.when(moves)
        def _():
            b1(part, 0, me.q, slot).start()

        here = (part == me.xh) if parts == 2 else True

        @pl.when(jnp.logical_and(stays, here))
        def _():
            keep_a1.start()

        @pl.when(jnp.logical_and(moves, here))
        def _():
            a1(0, me.p, me.p).start()

        if parts == 2:
            @pl.when(jnp.logical_not(here))
            def _():
                a1(4, lax.rem(me.p + 4, 8), me.p).start()

    def middle_a():
        for k in range(1, 8):
            a1(k, me.p, lax.rem(me.p + 8 - k, 8)).wait_recv()

        @pl.when(stays)
        def _():
            keep_a1.wait()

        @pl.when(moves)
        def _():
            a1(0, me.p, me.p).wait_recv()

        for k in FAR_Q:
            a2(k, lax.rem(me.q + k, 16), me.q).start()
        keep_a2.start()

    def middle_b():
        for part in range(parts):
            for k in range(1, 16):
                b1(part, k, me.q, lax.rem(me.q + k, 16)).wait_recv()

        @pl.when(stays)
        def _():
            for part in range(parts):
                keep_b1(part).wait()

        @pl.when(moves)
        def _():
            for part in range(parts):
                b1(part, 0, me.q, me.q).wait_recv()

        for k in FAR_P:
            b2(k, lax.rem(me.p + k, 8), me.p).start()
        keep_b2.start()

    def finish_a():
        for k in range(1, 16):
            a2(k, me.q, lax.rem(me.q + 16 - k, 16)).wait_recv()
        keep_a2.wait()

    def finish_b():
        for k in range(1, 8):
            b2(k, me.p, lax.rem(me.p + 8 - k, 8)).wait_recv()
        keep_b2.wait()

    def drain():
        for k in range(1, 8):
            a1(k, lax.rem(me.p + k, 8), me.p).wait_send()
            b2(k, lax.rem(me.p + k, 8), me.p).wait_send()
        for k in range(1, 16):
            for part in range(parts):
                b1(part, k, lax.rem(me.q + k, 16), slot).wait_send()
            a2(k, lax.rem(me.q + k, 16), me.q).wait_send()

        @pl.when(moves)
        def _():
            a1(0, me.p, me.p).wait_send()
            for part in range(parts):
                b1(part, 0, me.q, slot).wait_send()

    return begin, middle_a, middle_b, finish_a, finish_b, drain


def exchange_scratch():
    dma = pltpu.SemaphoreType.DMA
    return [
        pltpu.VMEM((8, 16, CUT), F32), pltpu.VMEM((16, 8, CELLS - CUT), F32),
        dma((8,)), dma((8,)), dma((32,)), dma((32,)), dma((16,)), dma((16,)), dma((8,)), dma((8,)), dma((6,)),
    ]


def gather_lent(me, picked, lent, send_sem, recv_sem, local, meanwhile):
    zlo, zhi = lax.rem(me.z, 2), lax.div(me.z, 2)

    def cell(q):
        z = lax.div(q, 2)
        return lent.at[me.grid, lax.rem(z, 2), lax.rem(q, 2), pl.ds(4 * me.p + lax.div(z, 2), 1), :]

    def over_q(k, q_to, q_from):
        return send(
            picked.at[pl.ds(lax.rem(q_to, 2), 1), :], cell(q_from), send_sem.at[k], recv_sem.at[k],
            device(me.p, q_to, me.grid),
        )

    keep = pltpu.make_async_copy(picked.at[pl.ds(me.core, 1), :], cell(me.q), local)
    for k in FAR_Q:
        over_q(k, lax.rem(me.q + k, 16), me.q).start()
    keep.start()
    for k in range(1, 16):
        over_q(k, me.q, lax.rem(me.q + 16 - k, 16)).wait_recv()
    keep.wait()

    def piece(half, grid, xh, y):
        return lent.at[grid, :, half, pl.ds(16 * xh + 4 * y, 4), :]

    started = []

    def x_peer(n):
        return lax.rem(me.xh + n // 2, 2), lax.rem(me.grid + n, 2)

    def along_x(slot, half, y, n):
        xh, grid = x_peer(n)
        part = piece(half, me.grid, me.xh, y)
        return send(part, part, send_sem.at[slot + n], recv_sem.at[slot + n], device(4 * xh + me.y, me.q, grid))

    def from_x(slot, half, y, n):
        xh, grid = x_peer(n)
        part = piece(half, grid, xh, y)
        return send(part, part, send_sem.at[slot + n], recv_sem.at[slot + n], device(4 * xh + me.y, me.q, grid))

    def along_y(slot, half, xh, grid, n):
        part = piece(half, grid, xh, me.y)
        return send(part, part, send_sem.at[slot + n], recv_sem.at[slot + n], device(4 * me.xh + lax.rem(me.y + n, 4), me.q, me.grid))

    def from_y(slot, half, xh, grid, n):
        part = piece(half, grid, xh, lax.rem(me.y + 4 - n, 4))
        return send(part, part, send_sem.at[slot + n], recv_sem.at[slot + n], device(4 * me.xh + lax.rem(me.y + n, 4), me.q, me.grid))

    def go(copy):
        copy.start()
        started.append(copy)

    for n in range(1, 4):
        go(along_x(16, 0, me.y, n))
        go(along_y(20, 1, me.xh, me.grid, n))
    for n in range(1, 4):
        go(along_y(24, 0, me.xh, me.grid, n))
        go(along_x(40, 1, me.y, n))
    for m in range(1, 4):
        from_x(16, 0, me.y, m).wait_recv()
        xh, grid = x_peer(m)
        for n in range(1, 4):
            go(along_y(24 + 4 * m, 0, xh, grid, n))
        from_y(20, 1, me.xh, me.grid, m).wait_recv()
        for n in range(1, 4):
            go(along_x(40 + 4 * m, 1, lax.rem(me.y + 4 - m, 4), n))
    meanwhile()
    for m in range(4):
        xh, grid = x_peer(m)
        for n in range(1, 4):
            from_y(24 + 4 * m, 0, xh, grid, n).wait_recv()
            from_x(40 + 4 * m, 1, lax.rem(me.y + 4 - m, 4), n).wait_recv()

    def drain():
        for k in range(1, 16):
            over_q(k, lax.rem(me.q + k, 16), me.q).wait_send()
        for c in started:
            c.wait_send()

    return drain


def add_up(me, product, matrix, first, second, m_send, m_recv, meanwhile):
    p, q, grid = me.p, me.q, me.grid
    where = 2 * p + grid
    far = (12, 4, 13, 5, 8, 9, 10, 6, 11, 7, 14, 2, 15, 3, 1)

    def block(c):
        return pl.ds(pl.multiple_of(8 * c, 8), 8)

    def ahead(k):
        return lax.rem(p + k // 2, 8), lax.rem(grid + k, 2)

    def behind(k):
        return lax.rem(p + 8 - k // 2, 8), lax.rem(grid + k, 2)

    def scatter(k, to, slot):
        return send(
            product.at[block(2 * to[0] + to[1]), :], first.at[slot], m_send.at[k], m_recv.at[k], device(to[0], q, to[1])
        )

    for k in far:
        scatter(k, ahead(k), where).start()
    first[where] = product[block(where), :]
    meanwhile()
    for k in range(1, 16):
        b = behind(k)
        scatter(k, (p, grid), 2 * b[0] + b[1]).wait_recv()
    total = first[0]
    for k in range(1, 16):
        total = total + first[k]
    second[q] = total

    def share(k, slot, to):
        return send(second.at[slot], second.at[slot], m_send.at[15 + k], m_recv.at[15 + k], device(p, to, grid))

    for k in FAR_Q:
        share(k, q, lax.rem(q + k, 16)).start()
    for k in range(1, 16):
        scatter(k, ahead(k), where).wait_send()
    for k in range(1, 16):
        share(k, lax.rem(q + 16 - k, 16), q).wait_recv()
    total = second[0]
    for k in range(1, 16):
        total = total + second[k]
    matrix[block(where), :] = total

    def spread(k, slot, to):
        return send(
            matrix.at[block(slot), :], matrix.at[block(slot), :], m_send.at[30 + k], m_recv.at[30 + k],
            device(to[0], q, to[1]),
        )

    for k in far:
        spread(k, where, ahead(k)).start()
    for k in range(1, 16):
        share(k, q, lax.rem(q + k, 16)).wait_send()
    for k in range(1, 16):
        b = behind(k)
        spread(k, 2 * b[0] + b[1], (p, grid)).wait_recv()
    for k in range(1, 16):
        spread(k, where, ahead(k)).wait_send()


def fock_kernel(
    owners, orb_hbm, tl, til, tr, tir, sq_rows, sq_pair, field_out, matrix,
    orb, weight, cols, whole, lent, blocks, picked, own_rows, lent_rows, work,
    given, kept, arrived, field, turned, product, first, second,
    own_sem, w_send, w_recv, g_send, g_recv, t_send, t_recv, m_send, m_recv, *rest,
):
    near, far = rest[: len(rest) // 2], rest[len(rest) // 2 :]
    me = Place()
    partner = {"grid": 1 - me.grid}
    load = pltpu.make_async_copy(orb_hbm.at[:, 0, :], orb, own_sem.at[0])
    load.start()
    barrier = meet(me)
    load.wait()
    from_plane(orb, work, 0)
    to_blocks(work, blocks, 0, 8, 0)
    pl.semaphore_wait(barrier, MET)

    same = me.core == me.grid
    differ = jnp.logical_not(same)
    begin, middle_a, middle_b, finish_a, finish_b, drain_near = exchange(
        me, blocks, near[0], near[1], cols, me.q, me.grid, near[2:], 1
    )
    begin(0)
    keep = pltpu.make_async_copy(orb, whole.at[me.grid], own_sem.at[0])
    to_twin = send(orb, whole.at[me.grid], w_send.at[0], w_recv.at[0], me.twin)
    to_partner = send(orb, whole.at[me.grid], w_send.at[0], w_recv.at[1], partner)
    from_partner = send(orb, whole.at[1 - me.grid], w_send.at[0], w_recv.at[1], partner)
    forward = send(whole.at[1 - me.grid], whole.at[1 - me.grid], w_send.at[1], w_recv.at[1], me.twin)

    @pl.when(same)
    def _():
        keep.start()
        to_twin.start()

    @pl.when(differ)
    def _():
        to_partner.start()

    fill_kernel(weight, sq_rows, sq_pair)
    middle_a()
    middle_b()
    finish_a()
    finish_b()
    for r in range(2):
        owner = owners[r]
        picked[r : r + 1, :] = cols[pl.ds(lax.div(owner, 16), 1), pl.ds(lax.rem(owner, 16), 1), :].reshape(1, CELLS)

    @pl.when(same)
    def _():
        from_partner.wait_recv()
        forward.start()

    def meanwhile():
        @pl.when(same)
        def _():
            keep.wait()

        @pl.when(differ)
        def _():
            to_twin.wait_recv()
            forward.wait_recv()

        for s in range(2):
            from_plane(whole.at[s], own_rows, s)

    drain_gather = gather_lent(me, picked, lent, g_send, g_recv, own_sem.at[1], meanwhile)

    for s in range(2):
        from_blocks(lent.at[s], lent_rows, s)
    spectra(own_rows, lent_rows, work, tl, til, tr, weight, 36, 36)
    begin, middle_a, middle_b, finish_a, finish_b, drain_far = exchange(
        me, kept, far[0], far[1], field, 2 * me.z + me.grid, me.core, far[2:], 2
    )

    def give(part):
        piece = pl.ds(4 * part, 4)
        return send(given.at[:, piece, :], arrived.at[:, piece, :], t_send.at[part], t_recv.at[part], me.twin)

    for part in range(2):
        row = (1 - me.core) * 2592 + part * 1296
        potentials(own_rows, lent_rows, work, til, tir, row, 9, 9)
        to_blocks(own_rows, given, row, 4, 4 * part)
        give(part).start()
    for part in range(2):
        row = me.core * 2592 + part * 1296
        potentials(own_rows, lent_rows, work, til, tir, row, 9, 9)
        to_blocks(own_rows, kept, row, 4, 4 * part)
    for part in range(2):
        give(part).wait_recv()
        at = slice(4 * part, 4 * part + 4)
        kept[:, at, :] = kept[:, at, :] + arrived[:, at, :]
        begin(part)

    @pl.when(same)
    def _():
        to_twin.wait_send()
        forward.wait_send()

    @pl.when(differ)
    def _():
        to_partner.wait_send()

    for part in range(2):
        give(part).wait_send()
    drain_gather()
    drain_near()
    middle_a()
    middle_b()
    dot = lambda a, b: lax.dot_general(a, b, (((1,), (1,)), ((), ())), preferred_element_type=F32)

    def overlap(lanes, width):
        oh, ol = halves(cols[:, :, lanes].reshape(BANDS, width))
        fh, fl = halves(field[:, :, lanes].reshape(BANDS, width))
        return (dot(oh, fl) + dot(ol, fh)) + dot(oh, fh)

    low, high = lane_parts()
    finish_b()
    product[...] = overlap(high, CELLS - CUT)
    finish_a()
    product[...] = (product[...] + overlap(low, CUT)) * (1.0 / 373248.0)
    store = pltpu.make_async_copy(turned, field_out.at[:, 0, :], own_sem.at[1])

    def turn():
        drain_far()
        for n in range(12):
            width = min(128, CELLS - 128 * n)
            tile = field[:, :, pl.ds(128 * n, width)].reshape(BANDS, width)
            turned[pl.ds(128 * n, width), :] = tile.T
        store.start()

    add_up(me, product, matrix, first, second, m_send, m_recv, turn)
    store.wait()


def fock_call(owners, orb):
    vm = pl.BlockSpec(memory_space=pltpu.VMEM)
    dma = pltpu.SemaphoreType.DMA
    v = lambda *shape: pltpu.VMEM(shape, F32)
    return pl.pallas_call(
        fock_kernel,
        out_shape=(
            jax.ShapeDtypeStruct((CELLS, 1, BANDS), F32),
            jax.ShapeDtypeStruct((BANDS, BANDS), F32),
        ),
        in_specs=[pl.BlockSpec(memory_space=pltpu.SMEM), pl.BlockSpec(memory_space=pl.ANY)] + [vm] * 6,
        out_specs=(pl.BlockSpec(memory_space=pl.ANY), vm),
        scratch_shapes=[
            v(36, 5184), v(N, PAD, 128), v(8, 16, CELLS), v(2, 36, 5184), v(2, 2, 2, 32, CELLS), v(16, 8, CELLS), v(2, CELLS),
            v(5184, 128), v(5184, 128), v(5184, 128),
            v(16, 8, CELLS), v(16, 8, CELLS), v(16, 8, CELLS), v(8, 16, CELLS), v(CELLS, BANDS), v(BANDS, BANDS), v(16, 8, BANDS), v(16, 8, BANDS),
            dma((2,)), dma((2,)), dma((2,)), dma((56,)), dma((56,)), dma((2,)), dma((2,)), dma((46,)), dma((46,)),
        ] + exchange_scratch() + exchange_scratch(),
        compiler_params=pltpu.CompilerParams(collective_id=0, has_side_effects=True, vmem_limit_bytes=60 << 20),
    )(owners, orb, *tables())


def shards(orbitals, owners):
    field, matrix = fock_call(owners, orbitals.transpose(1, 0, 2))
    return (field.transpose(1, 2, 0), matrix)


def solution(mesh):
    in_specs = (P("band", "grid", None), P())
    out_specs = (P("grid", None, "band"), P())
    return jax.shard_map(shards, mesh=mesh, in_specs=in_specs, out_specs=out_specs, check_vma=False)
```

```python
import functools
import math

import jax
import jax.numpy as jnp
import numpy as np
from jax import lax
from jax.experimental import pallas as pl
from jax.experimental.pallas import tpu as pltpu
from jax.sharding import PartitionSpec as P

N = 72
PAD = 80
GROUP = 9
BF = jnp.bfloat16
F32 = jnp.float32

def tables():
    pos = np.arange(N)
    half = N // 2
    freq = np.where(pos <= half, pos, pos - half)
    ang = (freq[:, None] * pos[None, :] % N) * (2.0 * math.pi / N)
    w = np.where((pos == 0) | (pos == half), 1.0 / math.sqrt(N), math.sqrt(2.0 / N))
    basis = np.where((pos <= half)[:, None], np.cos(ang), np.sin(ang)) * w[:, None]
    sq = (freq * (2.0 * math.pi / N)) ** 2

    def split(t):
        hi = jnp.asarray(t, F32).astype(BF)
        lo = (jnp.asarray(t, F32) - hi.astype(F32)).astype(BF)
        return hi, lo

    def left(t):
        hi, lo = split(t)
        put = lambda a: jnp.pad(a, ((0, PAD - N), (0, PAD - N)))
        return jnp.concatenate([put(hi), put(hi), put(lo)], axis=1)

    def right(t):
        hi, lo = split(t)
        put = lambda a: jnp.pad(a, ((0, 128 - N), (0, 128 - N)))
        top = jnp.concatenate([put(hi), put(lo)], axis=1)
        low = jnp.concatenate([put(hi), jnp.zeros((128, 128), BF)], axis=1)
        return jnp.concatenate([top, low], axis=0)

    sq_rows = np.zeros((PAD, 128), np.float32); sq_rows[:N] = sq[:, None]
    sq_pair = np.zeros((N, 128), np.float32); sq_pair[:, :N] = sq[:, None] + sq[None, :]
    return (left(basis), left(basis.T), right(basis.T), right(basis), jnp.asarray(sq_rows), jnp.asarray(sq_pair))


def halves(v):
    hi = v.astype(BF)
    lo = (v - hi.astype(F32)).astype(BF)
    return hi, lo


def left_dot(table, planes):
    cols = []
    for v in planes:
        hi, lo = halves(v)
        cols.append(jnp.concatenate([hi, lo, hi], axis=0))
    out = jnp.dot(table, jnp.concatenate(cols, axis=1), preferred_element_type=F32)
    return [out[:, 128 * i : 128 * i + 128] for i in range(len(planes))]


def right_dot(v, table):
    hi, lo = halves(v)
    out = jnp.dot(jnp.concatenate([hi, lo], axis=1), table, preferred_element_type=F32)
    return out[:, :128] + out[:, 128:]


def pad_rows(v):
    return jnp.concatenate([v, jnp.zeros((PAD - N, 128), F32)], axis=0)


def fill_kernel(weight, sq_rows, sq_pair):
    def one(b, carry):
        total = sq_rows[...] + sq_pair[pl.ds(b, 1), :]
        positive = total > 0
        weight[b] = jnp.where(positive, (-0.25 * math.pi) / jnp.where(positive, total, 1.0), 0.0)
        return carry

    lax.fori_loop(0, N, one, 0)


def spectra(own, lent, work, tl, til, tr, weight, UA, UB):
    lane = lax.broadcasted_iota(jnp.int32, (1, 128), 1) < N

    def stage_a(step, carry):
        span = 2 * N * GROUP
        for u in range(UA // GROUP):
            base = pl.multiple_of((step * (UA // GROUP) + u) * span, 8)
            rows = pl.ds(base, span)
            d = jnp.where(lane, own[rows, :] * lent[rows, :], 0.0)
            z = right_dot(d, tr[...])
            for n in range(GROUP):
                at = 2 * N * n
                planes = left_dot(tl[...], [pad_rows(z[at : at + N]), pad_rows(z[at + N : at + 2 * N])])
                work[pl.ds(base + at, 2 * N), :] = jnp.concatenate([v[:N] for v in planes], axis=0)
        return carry

    lax.fori_loop(0, 36 // UA, stage_a, 0)

    def stage_b(step, carry):
        for u in range(UB):
            b = (step * UB + u) * 2
            planes = [pad_rows(work[pl.ds(b + i, N, stride=N), :]) for i in range(2)]
            planes = left_dot(tl[...], planes)
            for i in range(2):
                planes[i] = planes[i] * weight[b + i]
            planes = left_dot(til[...], planes)
            for i in range(2):
                work[pl.ds(b + i, N, stride=N), :] = planes[i][:N]
        return carry

    lax.fori_loop(0, 36 // UB, stage_b, 0)


def potentials(own, lent, work, til, tir, slab, UC):
    def stage_c(step, carry):
        span = 2 * N * GROUP
        for u in range(UC // GROUP):
            base = pl.multiple_of(slab * 2592 + (step * (UC // GROUP) + u) * span, 8)
            planes = []
            for n in range(GROUP):
                v = work[pl.ds(base + 2 * N * n, 2 * N), :]
                planes += left_dot(til[...], [pad_rows(v[:N]), pad_rows(v[N:])])
            rows = pl.ds(base, span)
            own[rows, :] = right_dot(jnp.concatenate([v[:N] for v in planes], axis=0), tir[...]) * lent[rows, :]
        return carry

    lax.fori_loop(0, 18 // UC, stage_c, 0)


def from_plane(ref, dst, slab):
    for y in range(N):
        dst[pl.ds(slab * 2592 + y, 36, stride=N), :N] = ref[:, N * y : N * y + N]


def spans():
    for j in range(81):
        first, at = divmod(N * j, 1458)
        fit = min(N, 1458 - at)
        yield j, first, at, fit


def from_blocks(ref, dst, slab):
    for j, first, at, fit in spans():
        rows = pl.ds(slab * 2592 + j, 32, stride=81)
        v = ref[first // 2, first % 2, :, at : at + fit]
        if fit < N:
            v = jnp.concatenate([v, ref[(first + 1) // 2, (first + 1) % 2, :, : N - fit]], axis=1)
        dst[rows, :N] = v


def to_blocks(src, ref, slab):
    for h in range(4):
        for j, first, at, fit in spans():
            v = src[pl.ds(slab * 2592 + 81 * h + j, 8, stride=324), :]
            ref[4 * first + h, :, at : at + fit] = v[:, :fit]
            if fit < N:
                ref[4 * first + 4 + h, :, : N - fit] = v[:, fit:N]


MESH = pl.DeviceIdType.MESH
BANDS = 128
CELLS = 1458
CUT = 768


def send(src, dst, send_sem, recv_sem, device):
    return pltpu.make_async_remote_copy(
        src_ref=src, dst_ref=dst, send_sem=send_sem, recv_sem=recv_sem, device_id=device, device_id_type=MESH
    )


def greet(barrier, device):
    pl.semaphore_signal(barrier, inc=1, device_id=device, device_id_type=MESH)


class Place:
    def __init__(self):
        self.band, self.grid = lax.axis_index("band"), lax.axis_index("grid")
        self.p, self.q = lax.div(self.band, 16), lax.rem(self.band, 16)
        self.z, self.core = lax.div(self.q, 2), lax.rem(self.q, 2)
        self.xh, self.y = lax.div(self.p, 4), lax.rem(self.p, 4)
        self.twin = {"band": self.band + 1 - 2 * self.core}


def device(p, q, grid):
    return {"band": p * 16 + q, "grid": grid}


def meet(me):
    barrier = pltpu.get_barrier_semaphore()

    def near(k, carry):
        w = lax.rem(me.q * 2 + me.grid + k, 32)
        greet(barrier, device(me.p, lax.div(w, 2), lax.rem(w, 2)))
        return carry

    lax.fori_loop(1, 32, near, 0)

    def far(k, carry):
        p = lax.rem(me.p + k, 8)
        for n in range(4):
            greet(barrier, device(p, me.z * 2 + n // 2, n % 2))
        return carry

    lax.fori_loop(1, 8, far, 0)
    return barrier


MET = 31 + 28
FAR_Q = (8, 9, 7, 10, 6, 11, 5, 12, 4, 13, 3, 14, 2, 15, 1)
FAR_P = (6, 2, 4, 5, 3, 7, 1)


def lane_parts():
    return pl.ds(0, CUT), pl.ds(CUT, CELLS - CUT)


def exchange(me, blocks, via_a, via_b, cols, slot, grid_to, sems):
    s1, r1, s2, r2, s3, r3, s4, r4, local = sems
    low, high = lane_parts()
    stays = jnp.logical_and(slot == me.q, grid_to == me.grid)
    moves = jnp.logical_not(stays)

    def seat(q):
        return lax.rem(q, 4) * 4 + lax.div(q, 4)

    def a1(k, p_to, p_from):
        return send(blocks.at[:, p_to, low], via_a.at[p_from], s1.at[k], r1.at[k], device(p_to, slot, grid_to))

    def b1(k, q_to, q_from):
        return send(blocks.at[seat(q_to), :, high], via_b.at[q_from], s2.at[k], r2.at[q_from], device(me.p, q_to, grid_to))

    def a2(k, q_to, q_from):
        return send(via_a.at[:, seat(q_to), :], cols.at[:, q_from, low], s3.at[k], r3.at[k], device(me.p, q_to, me.grid))

    def b2(k, p_to, p_from):
        return send(via_b.at[:, p_to, :], cols.at[p_from, :, high], s4.at[k], r4.at[k], device(p_to, me.q, me.grid))

    keep_a1 = pltpu.make_async_copy(blocks.at[:, me.p, low], via_a.at[me.p], local.at[0])
    keep_b1 = pltpu.make_async_copy(blocks.at[seat(me.q), :, high], via_b.at[me.q], local.at[1])
    keep_a2 = pltpu.make_async_copy(via_a.at[:, seat(me.q), :], cols.at[:, me.q, low], local.at[2])
    keep_b2 = pltpu.make_async_copy(via_b.at[:, me.p, :], cols.at[me.p, :, high], local.at[3])

    for n in range(15):
        k = FAR_Q[n]
        b1(k, lax.rem(me.q + k, 16), slot).start()
        if n % 2 == 0 and n < 14:
            k = FAR_P[n // 2]
            a1(k, lax.rem(me.p + k, 8), me.p).start()

    @pl.when(stays)
    def _():
        keep_a1.start()
        keep_b1.start()

    @pl.when(moves)
    def _():
        a1(0, me.p, me.p).start()
        b1(0, me.q, slot).start()

    def middle_a():
        for k in range(1, 8):
            a1(k, me.p, lax.rem(me.p + 8 - k, 8)).wait_recv()

        @pl.when(stays)
        def _():
            keep_a1.wait()

        @pl.when(moves)
        def _():
            a1(0, me.p, me.p).wait_recv()

        for k in FAR_Q:
            a2(k, lax.rem(me.q + k, 16), me.q).start()
        keep_a2.start()

    def middle_b():
        for k in range(1, 16):
            b1(k, me.q, lax.rem(me.q + k, 16)).wait_recv()

        @pl.when(stays)
        def _():
            keep_b1.wait()

        @pl.when(moves)
        def _():
            b1(0, me.q, me.q).wait_recv()

        for k in FAR_P:
            b2(k, lax.rem(me.p + k, 8), me.p).start()
        keep_b2.start()

    def finish_a():
        for k in range(1, 16):
            a2(k, me.q, lax.rem(me.q + 16 - k, 16)).wait_recv()
        keep_a2.wait()

    def finish_b():
        for k in range(1, 8):
            b2(k, me.p, lax.rem(me.p + 8 - k, 8)).wait_recv()
        keep_b2.wait()

    def drain():
        for k in range(1, 8):
            a1(k, lax.rem(me.p + k, 8), me.p).wait_send()
            b2(k, lax.rem(me.p + k, 8), me.p).wait_send()
        for k in range(1, 16):
            b1(k, lax.rem(me.q + k, 16), slot).wait_send()
            a2(k, lax.rem(me.q + k, 16), me.q).wait_send()

        @pl.when(moves)
        def _():
            a1(0, me.p, me.p).wait_send()
            b1(0, me.q, slot).wait_send()

    return middle_a, middle_b, finish_a, finish_b, drain


def exchange_scratch():
    dma = pltpu.SemaphoreType.DMA
    return [
        pltpu.VMEM((8, 16, CUT), F32), pltpu.VMEM((16, 8, CELLS - CUT), F32),
        dma((8,)), dma((8,)), dma((16,)), dma((16,)), dma((16,)), dma((16,)), dma((8,)), dma((8,)), dma((4,)),
    ]


def gather_lent(me, picked, lent, send_sem, recv_sem, local, meanwhile):
    zlo, zhi = lax.rem(me.z, 2), lax.div(me.z, 2)

    def cell(q):
        z = lax.div(q, 2)
        return lent.at[me.grid, lax.rem(z, 2), lax.rem(q, 2), pl.ds(4 * me.p + lax.div(z, 2), 1), :]

    def over_q(k, q_to, q_from):
        return send(
            picked.at[pl.ds(lax.rem(q_to, 2), 1), :], cell(q_from), send_sem.at[k], recv_sem.at[k],
            device(me.p, q_to, me.grid),
        )

    keep = pltpu.make_async_copy(picked.at[pl.ds(me.core, 1), :], cell(me.q), local)
    for k in FAR_Q:
        over_q(k, lax.rem(me.q + k, 16), me.q).start()
    keep.start()
    for k in range(1, 16):
        over_q(k, me.q, lax.rem(me.q + 16 - k, 16)).wait_recv()
    keep.wait()

    def piece(half, grid, xh, y):
        return lent.at[grid, :, half, pl.ds(16 * xh + 4 * y, 4), :]

    started = []

    def x_peer(n):
        return lax.rem(me.xh + n // 2, 2), lax.rem(me.grid + n, 2)

    def along_x(slot, half, y, n):
        xh, grid = x_peer(n)
        part = piece(half, me.grid, me.xh, y)
        return send(part, part, send_sem.at[slot + n], recv_sem.at[slot + n], device(4 * xh + me.y, me.q, grid))

    def from_x(slot, half, y, n):
        xh, grid = x_peer(n)
        part = piece(half, grid, xh, y)
        return send(part, part, send_sem.at[slot + n], recv_sem.at[slot + n], device(4 * xh + me.y, me.q, grid))

    def along_y(slot, half, xh, grid, n):
        part = piece(half, grid, xh, me.y)
        return send(part, part, send_sem.at[slot + n], recv_sem.at[slot + n], device(4 * me.xh + lax.rem(me.y + n, 4), me.q, me.grid))

    def from_y(slot, half, xh, grid, n):
        part = piece(half, grid, xh, lax.rem(me.y + 4 - n, 4))
        return send(part, part, send_sem.at[slot + n], recv_sem.at[slot + n], device(4 * me.xh + lax.rem(me.y + n, 4), me.q, me.grid))

    def go(copy):
        copy.start()
        started.append(copy)

    for n in (2, 1, 3):
        go(along_x(16, 0, me.y, n))
        go(along_y(20, 1, me.xh, me.grid, n))
    for n in (2, 1, 3):
        go(along_y(24, 0, me.xh, me.grid, n))
        go(along_x(40, 1, me.y, n))
    for m in range(1, 4):
        from_x(16, 0, me.y, m).wait_recv()
        xh, grid = x_peer(m)
        for n in (2, 1, 3):
            go(along_y(24 + 4 * m, 0, xh, grid, n))
        from_y(20, 1, me.xh, me.grid, m).wait_recv()
        for n in (2, 1, 3):
            go(along_x(40 + 4 * m, 1, lax.rem(me.y + 4 - m, 4), n))
    meanwhile()
    for m in range(4):
        xh, grid = x_peer(m)
        for n in range(1, 4):
            from_y(24 + 4 * m, 0, xh, grid, n).wait_recv()
            from_x(40 + 4 * m, 1, lax.rem(me.y + 4 - m, 4), n).wait_recv()

    def drain():
        for k in range(1, 16):
            over_q(k, lax.rem(me.q + k, 16), me.q).wait_send()
        for c in started:
            c.wait_send()

    return drain


def add_up(me, product, matrix, first, second, m_send, m_recv, meanwhile):
    p, q, grid = me.p, me.q, me.grid
    where = 2 * p + grid
    far = (12, 4, 13, 5, 8, 9, 10, 6, 11, 7, 14, 2, 15, 3, 1)

    def block(c):
        return pl.ds(pl.multiple_of(8 * c, 8), 8)

    def ahead(k):
        return lax.rem(p + k // 2, 8), lax.rem(grid + k, 2)

    def behind(k):
        return lax.rem(p + 8 - k // 2, 8), lax.rem(grid + k, 2)

    def scatter(k, to, slot):
        return send(
            product.at[block(2 * to[0] + to[1]), :], first.at[slot], m_send.at[k], m_recv.at[k], device(to[0], q, to[1])
        )

    for k in far:
        scatter(k, ahead(k), where).start()
    first[where] = product[block(where), :]
    meanwhile()
    for k in range(1, 16):
        b = behind(k)
        scatter(k, (p, grid), 2 * b[0] + b[1]).wait_recv()
    total = first[0]
    for k in range(1, 16):
        total = total + first[k]
    second[q] = total

    def share(k, slot, to):
        return send(second.at[slot], second.at[slot], m_send.at[15 + k], m_recv.at[15 + k], device(p, to, grid))

    for k in FAR_Q:
        share(k, q, lax.rem(q + k, 16)).start()
    for k in range(1, 16):
        scatter(k, ahead(k), where).wait_send()
    for k in range(1, 16):
        share(k, lax.rem(q + 16 - k, 16), q).wait_recv()
    total = second[0]
    for k in range(1, 16):
        total = total + second[k]
    matrix[block(where), :] = total

    def spread(k, slot, to):
        return send(
            matrix.at[block(slot), :], matrix.at[block(slot), :], m_send.at[30 + k], m_recv.at[30 + k],
            device(to[0], q, to[1]),
        )

    for k in far:
        spread(k, where, ahead(k)).start()
    for k in range(1, 16):
        share(k, q, lax.rem(q + k, 16)).wait_send()
    for k in range(1, 16):
        b = behind(k)
        spread(k, 2 * b[0] + b[1], (p, grid)).wait_recv()
    for k in range(1, 16):
        spread(k, where, ahead(k)).wait_send()


def fock_kernel(
    owners, orb_hbm, tl, til, tr, tir, sq_rows, sq_pair, field_out, matrix,
    orb, weight, cols, whole, lent, blocks, picked, own_rows, lent_rows, work,
    given, kept, arrived, field, turned, product, first, second,
    own_sem, w_send, w_recv, g_send, g_recv, t_send, t_recv, m_send, m_recv, *rest,
):
    near, far = rest[: len(rest) // 2], rest[len(rest) // 2 :]
    me = Place()
    partner = {"grid": 1 - me.grid}
    load = pltpu.make_async_copy(orb_hbm.at[:, 0, :], orb, own_sem.at[0])
    load.start()
    barrier = meet(me)
    load.wait()
    from_plane(orb, work, 0)
    to_blocks(work, blocks, 0)
    pl.semaphore_wait(barrier, MET)

    same = me.core == me.grid
    differ = jnp.logical_not(same)
    middle_a, middle_b, finish_a, finish_b, drain_near = exchange(me, blocks, near[0], near[1], cols, me.q, me.grid, near[2:])
    keep = pltpu.make_async_copy(orb, whole.at[me.grid], own_sem.at[0])
    to_twin = send(orb, whole.at[me.grid], w_send.at[0], w_recv.at[0], me.twin)
    to_partner = send(orb, whole.at[me.grid], w_send.at[0], w_recv.at[1], partner)
    from_partner = send(orb, whole.at[1 - me.grid], w_send.at[0], w_recv.at[1], partner)
    forward = send(whole.at[1 - me.grid], whole.at[1 - me.grid], w_send.at[1], w_recv.at[1], me.twin)

    @pl.when(same)
    def _():
        keep.start()
        to_twin.start()

    @pl.when(differ)
    def _():
        to_partner.start()

    fill_kernel(weight, sq_rows, sq_pair)
    middle_a()
    middle_b()
    finish_a()
    finish_b()
    for r in range(2):
        owner = owners[r]
        picked[r : r + 1, :] = cols[pl.ds(lax.div(owner, 16), 1), pl.ds(lax.rem(owner, 16), 1), :].reshape(1, CELLS)

    @pl.when(same)
    def _():
        from_partner.wait_recv()
        forward.start()

    def meanwhile():
        @pl.when(same)
        def _():
            keep.wait()

        @pl.when(differ)
        def _():
            to_twin.wait_recv()
            forward.wait_recv()

        for s in range(2):
            from_plane(whole.at[s], own_rows, s)

    drain_gather = gather_lent(me, picked, lent, g_send, g_recv, own_sem.at[1], meanwhile)

    for s in range(2):
        from_blocks(lent.at[s], lent_rows, s)
    spectra(own_rows, lent_rows, work, tl, til, tr, weight, 36, 36)
    potentials(own_rows, lent_rows, work, til, tir, 1 - me.core, 18)
    to_blocks(own_rows, given, 1 - me.core)
    give = send(given, arrived, t_send, t_recv, me.twin)
    give.start()
    potentials(own_rows, lent_rows, work, til, tir, me.core, 18)
    to_blocks(own_rows, kept, me.core)
    give.wait_recv()
    kept[...] = kept[...] + arrived[...]

    middle_a, middle_b, finish_a, finish_b, drain_far = exchange(
        me, kept, far[0], far[1], field, 2 * me.z + me.grid, me.core, far[2:]
    )

    @pl.when(same)
    def _():
        to_twin.wait_send()
        forward.wait_send()

    @pl.when(differ)
    def _():
        to_partner.wait_send()

    give.wait_send()
    drain_gather()
    drain_near()
    middle_a()
    middle_b()
    dot = lambda a, b: lax.dot_general(a, b, (((1,), (1,)), ((), ())), preferred_element_type=F32)

    def overlap(lanes, width):
        oh, ol = halves(cols[:, :, lanes].reshape(BANDS, width))
        fh, fl = halves(field[:, :, lanes].reshape(BANDS, width))
        return (dot(oh, fl) + dot(ol, fh)) + dot(oh, fh)

    low, high = lane_parts()
    finish_b()
    product[...] = overlap(high, CELLS - CUT)
    finish_a()
    product[...] = (product[...] + overlap(low, CUT)) * (1.0 / 373248.0)
    store = pltpu.make_async_copy(turned, field_out.at[:, 0, :], own_sem.at[1])

    def turn():
        drain_far()
        for n in range(12):
            width = min(128, CELLS - 128 * n)
            tile = field[:, :, pl.ds(128 * n, width)].reshape(BANDS, width)
            turned[pl.ds(128 * n, width), :] = tile.T
        store.start()

    add_up(me, product, matrix, first, second, m_send, m_recv, turn)
    store.wait()


def fock_call(owners, orb):
    vm = pl.BlockSpec(memory_space=pltpu.VMEM)
    dma = pltpu.SemaphoreType.DMA
    v = lambda *shape: pltpu.VMEM(shape, F32)
    return pl.pallas_call(
        fock_kernel,
        out_shape=(
            jax.ShapeDtypeStruct((CELLS, 1, BANDS), F32),
            jax.ShapeDtypeStruct((BANDS, BANDS), F32),
        ),
        in_specs=[pl.BlockSpec(memory_space=pltpu.SMEM), pl.BlockSpec(memory_space=pl.ANY)] + [vm] * 6,
        out_specs=(pl.BlockSpec(memory_space=pl.ANY), vm),
        scratch_shapes=[
            v(36, 5184), v(N, PAD, 128), v(8, 16, CELLS), v(2, 36, 5184), v(2, 2, 2, 32, CELLS), v(16, 8, CELLS), v(2, CELLS),
            v(5184, 128), v(5184, 128), v(5184, 128),
            v(16, 8, CELLS), v(16, 8, CELLS), v(16, 8, CELLS), v(8, 16, CELLS), v(CELLS, BANDS), v(BANDS, BANDS), v(16, 8, BANDS), v(16, 8, BANDS),
            dma((2,)), dma((2,)), dma((2,)), dma((56,)), dma((56,)), dma, dma, dma((46,)), dma((46,)),
        ] + exchange_scratch() + exchange_scratch(),
        compiler_params=pltpu.CompilerParams(collective_id=0, has_side_effects=True, vmem_limit_bytes=60 << 20),
    )(owners, orb, *tables())


def shards(orbitals, owners):
    field, matrix = fock_call(owners, orbitals.transpose(1, 0, 2))
    return (field.transpose(1, 2, 0), matrix)


def solution(mesh):
    in_specs = (P("band", "grid", None), P())
    out_specs = (P("grid", None, "band"), P())
    return jax.shard_map(shards, mesh=mesh, in_specs=in_specs, out_specs=out_specs, check_vma=False)
```

```python
import functools
import math

import jax
import jax.numpy as jnp
import numpy as np
from jax import lax
from jax.experimental import pallas as pl
from jax.experimental.pallas import tpu as pltpu
from jax.sharding import PartitionSpec as P

N = 72
PAD = 80
GROUP = 9
BF = jnp.bfloat16
F32 = jnp.float32

def tables():
    pos = np.arange(N)
    half = N // 2
    freq = np.where(pos <= half, pos, pos - half)
    ang = (freq[:, None] * pos[None, :] % N) * (2.0 * math.pi / N)
    w = np.where((pos == 0) | (pos == half), 1.0 / math.sqrt(N), math.sqrt(2.0 / N))
    basis = np.where((pos <= half)[:, None], np.cos(ang), np.sin(ang)) * w[:, None]
    sq = (freq * (2.0 * math.pi / N)) ** 2

    def split(t):
        hi = jnp.asarray(t, F32).astype(BF)
        lo = (jnp.asarray(t, F32) - hi.astype(F32)).astype(BF)
        return hi, lo

    def left(t):
        hi, lo = split(t)
        put = lambda a: jnp.pad(a, ((0, PAD - N), (0, PAD - N)))
        return jnp.concatenate([put(hi), put(hi), put(lo)], axis=1)

    def right(t):
        hi, lo = split(t)
        put = lambda a: jnp.pad(a, ((0, 128 - N), (0, 128 - N)))
        top = jnp.concatenate([put(hi), put(lo)], axis=1)
        low = jnp.concatenate([put(hi), jnp.zeros((128, 128), BF)], axis=1)
        return jnp.concatenate([top, low], axis=0)

    sq_rows = np.zeros((PAD, 128), np.float32); sq_rows[:N] = sq[:, None]
    sq_pair = np.zeros((N, 128), np.float32); sq_pair[:, :N] = sq[:, None] + sq[None, :]
    return (left(basis), left(basis.T), right(basis.T), right(basis), jnp.asarray(sq_rows), jnp.asarray(sq_pair))


def halves(v):
    hi = v.astype(BF)
    lo = (v - hi.astype(F32)).astype(BF)
    return hi, lo


def left_dot(table, planes):
    cols = []
    for v in planes:
        hi, lo = halves(v)
        cols.append(jnp.concatenate([hi, lo, hi], axis=0))
    out = jnp.dot(table, jnp.concatenate(cols, axis=1), preferred_element_type=F32)
    return [out[:, 128 * i : 128 * i + 128] for i in range(len(planes))]


def right_dot(v, table):
    hi, lo = halves(v)
    out = jnp.dot(jnp.concatenate([hi, lo], axis=1), table, preferred_element_type=F32)
    return out[:, :128] + out[:, 128:]


def pad_rows(v):
    return jnp.concatenate([v, jnp.zeros((PAD - N, 128), F32)], axis=0)


def fill_kernel(weight, sq_rows, sq_pair):
    def one(b, carry):
        total = sq_rows[...] + sq_pair[pl.ds(b, 1), :]
        positive = total > 0
        weight[b] = jnp.where(positive, (-0.25 * math.pi) / jnp.where(positive, total, 1.0), 0.0)
        return carry

    lax.fori_loop(0, N, one, 0)


def spectra(own, lent, work, tl, til, tr, weight, UA, UB):
    lane = lax.broadcasted_iota(jnp.int32, (1, 128), 1) < N

    def stage_a(step, carry):
        span = 2 * N * GROUP
        for u in range(UA // GROUP):
            base = pl.multiple_of((step * (UA // GROUP) + u) * span, 8)
            rows = pl.ds(base, span)
            d = jnp.where(lane, own[rows, :] * lent[rows, :], 0.0)
            z = right_dot(d, tr[...])
            for n in range(GROUP):
                at = 2 * N * n
                planes = left_dot(tl[...], [pad_rows(z[at : at + N]), pad_rows(z[at + N : at + 2 * N])])
                work[pl.ds(base + at, 2 * N), :] = jnp.concatenate([v[:N] for v in planes], axis=0)
        return carry

    lax.fori_loop(0, 36 // UA, stage_a, 0)

    def stage_b(step, carry):
        for u in range(UB):
            b = (step * UB + u) * 2
            planes = [pad_rows(work[pl.ds(b + i, N, stride=N), :]) for i in range(2)]
            planes = left_dot(tl[...], planes)
            for i in range(2):
                planes[i] = planes[i] * weight[b + i]
            planes = left_dot(til[...], planes)
            for i in range(2):
                work[pl.ds(b + i, N, stride=N), :] = planes[i][:N]
        return carry

    lax.fori_loop(0, 36 // UB, stage_b, 0)


def potentials(own, lent, work, til, tir, slab, UC):
    def stage_c(step, carry):
        span = 2 * N * GROUP
        for u in range(UC // GROUP):
            base = pl.multiple_of(slab * 2592 + (step * (UC // GROUP) + u) * span, 8)
            planes = []
            for n in range(GROUP):
                v = work[pl.ds(base + 2 * N * n, 2 * N), :]
                planes += left_dot(til[...], [pad_rows(v[:N]), pad_rows(v[N:])])
            rows = pl.ds(base, span)
            own[rows, :] = right_dot(jnp.concatenate([v[:N] for v in planes], axis=0), tir[...]) * lent[rows, :]
        return carry

    lax.fori_loop(0, 18 // UC, stage_c, 0)


def from_plane(ref, dst, slab):
    for y in range(N):
        dst[pl.ds(slab * 2592 + y, 36, stride=N), :N] = ref[:, N * y : N * y + N]


def spans():
    for j in range(81):
        first, at = divmod(N * j, 1458)
        fit = min(N, 1458 - at)
        yield j, first, at, fit


def from_blocks(ref, dst, slab):
    for j, first, at, fit in spans():
        rows = pl.ds(slab * 2592 + j, 32, stride=81)
        v = ref[first // 2, first % 2, :, at : at + fit]
        if fit < N:
            v = jnp.concatenate([v, ref[(first + 1) // 2, (first + 1) % 2, :, : N - fit]], axis=1)
        dst[rows, :N] = v


def to_blocks(src, ref, slab):
    for h in range(4):
        for j, first, at, fit in spans():
            v = src[pl.ds(slab * 2592 + 81 * h + j, 8, stride=324), :]
            ref[4 * first + h, :, at : at + fit] = v[:, :fit]
            if fit < N:
                ref[4 * first + 4 + h, :, : N - fit] = v[:, fit:N]


MESH = pl.DeviceIdType.MESH
BANDS = 128
CELLS = 1458
CUT = 768


def send(src, dst, send_sem, recv_sem, device):
    return pltpu.make_async_remote_copy(
        src_ref=src, dst_ref=dst, send_sem=send_sem, recv_sem=recv_sem, device_id=device, device_id_type=MESH
    )


def greet(barrier, device):
    pl.semaphore_signal(barrier, inc=1, device_id=device, device_id_type=MESH)


class Place:
    def __init__(self):
        self.band, self.grid = lax.axis_index("band"), lax.axis_index("grid")
        self.p, self.q = lax.div(self.band, 16), lax.rem(self.band, 16)
        self.z, self.core = lax.div(self.q, 2), lax.rem(self.q, 2)
        self.xh, self.y = lax.div(self.p, 4), lax.rem(self.p, 4)
        self.twin = {"band": self.band + 1 - 2 * self.core}


def device(p, q, grid):
    return {"band": p * 16 + q, "grid": grid}


def meet(me):
    barrier = pltpu.get_barrier_semaphore()

    def near(k, carry):
        w = lax.rem(me.q * 2 + me.grid + k, 32)
        greet(barrier, device(me.p, lax.div(w, 2), lax.rem(w, 2)))
        return carry

    lax.fori_loop(1, 32, near, 0)

    def far(k, carry):
        p = lax.rem(me.p + k, 8)
        for n in range(4):
            greet(barrier, device(p, me.z * 2 + n // 2, n % 2))
        return carry

    lax.fori_loop(1, 8, far, 0)
    return barrier


MET = 31 + 28
FAR_Q = (8, 9, 7, 10, 6, 11, 5, 12, 4, 13, 3, 14, 2, 15, 1)
FAR_P = (6, 2, 4, 5, 3, 7, 1)


def lane_parts():
    return pl.ds(0, CUT), pl.ds(CUT, CELLS - CUT)


def exchange(me, blocks, via_a, via_b, cols, slot, grid_to, sems):
    s1, r1, s2, r2, s3, r3, s4, r4, local = sems
    low, high = lane_parts()
    stays = jnp.logical_and(slot == me.q, grid_to == me.grid)
    moves = jnp.logical_not(stays)

    def seat(q):
        return lax.rem(q, 4) * 4 + lax.div(q, 4)

    def a1(k, p_to, p_from):
        return send(blocks.at[:, p_to, low], via_a.at[p_from], s1.at[k], r1.at[k], device(p_to, slot, grid_to))

    def b1(k, q_to, q_from):
        return send(blocks.at[seat(q_to), :, high], via_b.at[q_from], s2.at[k], r2.at[q_from], device(me.p, q_to, grid_to))

    def a2(k, q_to, q_from):
        return send(via_a.at[:, seat(q_to), :], cols.at[:, q_from, low], s3.at[k], r3.at[k], device(me.p, q_to, me.grid))

    def b2(k, p_to, p_from):
        return send(via_b.at[:, p_to, :], cols.at[p_from, :, high], s4.at[k], r4.at[k], device(p_to, me.q, me.grid))

    keep_a1 = pltpu.make_async_copy(blocks.at[:, me.p, low], via_a.at[me.p], local.at[0])
    keep_b1 = pltpu.make_async_copy(blocks.at[seat(me.q), :, high], via_b.at[me.q], local.at[1])
    keep_a2 = pltpu.make_async_copy(via_a.at[:, seat(me.q), :], cols.at[:, me.q, low], local.at[2])
    keep_b2 = pltpu.make_async_copy(via_b.at[:, me.p, :], cols.at[me.p, :, high], local.at[3])

    for n in range(15):
        k = FAR_Q[n]
        b1(k, lax.rem(me.q + k, 16), slot).start()
        if n % 2 == 0 and n < 14:
            k = FAR_P[n // 2]
            a1(k, lax.rem(me.p + k, 8), me.p).start()

    @pl.when(stays)
    def _():
        keep_a1.start()
        keep_b1.start()

    @pl.when(moves)
    def _():
        a1(0, me.p, me.p).start()
        b1(0, me.q, slot).start()

    def middle_a():
        for k in range(1, 8):
            a1(k, me.p, lax.rem(me.p + 8 - k, 8)).wait_recv()

        @pl.when(stays)
        def _():
            keep_a1.wait()

        @pl.when(moves)
        def _():
            a1(0, me.p, me.p).wait_recv()

        for k in FAR_Q:
            a2(k, lax.rem(me.q + k, 16), me.q).start()
        keep_a2.start()

    def middle_b():
        for k in range(1, 16):
            b1(k, me.q, lax.rem(me.q + k, 16)).wait_recv()

        @pl.when(stays)
        def _():
            keep_b1.wait()

        @pl.when(moves)
        def _():
            b1(0, me.q, me.q).wait_recv()

        for k in FAR_P:
            b2(k, lax.rem(me.p + k, 8), me.p).start()
        keep_b2.start()

    def finish_a():
        for k in range(1, 16):
            a2(k, me.q, lax.rem(me.q + 16 - k, 16)).wait_recv()
        keep_a2.wait()

    def finish_b():
        for k in range(1, 8):
            b2(k, me.p, lax.rem(me.p + 8 - k, 8)).wait_recv()
        keep_b2.wait()

    def drain():
        for k in range(1, 8):
            a1(k, lax.rem(me.p + k, 8), me.p).wait_send()
            b2(k, lax.rem(me.p + k, 8), me.p).wait_send()
        for k in range(1, 16):
            b1(k, lax.rem(me.q + k, 16), slot).wait_send()
            a2(k, lax.rem(me.q + k, 16), me.q).wait_send()

        @pl.when(moves)
        def _():
            a1(0, me.p, me.p).wait_send()
            b1(0, me.q, slot).wait_send()

    return middle_a, middle_b, finish_a, finish_b, drain


def exchange_scratch():
    dma = pltpu.SemaphoreType.DMA
    return [
        pltpu.VMEM((8, 16, CUT), F32), pltpu.VMEM((16, 8, CELLS - CUT), F32),
        dma((8,)), dma((8,)), dma((16,)), dma((16,)), dma((16,)), dma((16,)), dma((8,)), dma((8,)), dma((4,)),
    ]


def gather_lent(me, picked, lent, send_sem, recv_sem, local, meanwhile):
    zlo, zhi = lax.rem(me.z, 2), lax.div(me.z, 2)

    def cell(q):
        z = lax.div(q, 2)
        return lent.at[me.grid, lax.rem(z, 2), lax.rem(q, 2), pl.ds(4 * me.p + lax.div(z, 2), 1), :]

    def over_q(k, q_to, q_from):
        return send(
            picked.at[pl.ds(lax.rem(q_to, 2), 1), :], cell(q_from), send_sem.at[k], recv_sem.at[k],
            device(me.p, q_to, me.grid),
        )

    keep = pltpu.make_async_copy(picked.at[pl.ds(me.core, 1), :], cell(me.q), local)
    for k in FAR_Q:
        over_q(k, lax.rem(me.q + k, 16), me.q).start()
    keep.start()
    for k in range(1, 16):
        over_q(k, me.q, lax.rem(me.q + 16 - k, 16)).wait_recv()
    keep.wait()

    def piece(half, grid, xh, y):
        return lent.at[grid, :, half, pl.ds(16 * xh + 4 * y, 4), :]

    started = []

    def x_peer(n):
        return lax.rem(me.xh + n // 2, 2), lax.rem(me.grid + n, 2)

    def along_x(slot, half, y, n):
        xh, grid = x_peer(n)
        part = piece(half, me.grid, me.xh, y)
        return send(part, part, send_sem.at[slot + n], recv_sem.at[slot + n], device(4 * xh + me.y, me.q, grid))

    def from_x(slot, half, y, n):
        xh, grid = x_peer(n)
        part = piece(half, grid, xh, y)
        return send(part, part, send_sem.at[slot + n], recv_sem.at[slot + n], device(4 * xh + me.y, me.q, grid))

    def along_y(slot, half, xh, grid, n):
        part = piece(half, grid, xh, me.y)
        return send(part, part, send_sem.at[slot + n], recv_sem.at[slot + n], device(4 * me.xh + lax.rem(me.y + n, 4), me.q, me.grid))

    def from_y(slot, half, xh, grid, n):
        part = piece(half, grid, xh, lax.rem(me.y + 4 - n, 4))
        return send(part, part, send_sem.at[slot + n], recv_sem.at[slot + n], device(4 * me.xh + lax.rem(me.y + n, 4), me.q, me.grid))

    def go(copy):
        copy.start()
        started.append(copy)

    for n in (2, 1, 3):
        go(along_x(16, 0, me.y, n))
        go(along_y(20, 1, me.xh, me.grid, n))
    for n in (2, 1, 3):
        go(along_y(24, 0, me.xh, me.grid, n))
        go(along_x(40, 1, me.y, n))
    for m in range(1, 4):
        from_x(16, 0, me.y, m).wait_recv()
        xh, grid = x_peer(m)
        for n in (2, 1, 3):
            go(along_y(24 + 4 * m, 0, xh, grid, n))
        from_y(20, 1, me.xh, me.grid, m).wait_recv()
        for n in (2, 1, 3):
            go(along_x(40 + 4 * m, 1, lax.rem(me.y + 4 - m, 4), n))
    meanwhile()
    for m in range(4):
        xh, grid = x_peer(m)
        for n in range(1, 4):
            from_y(24 + 4 * m, 0, xh, grid, n).wait_recv()
            from_x(40 + 4 * m, 1, lax.rem(me.y + 4 - m, 4), n).wait_recv()

    def drain():
        for k in range(1, 16):
            over_q(k, lax.rem(me.q + k, 16), me.q).wait_send()
        for c in started:
            c.wait_send()

    return drain


def add_up(me, product, matrix, first, second, m_send, m_recv, meanwhile):
    p, q, grid = me.p, me.q, me.grid
    where = 2 * p + grid
    far = (12, 4, 13, 5, 8, 9, 10, 6, 11, 7, 14, 2, 15, 3, 1)

    def block(c):
        return pl.ds(pl.multiple_of(8 * c, 8), 8)

    def ahead(k):
        return lax.rem(p + k // 2, 8), lax.rem(grid + k, 2)

    def behind(k):
        return lax.rem(p + 8 - k // 2, 8), lax.rem(grid + k, 2)

    def scatter(k, to, slot):
        return send(
            product.at[block(2 * to[0] + to[1]), :], first.at[slot], m_send.at[k], m_recv.at[k], device(to[0], q, to[1])
        )

    for k in far:
        scatter(k, ahead(k), where).start()
    first[where] = product[block(where), :]
    meanwhile()
    for k in range(1, 16):
        b = behind(k)
        scatter(k, (p, grid), 2 * b[0] + b[1]).wait_recv()
    total = first[0]
    for k in range(1, 16):
        total = total + first[k]
    second[q] = total

    def share(k, slot, to):
        return send(second.at[slot], second.at[slot], m_send.at[15 + k], m_recv.at[15 + k], device(p, to, grid))

    for k in FAR_Q:
        share(k, q, lax.rem(q + k, 16)).start()
    for k in range(1, 16):
        scatter(k, ahead(k), where).wait_send()
    for k in range(1, 16):
        share(k, lax.rem(q + 16 - k, 16), q).wait_recv()
    total = second[0]
    for k in range(1, 16):
        total = total + second[k]
    matrix[block(where), :] = total

    def spread(k, slot, to):
        return send(
            matrix.at[block(slot), :], matrix.at[block(slot), :], m_send.at[30 + k], m_recv.at[30 + k],
            device(to[0], q, to[1]),
        )

    for k in far:
        spread(k, where, ahead(k)).start()
    for k in range(1, 16):
        share(k, q, lax.rem(q + k, 16)).wait_send()
    for k in range(1, 16):
        b = behind(k)
        spread(k, 2 * b[0] + b[1], (p, grid)).wait_recv()
    for k in range(1, 16):
        spread(k, where, ahead(k)).wait_send()


def fock_kernel(
    owners, orb_hbm, tl, til, tr, tir, sq_rows, sq_pair, field_out, matrix,
    orb, weight, cols, whole, lent, blocks, picked, own_rows, lent_rows, work,
    given, kept, arrived, field, turned, product, first, second,
    own_sem, w_send, w_recv, g_send, g_recv, t_send, t_recv, m_send, m_recv, *rest,
):
    near, far = rest[: len(rest) // 2], rest[len(rest) // 2 :]
    me = Place()
    partner = {"grid": 1 - me.grid}
    load = pltpu.make_async_copy(orb_hbm.at[:, 0, :], orb, own_sem.at[0])
    load.start()
    barrier = meet(me)
    load.wait()
    from_plane(orb, work, 0)
    to_blocks(work, blocks, 0)
    pl.semaphore_wait(barrier, MET)

    same = me.core == me.grid
    differ = jnp.logical_not(same)
    middle_a, middle_b, finish_a, finish_b, drain_near = exchange(me, blocks, near[0], near[1], cols, me.q, me.grid, near[2:])
    keep = pltpu.make_async_copy(orb, whole.at[me.grid], own_sem.at[0])
    to_twin = send(orb, whole.at[me.grid], w_send.at[0], w_recv.at[0], me.twin)
    to_partner = send(orb, whole.at[me.grid], w_send.at[0], w_recv.at[1], partner)
    from_partner = send(orb, whole.at[1 - me.grid], w_send.at[0], w_recv.at[1], partner)
    forward = send(whole.at[1 - me.grid], whole.at[1 - me.grid], w_send.at[1], w_recv.at[1], me.twin)

    @pl.when(same)
    def _():
        keep.start()
        to_twin.start()

    fill_kernel(weight, sq_rows, sq_pair)
    middle_a()

    @pl.when(differ)
    def _():
        to_partner.start()

    middle_b()
    finish_a()
    finish_b()
    for r in range(2):
        owner = owners[r]
        picked[r : r + 1, :] = cols[pl.ds(lax.div(owner, 16), 1), pl.ds(lax.rem(owner, 16), 1), :].reshape(1, CELLS)

    @pl.when(same)
    def _():
        from_partner.wait_recv()
        forward.start()

    def meanwhile():
        @pl.when(same)
        def _():
            keep.wait()

        @pl.when(differ)
        def _():
            to_twin.wait_recv()
            forward.wait_recv()

        for s in range(2):
            from_plane(whole.at[s], own_rows, s)

    drain_gather = gather_lent(me, picked, lent, g_send, g_recv, own_sem.at[1], meanwhile)

    for s in range(2):
        from_blocks(lent.at[s], lent_rows, s)
    spectra(own_rows, lent_rows, work, tl, til, tr, weight, 36, 36)
    potentials(own_rows, lent_rows, work, til, tir, 1 - me.core, 18)
    to_blocks(own_rows, given, 1 - me.core)
    give = send(given, arrived, t_send, t_recv, me.twin)
    give.start()
    potentials(own_rows, lent_rows, work, til, tir, me.core, 18)
    to_blocks(own_rows, kept, me.core)
    give.wait_recv()
    kept[...] = kept[...] + arrived[...]

    middle_a, middle_b, finish_a, finish_b, drain_far = exchange(
        me, kept, far[0], far[1], field, 2 * me.z + me.grid, me.core, far[2:]
    )

    @pl.when(same)
    def _():
        to_twin.wait_send()
        forward.wait_send()

    @pl.when(differ)
    def _():
        to_partner.wait_send()

    give.wait_send()
    drain_gather()
    drain_near()
    middle_a()
    middle_b()
    dot = lambda a, b: lax.dot_general(a, b, (((1,), (1,)), ((), ())), preferred_element_type=F32)

    def overlap(lanes, width):
        oh, ol = halves(cols[:, :, lanes].reshape(BANDS, width))
        fh, fl = halves(field[:, :, lanes].reshape(BANDS, width))
        return (dot(oh, fl) + dot(ol, fh)) + dot(oh, fh)

    low, high = lane_parts()
    finish_b()
    product[...] = overlap(high, CELLS - CUT)
    finish_a()
    product[...] = (product[...] + overlap(low, CUT)) * (1.0 / 373248.0)
    store = pltpu.make_async_copy(turned, field_out.at[:, 0, :], own_sem.at[1])

    def turn():
        drain_far()
        for n in range(12):
            width = min(128, CELLS - 128 * n)
            tile = field[:, :, pl.ds(128 * n, width)].reshape(BANDS, width)
            turned[pl.ds(128 * n, width), :] = tile.T
        store.start()

    add_up(me, product, matrix, first, second, m_send, m_recv, turn)
    store.wait()


def fock_call(owners, orb):
    vm = pl.BlockSpec(memory_space=pltpu.VMEM)
    dma = pltpu.SemaphoreType.DMA
    v = lambda *shape: pltpu.VMEM(shape, F32)
    return pl.pallas_call(
        fock_kernel,
        out_shape=(
            jax.ShapeDtypeStruct((CELLS, 1, BANDS), F32),
            jax.ShapeDtypeStruct((BANDS, BANDS), F32),
        ),
        in_specs=[pl.BlockSpec(memory_space=pltpu.SMEM), pl.BlockSpec(memory_space=pl.ANY)] + [vm] * 6,
        out_specs=(pl.BlockSpec(memory_space=pl.ANY), vm),
        scratch_shapes=[
            v(36, 5184), v(N, PAD, 128), v(8, 16, CELLS), v(2, 36, 5184), v(2, 2, 2, 32, CELLS), v(16, 8, CELLS), v(2, CELLS),
            v(5184, 128), v(5184, 128), v(5184, 128),
            v(16, 8, CELLS), v(16, 8, CELLS), v(16, 8, CELLS), v(8, 16, CELLS), v(CELLS, BANDS), v(BANDS, BANDS), v(16, 8, BANDS), v(16, 8, BANDS),
            dma((2,)), dma((2,)), dma((2,)), dma((56,)), dma((56,)), dma, dma, dma((46,)), dma((46,)),
        ] + exchange_scratch() + exchange_scratch(),
        compiler_params=pltpu.CompilerParams(collective_id=0, has_side_effects=True, vmem_limit_bytes=60 << 20),
    )(owners, orb, *tables())


def shards(orbitals, owners):
    field, matrix = fock_call(owners, orbitals.transpose(1, 0, 2))
    return (field.transpose(1, 2, 0), matrix)


def solution(mesh):
    in_specs = (P("band", "grid", None), P())
    out_specs = (P("grid", None, "band"), P())
    return jax.shard_map(shards, mesh=mesh, in_specs=in_specs, out_specs=out_specs, check_vma=False)
```
